32 devices in a mesh: wide: 16 (over z, y, core), narrow: 2 (over x).
Axes of the slice: x: 2, y: 2, z: 4, core: 2. Of those that a mesh axis runs over, the one named last changes fastest.
Arguments:
- tokens: bfloat16 [32, 512, 768], P(('wide', 'narrow')), may hold values from -6 to 6
- lengths: int32 [32], P(('wide', 'narrow')), may hold values from 128 to 512, as said below
- w_qkv: bfloat16 [768, 2304], P('wide'), may hold values from -0.21875 to 0.21875
- w_out: bfloat16 [768, 768], P('wide'), may hold values from -1.75 to 1.75
- w_in: bfloat16 [768, 3072], P('wide'), may hold values from -0.21875 to 0.21875
- w_down: bfloat16 [3072, 768], P('wide'), may hold values from -0.109375 to 0.109375
- norms_biases: bfloat16 [9216], P('wide'), may hold values from -0.4 to 1.6, as said below
- cotangent: bfloat16 [32, 512, 768], P(('wide', 'narrow')), may hold values from -6 to 6
Outputs:
- output: bfloat16 [32, 512, 768], P(('wide', 'narrow'))
- grad_tokens: float32 [32, 512, 768], P(('wide', 'narrow'))
- grad_qkv: float32 [768, 2304], P('wide')
- grad_out: float32 [768, 768], P('wide')
- grad_in: float32 [768, 3072], P('wide')
- grad_down: float32 [3072, 768], P('wide')
- grad_norms_biases: float32 [9216], P('wide')
The draws below stay inside these ranges and needn't reach their ends.
Inputs may be any that keep to these rules, and one draw needn't show every extreme that they name: `lengths`: the number of real tokens of each sequence; keys at positions at or past it are padding; some sequence has 512 and some has 128. `norms_biases`: the gains g1 and g2 lie within 0.6 and 1.6, the biases and shifts within -0.4 and 0.4.
All inputs are finite; a program needn't handle non-finite values.
Results may differ from the reference program's by a relative error of at most 0.019.
Values may be sent and summed in bfloat16 or wider, within the bound.
A program may use at most 128 MiB of HBM per device.

```python
import jax
import jax.numpy as jnp
from jax import lax

D = 768
HEADS = 12
FF = 3072
SEQ = 512
SEQS = 32


def draw_lengths(key, part):
    key = jax.random.fold_in(key, 11)
    key_lengths, key_places = jax.random.split(key)
    picked_len = jax.random.randint(key_lengths, (SEQS,), SEQ // 4, SEQ + 1)
    places = jax.random.permutation(key_places, SEQS)
    picked_len = picked_len.at[places[0]].set(SEQ).at[places[1]].set(SEQ // 4)
    return picked_len.astype(jnp.int32)


def draw_norms_biases(key, part):
    key = jax.random.fold_in(key, 23)
    key_gain, key_bias = jax.random.split(key)
    position = jnp.arange(8 * D + FF)
    is_gain = (position // D == 3) | (position // D == 6)
    gains = jnp.exp(jax.random.uniform(key_gain, (8 * D + FF,), jnp.float32, jnp.log(0.61), jnp.log(1.58)))
    biases = jax.random.uniform(key_bias, (8 * D + FF,), jnp.float32, -0.39, 0.39)
    return jnp.where(is_gain, gains, biases).astype(jnp.bfloat16)


def block_levels(rng, dims, shards, low, top_value):
    gain, own = 1.0, jax.random.fold_in(rng, 6)
    for dim, blocks in shards:
        heights = jnp.exp(jax.random.uniform(jax.random.fold_in(own, dim), (blocks,), jnp.float32, low / len(shards), top_value / len(shards)))
        gain = gain * jnp.repeat(heights, dims[dim] // blocks).reshape([-1 if axis == dim else 1 for axis in range(len(dims))])
    return gain


def scatter_about(key, extent, scale, reach, cuts=(), kind=jnp.bfloat16):
    gain = block_levels(key, extent, cuts, -0.22, 0.18) if cuts else 1.0
    values = jax.random.normal(key, extent, jnp.float32) * scale * gain
    return jnp.minimum(jnp.maximum(values, -reach), reach).astype(kind)


def setup_inputs(seed: int = 0) -> dict:
    keys = jax.random.split(jax.random.key(seed), 9)
    return {
        "tokens": scatter_about(keys[0], (SEQS, SEQ, D), 1.0, 6.0, ((0, 32),)),
        "lengths": draw_lengths(jax.random.fold_in(keys[8], 71), 0),
        "w_qkv": scatter_about(keys[2], (D, 3 * D), D ** -0.5, 0.21875, ((0, 16),)),
        "w_out": scatter_about(keys[3], (D, D), (D // 64) ** -0.5, 1.75, ((0, 16),)),
        "w_in": scatter_about(keys[4], (D, FF), D ** -0.5, 0.21875, ((0, 16),)),
        "w_down": scatter_about(keys[5], (FF, D), FF ** -0.5, 0.109375, ((0, 16),)),
        "norms_biases": draw_norms_biases(jax.random.fold_in(keys[8], 71), 0),
        "cotangent": scatter_about(keys[7], (SEQS, SEQ, D), 1.0, 6.0, ((0, 32),)),
    }


@jax.custom_vjp
def low(v):
    return lax.optimization_barrier(v.astype(jnp.bfloat16)).astype(jnp.float32)

@jax.custom_vjp
def low_back(v):
    return v

def low_keep(v):
    return (low(v), None)

def low_pass(kept, grad):
    return (grad,)

def back_keep(v):
    return (v, None)

def back_low(kept, grad):
    return (low(grad),)
low.defvjp(low_keep, low_pass)
low_back.defvjp(back_keep, back_low)
precise = lax.Precision.HIGHEST

def product(left, right):
    return jnp.dot(left, right, precision=precise)

def norm_rows(values, gain_row, shift_row):
    average = lax.optimization_barrier(jnp.mean(values, -1, keepdims=True))
    centred = values - average
    spread = lax.optimization_barrier(jnp.mean(centred * centred, -1, keepdims=True))
    return centred * lax.rsqrt(spread + 1e-06) * gain_row + shift_row

def split_vector(vector):
    segments = [vector[position * D:(position + 1) * D] for position in range(8)]
    return segments + [vector[8 * D:8 * D + FF]]

def sequence_layer(inputs, length, w_qkv, w_out, w_in, w_down, vector):
    q_bias, v_bias, o_bias, gain_one, shift_one, down_bias, gain_two, shift_two, in_bias = split_vector(vector)
    head_size = D // HEADS
    joined_bias = jnp.concatenate([q_bias, jnp.zeros((D,), jnp.float32), v_bias])
    projected = low(low_back(product(inputs, w_qkv) + joined_bias))
    queries = projected[:, :D].reshape(SEQ, HEADS, head_size)
    key_rows = projected[:, D:2 * D].reshape(SEQ, HEADS, head_size)
    values = projected[:, 2 * D:].reshape(SEQ, HEADS, head_size)
    scores = low_back(jnp.einsum('qhd,khd->hqk', queries, key_rows, precision=precise) * head_size ** (-0.5))
    usable = jnp.arange(SEQ) < length
    scores = jnp.where(usable[None, None, :], scores, -1000000000.0)
    highest = lax.optimization_barrier(jnp.max(scores, -1, keepdims=True))
    raised = jnp.exp(scores - highest)
    attend = low(raised / lax.optimization_barrier(jnp.sum(raised, -1, keepdims=True)))
    context = low(low_back(jnp.einsum('hqk,khd->qhd', attend, values, precision=precise).reshape(SEQ, D)))
    attended = low_back(product(context, w_out) + o_bias)
    normed_one = norm_rows(inputs + attended, gain_one, shift_one)
    pre_act = low_back(product(low(normed_one), w_in) + in_bias)
    activated = low(jax.nn.gelu(pre_act, approximate=False))
    feed_out = low_back(product(activated, w_down) + down_bias)
    return norm_rows(normed_one + feed_out, gain_two, shift_two)

def whole_batch(inputs, lengths, w_qkv, w_out, w_in, w_down, vector):
    checked_layer = jax.checkpoint(sequence_layer)

    def one_sequence(sequence):
        return checked_layer(sequence[0], sequence[1], w_qkv, w_out, w_in, w_down, vector)
    return lax.map(one_sequence, (inputs, lengths))

def reference(tokens, lengths, w_qkv, w_out, w_in, w_down, norms_biases, cotangent):

    def forward(inputs, a_qkv, a_out, a_in, a_down, a_vector):
        return whole_batch(inputs, lengths, a_qkv, a_out, a_in, a_down, a_vector)
    result, pullback = jax.vjp(forward, tokens.astype(jnp.float32), w_qkv.astype(jnp.float32), w_out.astype(jnp.float32), w_in.astype(jnp.float32), w_down.astype(jnp.float32), norms_biases.astype(jnp.float32))
    grad_inputs, grad_qkv, grad_out, grad_in, grad_down, grad_vector = pullback(cotangent.astype(jnp.float32))
    return (result.astype(jnp.bfloat16), grad_inputs, grad_qkv, grad_out, grad_in, grad_down, grad_vector)
```

```python
import functools

import jax
import jax.numpy as jnp
import numpy as np
from jax import lax
from jax.experimental import pallas as pl
from jax.experimental.pallas import tpu as pltpu
from jax.sharding import PartitionSpec as P

HEADS = 12
MESH = pl.DeviceIdType.MESH
BF = jnp.bfloat16
F32 = jnp.float32
NT = (((1,), (1,)), ((), ()))
TN = (((0,), (0,)), ((), ()))
ZH, ZL, YS, CS = 2, 2, 2, 2
ZS = ZH * ZL
QKV, OUT, IN, DOWN, CHUNKS = 0, 3, 4, 8, 12
SQRT_HALF = 0.7071067811865476
INV_SQRT_TAU = 0.3989422804014327


def dot(left, right, dims=None):
    if dims is None:
        return jnp.dot(left, right, preferred_element_type=F32)
    return lax.dot_general(left, right, dims, preferred_element_type=F32)


def loop(count, body):
    def step(index, carry):
        body(index)
        return carry

    lax.fori_loop(0, count, step, 0)


def span(index, size):
    return pl.ds(pl.multiple_of(index * size, size), size)


def layer_kernel(
    x_hbm, len_ref, wqkv_hbm, wout_hbm, win_hbm, wdown_hbm, vec_hbm, cot_hbm,
    out_hbm, gtok_hbm, gqkv_hbm, gout_hbm, gin_hbm, gdown_hbm, gvec_hbm,
    wa, wd, vb, gd, go, gv, rcore, rya, rxb, rza, ryb, rzb, rxa, rfb, rv_core, rv_y, rv_z, rv_x, fin, fv,
    x, cot, qkv, vt, pt, ct, n1, y1b, y1t, act, dact, h2, dfb, dcx, rs1, prm, vg,
    s_load, s_vload, s_io, s_store,
    gsz, grz, gsy, gry, gsx1, grx1, gsx2, grx2, gsc, grc, vsz, vrz, vsy, vry, vsc, vrc,
    rsc, rrc, rsya, rrya, rsxb, rrxb, rsza, rrza, rsyb, rryb, rszb, rrzb, rsxa, rrxa, rsfb, rrfb,
    wsc, wrc, wsy, wry, wsz, wrz, wsx, wrx,
):
    seq, model = x.shape
    rows = wa.shape[-2]
    hidden = act.shape[1]
    pair = 2 * (model // HEADS)
    head = model // HEADS
    group = model // 3
    half = model // 2
    wide = lax.axis_index("wide")
    px = lax.axis_index("narrow")
    c = lax.rem(wide, CS)
    y = lax.rem(wide // CS, YS)
    z = wide // (CS * YS)
    zl = lax.rem(z, ZL)
    zh = z // ZL

    def device(zz, yy, cc, xx):
        return ((zz * YS + yy) * CS + cc, xx)

    sibling = device(z, y, 1 - c, px)
    across_y = device(z, 1 - y, c, px)
    across_x = device(z, y, c, 1 - px)

    def ahead(dz):
        return lax.rem(z + dz, ZS)

    def behind(dz):
        return lax.rem(z + ZS - dz, ZS)

    def remote(src, dst, send, recv, where):
        return pltpu.make_async_remote_copy(
            src_ref=src, dst_ref=dst, send_sem=send, recv_sem=recv, device_id=where, device_id_type=MESH
        )

    ALL = slice(None)

    def wpiece(k, zz, yy, cc, r=ALL):
        zi = (ALL, ALL) if zz is None else (zz // ZL, lax.rem(zz, ZL))
        if k < DOWN:
            return wa.at[(k, *zi, yy, cc, r)]
        return wd.at[(*zi, yy, cc, k - DOWN, r)]

    loads = []

    def load(src, dst, sem):
        cp = pltpu.make_async_copy(src, dst, sem)
        cp.start()
        return cp

    own_loads = [[] for _ in range(CHUNKS)]
    load_vec = load(vec_hbm, vb.at[zh, zl, y, c], s_vload)
    load_x = load(x_hbm.at[0], x, s_io.at[0])
    for k in range(CHUNKS):
        if k < OUT:
            for part in range(3):
                own_loads[k].append(
                    load(
                        wqkv_hbm.at[:, pl.ds(part * model + k * group, group)],
                        wa.at[k, zh, zl, y, c, :, pl.ds(part * group, group)],
                        s_load.at[k, part],
                    )
                )
        elif k < IN:
            own_loads[k].append(load(wout_hbm, wa.at[k, zh, zl, y, c], s_load.at[k, 0]))
        elif k < DOWN:
            own_loads[k].append(
                load(win_hbm.at[:, pl.ds((k - IN) * model, model)], wa.at[k, zh, zl, y, c], s_load.at[k, 0])
            )
        else:
            own_loads[k].append(
                load(wdown_hbm.at[pl.ds((k - DOWN) * rows, rows)], wd.at[zh, zl, y, c, k - DOWN], s_load.at[k, 0])
            )
    load_cot = load(cot_hbm.at[0], cot, s_io.at[1])

    barrier = pltpu.get_barrier_semaphore()
    for where in (sibling, across_y, across_x, *(device(ahead(dz), y, c, px) for dz in (1, 2, 3))):
        pl.semaphore_signal(barrier, inc=1, device_id=where, device_id_type=MESH)
    pl.semaphore_wait(barrier, 6)

    third = rows // 3
    kept = pl.ds(pl.multiple_of(px * third, third), 2 * third)
    given = pl.ds(pl.multiple_of(px * 2 * third, third), third)
    taken = pl.ds(pl.multiple_of((1 - px) * 2 * third, third), third)

    def g_z(k, dz, source):
        piece = wpiece(k, source, y, c, kept)
        return remote(piece, piece, gsz.at[k, dz - 1], grz.at[k, dz - 1], device(ahead(dz), y, c, px))

    def g_y(k, column):
        piece = wpiece(k, None, column, c, kept)
        return remote(piece, piece, gsy.at[k], gry.at[k], across_y)

    def g_x1(k, dz, r):
        piece = wpiece(k, behind(dz), y, c, r)
        return remote(piece, piece, gsx1.at[k, dz - 1], grx1.at[k, dz - 1], across_x)

    def g_x2(k, r):
        piece = wpiece(k, None, 1 - y, c, r)
        return remote(piece, piece, gsx2.at[k], grx2.at[k], across_x)

    def g_core(k, core):
        piece = wpiece(k, None, ALL, core)
        return remote(piece, piece, gsc.at[k], grc.at[k], sibling)

    def v_z(dz, source):
        piece = vb.at[source // ZL, lax.rem(source, ZL), y, c]
        return remote(piece, piece, vsz.at[dz - 1], vrz.at[dz - 1], device(ahead(dz), y, c, px))

    def v_y(column):
        piece = vb.at[:, :, column, c]
        return remote(piece, piece, vsy, vry, across_y)

    def v_core(core):
        piece = vb.at[:, :, :, core]
        return remote(piece, piece, vsc, vrc, sibling)

    def e1(k):
        if not 0 <= k < CHUNKS:
            return
        for cp in own_loads[k]:
            cp.wait()
        if k == 0:
            load_vec.wait()
            for dz in (1, 2, 3):
                v_z(dz, z).start()
        for dz in (1, 2, 3):
            g_z(k, dz, z).start()

    def e2(k):
        if not 0 <= k < CHUNKS:
            return
        if k == 0:
            for dz in (1, 2, 3):
                v_z(dz, behind(dz)).wait_recv()
            v_y(y).start()
        for dz in (1, 2, 3):
            g_z(k, dz, behind(dz)).wait_recv()
        g_y(k, y).start()
        for dz in (1, 2, 3):
            g_x1(k, dz, given).start()

    def e3(k):
        if not 0 <= k < CHUNKS:
            return
        if k == 0:
            v_y(1 - y).wait_recv()
            v_core(c).start()
        g_y(k, 1 - y).wait_recv()
        g_x2(k, given).start()

    def e4(k):
        if not 0 <= k < CHUNKS:
            return
        for dz in (1, 2, 3):
            g_x1(k, dz, taken).wait_recv()
        g_x2(k, taken).wait_recv()
        g_core(k, c).start()

    def e5(k):
        if not 0 <= k < CHUNKS:
            return
        if k == 0:
            v_core(1 - c).wait_recv()
        g_core(k, 1 - c).wait_recv()

    def sent(k):
        for dz in (1, 2, 3):
            g_z(k, dz, z).wait_send()
            g_x1(k, dz, given).wait_send()
        g_y(k, y).wait_send()
        g_x2(k, given).wait_send()
        g_core(k, c).wait_send()

    def vec_sent():
        for dz in (1, 2, 3):
            v_z(dz, z).wait_send()
        v_y(y).wait_send()
        v_core(c).wait_send()

    def place_matrix(k, lanes):
        i = lax.broadcasted_iota(jnp.int32, (lanes, model), 0)
        j = lax.broadcasted_iota(jnp.int32, (lanes, model), 1)
        quarter = model // 4
        return jnp.where((i < quarter) & (j == i + k * quarter), 1.0, 0.0).astype(BF)

    def pick_matrix(k, count, total, slot):
        b = lax.broadcasted_iota(jnp.int32, (count, total), 0)
        r = lax.broadcasted_iota(jnp.int32, (count, total), 1)
        segment = 4 * b + k
        return jnp.where((r == slot * (segment // 3) + lax.rem(segment, 3)) & (b < 12), 1.0, 0.0).astype(BF)

    def spread_params():
        lanes = vb.shape[-1]
        segments = vb[...].reshape(-1, lanes)
        total = None
        for k in range(4):
            picked = dot(pick_matrix(k, 16, segments.shape[0], vb.shape[-2]), segments).astype(BF)
            part = dot(picked, place_matrix(k, lanes))
            total = part if total is None else total + part
        prm[...] = total

    def gather_grads():
        lanes = gv.shape[-1]
        low = vg[...].astype(BF)
        total = None
        for k in range(4):
            cut = dot(low, place_matrix(k, lanes), NT).astype(BF)
            part = dot(pick_matrix(k, 16, 16 * gv.shape[-2], gv.shape[-2]), cut, TN)
            total = part if total is None else total + part
        gv[...] = total.astype(BF).reshape(gv.shape)

    def weight(k, cols=ALL):
        block = wa[k, :, :, :, :, :, cols]
        return block.reshape(-1, block.shape[-1])

    def project(g):
        grouped = span(g, group)
        joined = dot(x[...], weight(g))
        q = (joined[:, :group] + prm[0:1, grouped]).astype(BF)
        qkv[g, :, 0:group] = q * jnp.asarray(head**-0.5, BF)
        qkv[g, :, group : 2 * group] = joined[:, group : 2 * group].astype(BF)
        v = (joined[:, 2 * group :] + prm[1:2, grouped]).astype(BF)
        qkv[g, :, 2 * group :] = v
        vt[grouped, :] = v.T

    def attend(g):
        length = len_ref[0]

        def one(h):
            cols = span(h // 2, pair)
            keys = pl.ds(pl.multiple_of(group + (h // 2) * pair, pair), pair)
            lane = lax.broadcasted_iota(jnp.int32, (seq, pair), 1) // head
            masked = jnp.where(lane == lax.rem(h, 2), qkv[g, :, keys], jnp.zeros((), BF))
            scores = dot(masked, qkv[g, :, cols], NT)
            key = lax.broadcasted_iota(jnp.int32, scores.shape, 0)
            scores = jnp.where(key < length, scores, -1000000000.0)
            raised = jnp.exp(scores - jnp.max(scores, axis=0, keepdims=True))
            probs = (raised * (1.0 / jnp.sum(raised, axis=0, keepdims=True))).astype(BF)
            pt[g, h] = probs
            mine = pl.ds(pl.multiple_of(g * group + h * head, head), head)
            ct[mine, :] = dot(vt[mine, :], probs).astype(BF)

        loop(group // head, one)

    def out_proj():
        context = ct[...].T
        bo, g1, c1 = prm[2:3, :], prm[3:4, :], prm[4:5, :]
        w = weight(OUT)

        def tile(i):
            r = span(i, 128)
            h1 = x[r, :].astype(F32) + (h2[r, :] + bo)
            centred = h1 - jnp.mean(h1, -1, keepdims=True)
            inverse = lax.rsqrt(jnp.mean(centred * centred, -1, keepdims=True) + 1e-06)
            normed = centred * inverse
            n1[r, :] = normed
            rs1[r, :] = inverse
            y1b[r, :] = (normed * g1 + c1).astype(BF)

        h2[...] = dot(context, w)
        loop(seq // 128, tile)

    def feed_up(j):
        def tile(i):
            cols = span(i, 256)
            wide_cols = pl.ds(pl.multiple_of(j * model + i * 256, 256), 256)
            u = dot(y1b[...], weight(IN + j, cols)) + prm[8 + j : 9 + j, cols]
            phi = 0.5 * (1.0 + lax.erf(u * SQRT_HALF))
            act[:, wide_cols] = (u * phi).astype(BF)
            dact[:, wide_cols] = (phi + u * (jnp.exp(-0.5 * u * u) * INV_SQRT_TAU)).astype(BF)

        loop(model // 256, tile)

    def feed_down():
        def tile(i):
            cols = span(i, 256)
            w = wd[:, :, :, :, :, :, cols].reshape(hidden, 256)
            y1 = n1[:, cols] * prm[3:4, cols] + prm[4:5, cols]
            h2[:, cols] = y1 + (dot(act[...], w) + prm[5:6, cols])

        loop(model // 256, tile)

    def vsum(row, value):
        vg[row : row + 1, :] += jnp.sum(value, axis=0, keepdims=True)

    def norm_back(dn, n, inverse):
        return (dn - jnp.mean(dn, -1, keepdims=True) - n * jnp.mean(dn * n, -1, keepdims=True)) * inverse

    def norm_two():
        g2, c2 = prm[6:7, :], prm[7:8, :]

        def tile(i):
            r = span(i, 128)
            h = h2[r, :]
            centred = h - jnp.mean(h, -1, keepdims=True)
            inverse = lax.rsqrt(jnp.mean(centred * centred, -1, keepdims=True) + 1e-06)
            n = centred * inverse
            dcx[r, :] = (n * g2 + c2).astype(BF)
            dy = cot[r, :].astype(F32)
            vsum(6, dy * n)
            vsum(7, dy)
            dh = norm_back(dy * g2, n, inverse)
            h2[r, :] = dh
            low = dh.astype(BF)
            dfb[r, :] = low
            vsum(5, low.astype(F32))

        loop(seq // 128, tile)

    def grad_down():
        def tile(i):
            cols = span(i, 2 * 4 * rows)
            g = dot(act[:, cols], dfb[...], TN).astype(BF).reshape(CS, 4, rows, model)
            zz = i // YS
            gd[zz // ZL, lax.rem(zz, ZL), lax.rem(i, YS)] = g

        loop(ZS * YS, tile)

    def grad_act(j):
        def tile(t):
            i = 2 * j + t
            cols = span(i, 2 * 4 * rows)
            zz = i // YS
            w = wd[zz // ZL, lax.rem(zz, ZL), lax.rem(i, YS)].reshape(2 * 4 * rows, model)
            du = (dot(dfb[...], w, NT) * dact[:, cols].astype(F32)).astype(BF)
            dact[:, cols] = du
            total = jnp.sum(du.astype(F32), axis=0, keepdims=True)
            if t == 0:
                vg[8 + j : 9 + j, 0:half] = total
            else:
                vg[8 + j : 9 + j, half:] = total

        tile(0)
        tile(1)

    def grad_in(j):
        if j == 0:
            y1t[...] = y1b[...].T

        def tile(i):
            cols = span(i, 256)
            wide_cols = pl.ds(pl.multiple_of(j * model + i * 256, 256), 256)
            g = dot(y1t[...], dact[:, wide_cols]).astype(BF)
            wd[:, :, :, :, j, :, cols] = g.reshape(ZH, ZL, YS, CS, rows, 256)

        loop(model // 256, tile)

    def grad_normed(j):
        def tile(i):
            cols = span(i, half)
            w = wa[IN + j, i].reshape(half, model)
            h2[:, cols] += dot(dact[:, j * model : (j + 1) * model], w, NT)

        loop(2, tile)

    def norm_one_back():
        g1 = prm[3:4, :]

        def tile(i):
            r = span(i, 128)
            dy, n = h2[r, :], n1[r, :]
            vsum(3, dy * n)
            vsum(4, dy)
            dh = norm_back(dy * g1, n, rs1[r, :])
            h2[r, :] = dh
            low = dh.astype(BF)
            dfb[r, :] = low
            vsum(2, low.astype(F32))

        loop(seq // 128, tile)

    def grad_out():
        g = dot(ct[...], dfb[...]).astype(BF)
        go[0] = g.reshape(ZH, ZL, YS, CS, rows, model)

    def grad_context():
        vt[...] = x[...].T
        dcx[...] = dot(dfb[...], weight(OUT), NT).astype(BF)

    def attend_back(g):
        def one(j):
            cols = span(j, pair)
            keys = pl.ds(pl.multiple_of(group + j * pair, pair), pair)
            vals = pl.ds(pl.multiple_of(2 * group + j * pair, pair), pair)
            wide_cols = pl.ds(pl.multiple_of(g * group + j * pair, pair), pair)
            lane = lax.broadcasted_iota(jnp.int32, (seq, pair), 1) // head
            dc = dcx[:, wide_cols]
            q, k, v = qkv[g, :, cols], qkv[g, :, keys], qkv[g, :, vals]
            kt = k.T
            dk, dv, dq = [], [], []
            for e in range(2):
                probs = pt[g, 2 * j + e]
                dv.append(dot(probs, dc))
                dp = dot(jnp.where(lane == e, v, jnp.zeros((), BF)), dc, NT)
                p32 = probs.astype(F32)
                t = p32 * dp
                ds = (t - p32 * jnp.sum(t, axis=0, keepdims=True)).astype(BF)
                dk.append(dot(ds, q))
                dq.append((dot(kt[e * head : (e + 1) * head, :], ds) * head**-0.5).astype(BF))
            qkv[g, :, cols] = jnp.concatenate(dq, axis=0).T
            qkv[g, :, keys] = jnp.where(lane == 0, dk[0], dk[1]).astype(BF)
            qkv[g, :, vals] = jnp.where(lane == 0, dv[0], dv[1]).astype(BF)

        loop(group // pair, one)
        grouped = span(g, group)
        vg[0:1, grouped] = jnp.sum(qkv[g, :, 0:group].astype(F32), axis=0, keepdims=True)
        vg[1:2, grouped] = jnp.sum(qkv[g, :, 2 * group :].astype(F32), axis=0, keepdims=True)

    def grad_qkv(g):
        r = dot(vt[...], qkv[g]).astype(BF)
        wa[IN + g] = r.reshape(ZH, ZL, YS, CS, rows, model)

    def grad_x():
        total = h2[...]
        for g in range(3):
            total = total + dot(qkv[g], weight(g), NT)
        n1[...] = total

    left, right = pl.ds(0, half), pl.ds(half, half)

    def gpiece(k, zi, yy, cc, cols=ALL):
        if k < 4:
            return gd.at[(*zi, yy, cc, k, ALL, cols)]
        if k < 8:
            return wd.at[(*zi, yy, cc, k - 4, ALL, cols)]
        if k < 9:
            return go.at[(0, *zi, yy, cc, ALL, cols)]
        return wa.at[(IN + k - 9, *zi, yy, cc, ALL, cols)]

    every = (ALL, ALL)
    mine = (zh, zl)

    def at_z(zz):
        return (zz // ZL, lax.rem(zz, ZL))

    def r_core(k):
        return remote(gpiece(k, every, ALL, 1 - c), rcore.at[k], rsc.at[k], rrc.at[k], sibling)

    def r_ya(k):
        return remote(gpiece(k, every, 1 - y, c, left), rya.at[k], rsya.at[k], rrya.at[k], across_y)

    def r_xb(k):
        return remote(gpiece(k, (ALL, 1 - px), ALL, c, right), rxb.at[k], rsxb.at[k], rrxb.at[k], across_x)

    def r_za(k, dz):
        piece = gpiece(k, at_z(ahead(dz)), y, c, left)
        return remote(piece, rza.at[k, dz - 1], rsza.at[k, dz - 1], rrza.at[k, dz - 1], device(ahead(dz), y, c, px))

    def r_yb(k):
        return remote(gpiece(k, (ALL, px), 1 - y, c, right), ryb.at[k], rsyb.at[k], rryb.at[k], across_y)

    def r_xa(k):
        return remote(gpiece(k, mine, y, c, left), rxa.at[k], rsxa.at[k], rrxa.at[k], across_x)

    def r_zb(k, dz):
        piece = gpiece(k, at_z(ahead(dz)), y, c, right)
        return remote(piece, rzb.at[k, dz - 1], rszb.at[k, dz - 1], rrzb.at[k, dz - 1], device(ahead(dz), y, c, px))

    def r_fb(k):
        return remote(gpiece(k, mine, y, c, right), rfb.at[k], rsfb.at[k], rrfb.at[k], across_x)

    same = zl == px

    def to_parity(dz, act_on):
        if dz == 2:
            pl.when(same)(act_on)
        else:
            pl.when(jnp.logical_not(same))(act_on)

    def add_into(ref, *others):
        total = ref[...].astype(F32)
        for other in others:
            total = total + other[...].astype(F32)
        ref[...] = total.astype(BF)

    def n_chunk(k):
        return 0 <= k < CHUNKS

    def r0(k):
        if n_chunk(k):
            r_core(k).start()
        if k == CHUNKS - 1:
            remote(gv.at[:, :, :, 1 - c], rv_core, wsc, wrc, sibling).start()

    def r1(k):
        if not n_chunk(k):
            return
        r_core(k).wait_recv()

        def add(i):
            piece = gpiece(k, at_z(i), ALL, c)
            add_into(piece, rcore.at[(k, *at_z(i))])

        loop(ZS, add)
        r_ya(k).start()
        r_xb(k).start()
        if k == CHUNKS - 1:
            remote(gv.at[:, :, :, 1 - c], rv_core, wsc, wrc, sibling).wait_recv()
            add_into(gv.at[:, :, :, c], rv_core)
            remote(gv.at[:, :, 1 - y, c], rv_y, wsy, wry, across_y).start()

    def v_rz(dz):
        return remote(
            gv.at[(*at_z(ahead(dz)), y, c)], rv_z.at[dz - 1], wsz.at[dz - 1], wrz.at[dz - 1],
            device(ahead(dz), y, c, px),
        )

    def v_rx():
        return remote(gv.at[(*mine, y, c)], rv_x, wsx, wrx, across_x)

    def r2(k):
        if not n_chunk(k):
            return
        r_ya(k).wait_recv()
        add_into(gpiece(k, every, y, c, left), rya.at[k])
        for dz in (1, 2, 3):
            r_za(k, dz).start()
        r_xb(k).wait_recv()
        add_into(gpiece(k, (ALL, px), ALL, c, right), rxb.at[k])
        r_yb(k).start()
        if k == CHUNKS - 1:
            remote(gv.at[:, :, 1 - y, c], rv_y, wsy, wry, across_y).wait_recv()
            add_into(gv.at[:, :, y, c], rv_y)
            for dz in (1, 2, 3):
                v_rz(dz).start()

    def r3(k):
        if not n_chunk(k):
            return
        r_yb(k).wait_recv()
        add_into(gpiece(k, (ALL, px), y, c, right), ryb.at[k])
        for dz in (1, 2, 3):
            to_parity(dz, lambda dz=dz: r_zb(k, dz).start())
        for dz in (1, 2, 3):
            r_za(k, dz).wait_recv()
        add_into(gpiece(k, mine, y, c, left), rza.at[k, 0], rza.at[k, 1], rza.at[k, 2])
        r_xa(k).start()
        if k == CHUNKS - 1:
            for dz in (1, 2, 3):
                v_rz(dz).wait_recv()
            add_into(gv.at[(*mine, y, c)], rv_z.at[0], rv_z.at[1], rv_z.at[2])
            v_rx().start()

    def r4(k):
        if not n_chunk(k):
            return

        @pl.when(same)
        def _():
            for dz in (1, 2, 3):
                r_zb(k, dz).wait_recv()
            add_into(gpiece(k, mine, y, c, right), rzb.at[k, 0], rzb.at[k, 1], rzb.at[k, 2])
            r_fb(k).start()
            fin[k, :, right] = gpiece(k, mine, y, c, right)[...].astype(F32)

        r_xa(k).wait_recv()
        fin[k, :, left] = gpiece(k, mine, y, c, left)[...].astype(F32) + rxa[k].astype(F32)
        if k == CHUNKS - 1:
            v_rx().wait_recv()
            fv[...] = gv[(*mine, y, c)].astype(F32) + rv_x[...].astype(F32)

    stores = []

    def store(src, dst):
        cp = pltpu.make_async_copy(src, dst, s_store.at[len(stores)])
        cp.start()
        stores.append(cp)

    def r5(k):
        if not n_chunk(k):
            return

        @pl.when(jnp.logical_not(same))
        def _():
            r_fb(k).wait_recv()
            fin[k, :, right] = rfb[k].astype(F32)

        if k < 4:
            store(fin.at[k], gdown_hbm.at[pl.ds(k * rows, rows)])
        elif k < 8:
            store(fin.at[k], gin_hbm.at[:, pl.ds((k - 4) * model, model)])
        elif k < 9:
            store(fin.at[k], gout_hbm)
        else:
            for part in range(3):
                store(
                    fin.at[k, :, pl.ds(part * group, group)],
                    gqkv_hbm.at[:, pl.ds(part * model + (k - 9) * group, group)],
                )

    def sums_sent(k):
        r_core(k).wait_send()
        r_ya(k).wait_send()
        r_xb(k).wait_send()
        r_yb(k).wait_send()
        r_xa(k).wait_send()
        for dz in (1, 2, 3):
            r_za(k, dz).wait_send()
            to_parity(dz, lambda dz=dz: r_zb(k, dz).wait_send())
        pl.when(same)(lambda: r_fb(k).wait_send())

    vg[...] = jnp.zeros_like(vg)
    e1(0)
    e1(1)
    load_x.wait()

    def forward(k):
        if k < 0:
            return
        if k < OUT:
            if k == 0:
                spread_params()
            project(k)
            attend(k)
        elif k < IN:
            out_proj()
        elif k < DOWN:
            feed_up(k - IN)

    for t in range(1, CHUNKS + 4):
        e5(t - 4)
        e4(t - 3)
        e3(t - 2)
        e2(t - 1)
        e1(t + 1)
        forward(t - 4)
    load_cot.wait()
    feed_down()
    norm_two()
    store(dcx, out_hbm.at[0])
    grad_down()
    for k in range(4):
        r0(k)
    r1(0)
    grad_act(0)
    grad_act(1)
    r1(1)
    r2(0)
    grad_act(2)
    grad_act(3)
    r1(2)
    r2(1)
    r3(0)
    for k in range(DOWN, CHUNKS):
        sent(k)
    grad_in(0)
    r0(4)
    grad_in(1)
    r0(5)
    r1(3)
    r2(2)
    r3(1)
    r4(0)
    grad_in(2)
    r0(6)
    grad_in(3)
    r0(7)
    r1(4)
    r2(3)
    r3(2)
    r4(1)
    r5(0)
    grad_normed(0)
    grad_normed(1)
    r1(5)
    r2(4)
    r3(3)
    r4(2)
    r5(1)
    grad_normed(2)
    grad_normed(3)
    norm_one_back()
    r1(6)
    r2(5)
    r3(4)
    r4(3)
    r5(2)
    stores[0].wait()
    grad_out()
    r0(8)
    grad_context()
    for k in range(IN, DOWN):
        sent(k)
    r1(7)
    r2(6)
    r3(5)
    r4(4)
    r5(3)
    attend_back(0)
    grad_qkv(0)
    r0(9)
    r1(8)
    r2(7)
    r3(6)
    r4(5)
    r5(4)
    attend_back(1)
    grad_qkv(1)
    r0(10)
    r1(9)
    r2(8)
    r3(7)
    r4(6)
    r5(5)
    attend_back(2)
    grad_qkv(2)
    gather_grads()
    r0(11)
    r1(10)
    r2(9)
    r3(8)
    r4(7)
    r5(6)
    r1(11)
    grad_x()
    store(n1, gtok_hbm.at[0])
    r2(10)
    r3(9)
    r4(8)
    r5(7)
    r2(11)
    r3(10)
    r4(9)
    r5(8)
    r3(11)
    r4(10)
    r5(9)
    r4(11)
    store(fv, gvec_hbm)
    r5(10)
    r5(11)
    for k in range(IN):
        sent(k)
    vec_sent()
    for k in range(CHUNKS):
        sums_sent(k)
    remote(gv.at[:, :, :, 1 - c], rv_core, wsc, wrc, sibling).wait_send()
    remote(gv.at[:, :, 1 - y, c], rv_y, wsy, wry, across_y).wait_send()
    for dz in (1, 2, 3):
        v_rz(dz).wait_send()
    v_rx().wait_send()
    for cp in stores[1:]:
        cp.wait()


def fused_layer(tokens, lengths, w_qkv, w_out, w_in, w_down, norms_biases, cotangent):
    seq, model = tokens.shape[1:]
    rows = w_qkv.shape[0]
    hidden = w_in.shape[1]
    half = model // 2
    group = model // 3
    segments = jnp.pad(norms_biases.reshape(3, -1), ((0, 13), (0, 256 - norms_biases.shape[0] // 3)))
    vm, dma = pltpu.VMEM, pltpu.SemaphoreType.DMA
    grid = (ZH, ZL, YS, CS)
    n = CHUNKS
    scratch = [
        vm((DOWN, *grid, rows, model), BF),
        vm((*grid, 4, rows, model), BF),
        vm((*grid, 16, 256), BF),
        vm((*grid, 4, rows, model), BF),
        vm((1, *grid, rows, model), BF),
        vm((*grid, 16, 256), BF),
        vm((n, ZH, ZL, YS, rows, model), BF),
        vm((n, ZH, ZL, rows, half), BF),
        vm((n, ZH, YS, rows, half), BF),
        vm((n, 3, rows, half), BF),
        vm((n, ZH, rows, half), BF),
        vm((n, 3, rows, half), BF),
        vm((n, rows, half), BF),
        vm((n, rows, half), BF),
        vm((ZH, ZL, YS, 16, 256), BF),
        vm((ZH, ZL, 16, 256), BF),
        vm((3, 16, 256), BF),
        vm((16, 256), BF),
        vm((n, rows, model), F32),
        vm((16, 256), F32),
        vm((seq, model), BF),
        vm((seq, model), BF),
        vm((3, seq, model), BF),
        vm((model, seq), BF),
        vm((3, group // (model // HEADS), seq, seq), BF),
        vm((model, seq), BF),
        vm((seq, model), F32),
        vm((seq, model), BF),
        vm((model, seq), BF),
        vm((seq, hidden), BF),
        vm((seq, hidden), BF),
        vm((seq, model), F32),
        vm((seq, model), BF),
        vm((seq, model), BF),
        vm((seq, 1), F32),
        vm((16, model), F32),
        vm((16, model), F32),
        dma((n, 3)), dma, dma((2,)), dma((21,)),
        dma((n, 3)), dma((n, 3)), dma((n,)), dma((n,)), dma((n, 3)), dma((n, 3)),
        dma((n,)), dma((n,)), dma((n,)), dma((n,)),
        dma((3,)), dma((3,)), dma, dma, dma, dma,
        dma((n,)), dma((n,)), dma((n,)), dma((n,)), dma((n,)), dma((n,)), dma((n, 3)), dma((n, 3)),
        dma((n,)), dma((n,)), dma((n, 3)), dma((n, 3)), dma((n,)), dma((n,)), dma((n,)), dma((n,)),
        dma, dma, dma, dma, dma((3,)), dma((3,)), dma, dma,
    ]
    hbm = pl.BlockSpec(memory_space=pl.ANY)
    shape = jax.ShapeDtypeStruct
    outs = pl.pallas_call(
        layer_kernel,
        out_shape=(
            shape(tokens.shape, BF),
            shape(tokens.shape, F32),
            shape(w_qkv.shape, F32),
            shape(w_out.shape, F32),
            shape(w_in.shape, F32),
            shape(w_down.shape, F32),
            shape((16, 256), F32),
        ),
        in_specs=[hbm, pl.BlockSpec(memory_space=pltpu.SMEM)] + [hbm] * 6,
        out_specs=(hbm,) * 7,
        scratch_shapes=scratch,
        compiler_params=pltpu.CompilerParams(
            collective_id=0, has_side_effects=True, vmem_limit_bytes=64 << 20
        ),
        name="layer",
    )(tokens, lengths, w_qkv, w_out, w_in, w_down, segments, cotangent)
    grad_vector = outs[6][:3, : norms_biases.shape[0] // 3].reshape(-1)
    return (*outs[:6], grad_vector)


def norm_rows(values, gain_row, shift_row):
    average = jnp.mean(values, -1, keepdims=True)
    centred = values - average
    spread = jnp.mean(centred * centred, -1, keepdims=True)
    return centred * lax.rsqrt(spread + 1e-06) * gain_row + shift_row


def gelu_exact(values):
    return jax.nn.gelu(values, approximate=False)


def column_sum(values):
    return jnp.sum(values.astype(jnp.float32), 0)


def split_vector(vector, model_width, hidden_width):
    segments = [
        vector[position * model_width : (position + 1) * model_width] for position in range(8)
    ]
    return segments + [vector[8 * model_width : 8 * model_width + hidden_width]]


def pair_blocks(projected, head_count):
    row_count = projected.shape[0]
    pair_count = head_count // 2
    pair_width = projected.shape[1] // (3 * pair_count)
    return projected.reshape(row_count, 3, pair_count, pair_width).transpose(2, 1, 0, 3)


def unpair_blocks(blocks):
    pair_count = blocks.shape[0]
    row_count = blocks.shape[2]
    pair_width = blocks.shape[3]
    return blocks.transpose(2, 1, 0, 3).reshape(row_count, 3 * pair_count * pair_width)


def pair_scores(head_block, usable, factor):
    row_count = head_block.shape[1]
    queries = head_block[0].reshape(row_count, 2, -1)
    key_rows = head_block[1].reshape(row_count, 2, -1)
    values = head_block[2].reshape(row_count, 2, -1)
    scores = (
        jnp.einsum("qhd,khd->hqk", queries, key_rows, preferred_element_type=jnp.float32) * factor
    )
    return (queries, key_rows, values, jnp.where(usable[None, None, :], scores, -1000000000.0))


def attention_forward(blocks, usable, factor):

    def one_pair(head_block):
        queries, key_rows, values, scores = pair_scores(head_block, usable, factor)
        highest = jnp.max(scores, -1, keepdims=True)
        raised = jnp.exp(scores - highest)
        summed = jnp.sum(raised, -1, keepdims=True)
        attend = (raised / summed).astype(jnp.bfloat16)
        context = jnp.einsum("hqk,khd->qhd", attend, values, preferred_element_type=jnp.float32)
        return (context.reshape(context.shape[0], -1), highest[..., 0] + jnp.log(summed[..., 0]))

    return lax.map(one_pair, blocks)


def attention_backward(blocks, grad_pairs, log_totals, usable, factor):

    def one_pair(pair_inputs):
        head_block, grad_context, log_total = pair_inputs
        queries, key_rows, values, scores = pair_scores(head_block, usable, factor)
        attend = jnp.exp(scores - log_total[..., None])
        row_count = grad_context.shape[0]
        grad_heads = grad_context.reshape(row_count, 2, -1)
        grad_values = jnp.einsum(
            "hqk,qhd->khd",
            attend.astype(jnp.bfloat16),
            grad_heads,
            preferred_element_type=jnp.float32,
        )
        grad_attend = jnp.einsum(
            "qhd,khd->hqk", grad_heads, values, preferred_element_type=jnp.float32
        )
        grad_scores = attend * (grad_attend - jnp.sum(attend * grad_attend, -1, keepdims=True))
        grad_low = grad_scores.astype(jnp.bfloat16)
        grad_queries = (
            jnp.einsum("hqk,khd->qhd", grad_low, key_rows, preferred_element_type=jnp.float32)
            * factor
        )
        grad_keys = (
            jnp.einsum("hqk,qhd->khd", grad_low, queries, preferred_element_type=jnp.float32)
            * factor
        )
        return jnp.stack(
            [
                grad_queries.reshape(row_count, -1),
                grad_keys.reshape(row_count, -1),
                grad_values.reshape(row_count, -1),
            ]
        )

    return lax.map(one_pair, (blocks, grad_pairs, log_totals))


def layer_forward(inputs, length, weights):
    w_qkv, w_out, w_in, w_down, vector = weights
    row_count, model_width = inputs.shape
    hidden_width = w_in.shape[1]
    params = split_vector(vector.astype(jnp.float32), model_width, hidden_width)
    joined_bias = jnp.concatenate([params[0], jnp.zeros((model_width,), jnp.float32), params[1]])
    projected = (jnp.dot(inputs, w_qkv, preferred_element_type=jnp.float32) + joined_bias).astype(
        jnp.bfloat16
    )
    blocks = pair_blocks(projected, HEADS)
    usable = jnp.arange(row_count) < length
    factor = (model_width // HEADS) ** (-0.5)
    context_pairs, log_totals = attention_forward(blocks, usable, factor)
    context = context_pairs.transpose(1, 0, 2).reshape(row_count, model_width).astype(jnp.bfloat16)
    resid_one = inputs.astype(jnp.float32) + (
        jnp.dot(context, w_out, preferred_element_type=jnp.float32) + params[2]
    )
    normed_one = norm_rows(resid_one, params[3], params[4])
    normed_low = normed_one.astype(jnp.bfloat16)
    pre_act = jnp.dot(normed_low, w_in, preferred_element_type=jnp.float32) + params[8]
    activated = gelu_exact(pre_act).astype(jnp.bfloat16)
    resid_two = normed_one + (
        jnp.dot(activated, w_down, preferred_element_type=jnp.float32) + params[5]
    )
    result = norm_rows(resid_two, params[6], params[7])
    saved = (
        params,
        blocks,
        usable,
        factor,
        log_totals,
        context,
        resid_one,
        normed_low,
        pre_act,
        activated,
        resid_two,
    )
    return (result, saved)


def layer_backward(inputs, length, grad_result, weights):
    w_qkv, w_out, w_in, w_down, vector = weights
    unused_result, saved = layer_forward(inputs, length, weights)
    (
        params,
        blocks,
        usable,
        factor,
        log_totals,
        context,
        resid_one,
        normed_low,
        pre_act,
        activated,
        resid_two,
    ) = saved
    row_count, model_width = inputs.shape
    unused_two, norm_two_back = jax.vjp(norm_rows, resid_two, params[6], params[7])
    grad_two, grad_gain_two, grad_shift_two = norm_two_back(grad_result)
    grad_feed = grad_two.astype(jnp.bfloat16)
    grad_down = jnp.einsum("sf,sd->fd", activated, grad_feed, preferred_element_type=jnp.float32)
    grad_act = jnp.einsum("sd,fd->sf", grad_feed, w_down, preferred_element_type=jnp.float32)
    unused_act, gelu_back = jax.vjp(gelu_exact, pre_act)
    grad_pre = gelu_back(grad_act)[0].astype(jnp.bfloat16)
    grad_in = jnp.einsum("sd,sf->df", normed_low, grad_pre, preferred_element_type=jnp.float32)
    grad_normed = grad_two + jnp.einsum(
        "sf,df->sd", grad_pre, w_in, preferred_element_type=jnp.float32
    )
    unused_one, norm_one_back = jax.vjp(norm_rows, resid_one, params[3], params[4])
    grad_one, grad_gain_one, grad_shift_one = norm_one_back(grad_normed)
    grad_attended = grad_one.astype(jnp.bfloat16)
    grad_out = jnp.einsum("sd,se->de", context, grad_attended, preferred_element_type=jnp.float32)
    grad_context = jnp.einsum(
        "se,de->sd", grad_attended, w_out, preferred_element_type=jnp.float32
    ).astype(jnp.bfloat16)
    grad_pairs = grad_context.reshape(row_count, HEADS // 2, -1).transpose(1, 0, 2)
    grad_blocks = attention_backward(blocks, grad_pairs, log_totals, usable, factor)
    grad_projected = unpair_blocks(grad_blocks).astype(jnp.bfloat16)
    grad_qkv = jnp.einsum("sd,se->de", inputs, grad_projected, preferred_element_type=jnp.float32)
    grad_inputs = grad_one + jnp.einsum(
        "se,de->sd", grad_projected, w_qkv, preferred_element_type=jnp.float32
    )
    projected_sums = column_sum(grad_projected)
    grad_vector = jnp.concatenate(
        [
            projected_sums[:model_width],
            projected_sums[2 * model_width :],
            column_sum(grad_attended),
            grad_gain_one,
            grad_shift_one,
            column_sum(grad_feed),
            grad_gain_two,
            grad_shift_two,
            column_sum(grad_pre),
        ]
    )
    return (grad_inputs, (grad_qkv, grad_out, grad_in, grad_down, grad_vector))


def local(tokens, lengths, w_qkv, w_out, w_in, w_down, norms_biases, cotangent):
    weights = (
        lax.all_gather(w_qkv, "wide", axis=0, tiled=True),
        lax.all_gather(w_out, "wide", axis=0, tiled=True),
        lax.all_gather(w_in, "wide", axis=0, tiled=True),
        lax.all_gather(w_down, "wide", axis=0, tiled=True),
        lax.all_gather(norms_biases, "wide", axis=0, tiled=True),
    )

    def forward_one(sequence):
        return layer_forward(sequence[0], sequence[1], weights)[0].astype(jnp.bfloat16)

    output = lax.map(forward_one, (tokens, lengths))
    second_copy = (
        lax.all_gather(w_qkv, "wide", axis=0, tiled=True),
        lax.all_gather(w_out, "wide", axis=0, tiled=True),
        lax.all_gather(w_in, "wide", axis=0, tiled=True),
        lax.all_gather(w_down, "wide", axis=0, tiled=True),
        lax.all_gather(norms_biases, "wide", axis=0, tiled=True),
    )
    running = tuple((jnp.zeros(member.shape, jnp.float32) for member in second_copy))

    def advance(totals, sequence):
        grad_inputs, gradients = layer_backward(
            sequence[0], sequence[1], sequence[2].astype(jnp.float32), second_copy
        )
        return (jax.tree.map(jnp.add, totals, gradients), grad_inputs)

    totals, grad_tokens = lax.scan(advance, running, (tokens, lengths, cotangent))
    owned_rows = (
        lax.psum_scatter(
            totals[0].astype(jnp.bfloat16), "wide", scatter_dimension=0, tiled=True
        ).astype(jnp.float32),
        lax.psum_scatter(
            totals[1].astype(jnp.bfloat16), "wide", scatter_dimension=0, tiled=True
        ).astype(jnp.float32),
        lax.psum_scatter(
            totals[2].astype(jnp.bfloat16), "wide", scatter_dimension=0, tiled=True
        ).astype(jnp.float32),
        lax.psum_scatter(
            totals[3].astype(jnp.bfloat16), "wide", scatter_dimension=0, tiled=True
        ).astype(jnp.float32),
        lax.psum_scatter(
            totals[4].astype(jnp.bfloat16), "wide", scatter_dimension=0, tiled=True
        ).astype(jnp.float32),
    )
    summed_all = (
        lax.psum(owned_rows[0].astype(jnp.bfloat16), "narrow").astype(jnp.float32),
        lax.psum(owned_rows[1].astype(jnp.bfloat16), "narrow").astype(jnp.float32),
        lax.psum(owned_rows[2].astype(jnp.bfloat16), "narrow").astype(jnp.float32),
        lax.psum(owned_rows[3].astype(jnp.bfloat16), "narrow").astype(jnp.float32),
        lax.psum(owned_rows[4].astype(jnp.bfloat16), "narrow").astype(jnp.float32),
    )
    return (
        output,
        grad_tokens,
        summed_all[0],
        summed_all[1],
        summed_all[2],
        summed_all[3],
        summed_all[4],
    )


def solution(mesh):
    in_specs = (
        P(("wide", "narrow"), None, None),
        P(("wide", "narrow")),
        P("wide", None),
        P("wide", None),
        P("wide", None),
        P("wide", None),
        P("wide"),
        P(("wide", "narrow"), None, None),
    )
    out_specs = (
        P(("wide", "narrow"), None, None),
        P(("wide", "narrow"), None, None),
        P("wide", None),
        P("wide", None),
        P("wide", None),
        P("wide", None),
        P("wide"),
    )
    chips = (ZS * YS * CS, 2)
    fused = tuple(mesh.shape[axis] for axis in ("wide", "narrow")) == chips
    step = fused_layer if fused else local
    return jax.shard_map(step, mesh=mesh, in_specs=in_specs, out_specs=out_specs, check_vma=False)
```

```python
import functools

import jax
import jax.numpy as jnp
import numpy as np
from jax import lax
from jax.experimental import pallas as pl
from jax.experimental.pallas import tpu as pltpu
from jax.sharding import PartitionSpec as P

HEADS = 12
MESH = pl.DeviceIdType.MESH
BF = jnp.bfloat16
F32 = jnp.float32
NT = (((1,), (1,)), ((), ()))
TN = (((0,), (0,)), ((), ()))
ZH, ZL, YS, CS = 2, 2, 2, 2
ZS = ZH * ZL
QKV, OUT, IN, DOWN, CHUNKS = 0, 3, 4, 8, 12
CUTS = 1
PARTS = CUTS * CHUNKS
LAGS = (2, 1, 1, 1)
SQRT_HALF = 0.7071067811865476
INV_SQRT_TAU = 0.3989422804014327


def dot(left, right, dims=None):
    if dims is None:
        return jnp.dot(left, right, preferred_element_type=F32)
    return lax.dot_general(left, right, dims, preferred_element_type=F32)


def loop(count, body):
    def step(index, carry):
        body(index)
        return carry

    lax.fori_loop(0, count, step, 0)


def span(index, size):
    return pl.ds(pl.multiple_of(index * size, size), size)


def layer_kernel(
    x_hbm, len_ref, wqkv_hbm, wout_hbm, win_hbm, wdown_hbm, vec_hbm, cot_hbm,
    out_hbm, gtok_hbm, gqkv_hbm, gout_hbm, gin_hbm, gdown_hbm, gvec_hbm,
    wa, wd, vb, gd, go, gv, rcore, rya, rxb, rza, ryb, rzb, rxa, rfb, rv_core, rv_y, rv_z, rv_x, fin, fv,
    x, cot, qkv, vt, pt, ct, n1, y1b, y1t, act, dact, h2, dfb, dcx, rs1, prm, vg,
    s_load, s_vload, s_io, s_store,
    g_sent, grz, gry, grx, grc, v_sent, vrz, vry, vrc,
    r_sent, rv_sent, rrc, rry, rrx, rrz, rrf, wrc, wry, wrz, wrx,
):
    seq, model = x.shape
    rows = wa.shape[-2]
    hidden = dact.shape[1]
    pair = 2 * (model // HEADS)
    head = model // HEADS
    group = model // 3
    half = model // 2
    wide = lax.axis_index("wide")
    px = lax.axis_index("narrow")
    c = lax.rem(wide, CS)
    y = lax.rem(wide // CS, YS)
    z = wide // (CS * YS)
    zl = lax.rem(z, ZL)
    zh = z // ZL

    def device(zz, yy, cc, xx):
        return ((zz * YS + yy) * CS + cc, xx)

    sibling = device(z, y, 1 - c, px)
    across_y = device(z, 1 - y, c, px)
    across_x = device(z, y, c, 1 - px)

    def ahead(dz):
        return lax.rem(z + dz, ZS)

    def behind(dz):
        return lax.rem(z + ZS - dz, ZS)

    def remote(src, dst, send, recv, where):
        return pltpu.make_async_remote_copy(
            src_ref=src, dst_ref=dst, send_sem=send, recv_sem=recv, device_id=where, device_id_type=MESH
        )

    ALL = slice(None)

    def drained(ref, sem):
        pltpu.make_async_copy(ref, ref, sem).wait()

    def rows_of(count):
        return x.at[pl.ds(0, count), pl.ds(0, model // CUTS)]

    def wpiece(k, zz, yy, cc, r=ALL):
        zi = (ALL, ALL) if zz is None else (zz // ZL, lax.rem(zz, ZL))
        if k < DOWN:
            return wa.at[(k, *zi, yy, cc, r)]
        return wd.at[(*zi, yy, cc, k - DOWN, r)]

    def load(src, dst, sem):
        cp = pltpu.make_async_copy(src, dst, sem)
        cp.start()
        return cp

    load_vec = load(vec_hbm, vb.at[zh, zl, y, c], s_vload)
    load_x = load(x_hbm.at[0], x, s_io.at[0])
    for k in range(CHUNKS):
        if k < OUT:
            for part in range(3):
                load(
                    wqkv_hbm.at[:, pl.ds(part * model + k * group, group)],
                    wa.at[k, zh, zl, y, c, :, pl.ds(part * group, group)],
                    s_load.at[k],
                )
        elif k < IN:
            load(wout_hbm, wa.at[k, zh, zl, y, c], s_load.at[k])
        elif k < DOWN:
            load(win_hbm.at[:, pl.ds((k - IN) * model, model)], wa.at[k, zh, zl, y, c], s_load.at[k])
        else:
            load(wdown_hbm.at[pl.ds((k - DOWN) * rows, rows)], wd.at[zh, zl, y, c, k - DOWN], s_load.at[k])
    load_cot = load(cot_hbm.at[0], cot, s_io.at[1])

    barrier = pltpu.get_barrier_semaphore()
    for where in (sibling, across_y, across_x, *(device(ahead(dz), y, c, px) for dz in (1, 2, 3))):
        pl.semaphore_signal(barrier, inc=1, device_id=where, device_id_type=MESH)
    pl.semaphore_wait(barrier, 6)

    third = rows // 3
    kept = pl.ds(pl.multiple_of(px * third, third), 2 * third)
    given = pl.ds(pl.multiple_of(px * 2 * third, third), third)
    taken = pl.ds(pl.multiple_of((1 - px) * 2 * third, third), third)

    def wcut(i, zz, yy, cc, r=ALL):
        cols = pl.ds((i % CUTS) * (model // CUTS), model // CUTS)
        k = i // CUTS
        zi = (ALL, ALL) if zz is None else (zz // ZL, lax.rem(zz, ZL))
        if k < DOWN:
            return wa.at[(k, *zi, yy, cc, r, cols)]
        return wd.at[(*zi, yy, cc, k - DOWN, r, cols)]

    def g_z(i, dz, source):
        piece = wcut(i, source, y, c, kept)
        return remote(piece, piece, g_sent.at[i], grz.at[i], device(ahead(dz), y, c, px))

    def g_y(i, dz, column):
        piece = wcut(i, behind(dz), column, c, kept)
        return remote(piece, piece, g_sent.at[i], gry.at[i], across_y)

    def g_x1(i, dz, r):
        piece = wcut(i, behind(dz), y, c, r)
        return remote(piece, piece, g_sent.at[i], grx.at[i], across_x)

    def g_x2(i, r):
        piece = wcut(i, None, 1 - y, c, r)
        return remote(piece, piece, g_sent.at[i], grx.at[i], across_x)

    def g_core(i, core):
        piece = wcut(i, None, ALL, core)
        return remote(piece, piece, g_sent.at[i], grc.at[i], sibling)

    def v_z(dz, source):
        piece = vb.at[source // ZL, lax.rem(source, ZL), y, c]
        return remote(piece, piece, v_sent, vrz, device(ahead(dz), y, c, px))

    def v_y(column):
        piece = vb.at[:, :, column, c]
        return remote(piece, piece, v_sent, vry, across_y)

    def v_core(core):
        piece = vb.at[:, :, :, core]
        return remote(piece, piece, v_sent, vrc, sibling)

    def e1(i):
        if not 0 <= i < PARTS:
            return
        if i % CUTS == 0:
            drained(x.at[pl.ds(0, rows)], s_load.at[i // CUTS])
        if i == 0:
            load_vec.wait()
            for dz in (1, 2, 3):
                v_z(dz, z).start()
        for dz in (1, 2, 3):
            g_z(i, dz, z).start()
        g_y(i, 0, y).start()

    def e2(i):
        if not 0 <= i < PARTS:
            return
        if i == 0:
            drained(rv_z, vrz)
            v_y(y).start()
        drained(rows_of(3 * 2 * third), grz.at[i])
        for dz in (1, 2, 3):
            g_y(i, dz, y).start()
            g_x1(i, dz, given).start()

    def e3(i):
        if not 0 <= i < PARTS:
            return
        if i == 0:
            v_y(1 - y).wait_recv()
            v_core(c).start()
        drained(rows_of(ZS * 2 * third), gry.at[i])
        g_x2(i, given).start()

    def e4(i):
        if not 0 <= i < PARTS:
            return
        drained(rows_of((ZS + ZS - 1) * third), grx.at[i])
        g_core(i, c).start()

    def e5(i):
        if not 0 <= i < PARTS:
            return
        if i == 0:
            v_core(1 - c).wait_recv()
        g_core(i, 1 - c).wait_recv()

    def sent(k):
        count = (3 + ZS) * 2 * third + (2 * ZS - 1) * third + ZS * YS * rows
        for i in range(CUTS * k, CUTS * (k + 1)):
            drained(qkv.at[:, pl.ds(0, count // 3), pl.ds(0, model // CUTS)], g_sent.at[i])

    def vec_sent():
        drained(x.at[pl.ds(0, 80)], v_sent)

    def place_matrix(k, lanes):
        i = lax.broadcasted_iota(jnp.int32, (lanes, model), 0)
        j = lax.broadcasted_iota(jnp.int32, (lanes, model), 1)
        quarter = model // 4
        return jnp.where((i < quarter) & (j == i + k * quarter), 1.0, 0.0).astype(BF)

    def pick_matrix(k, count, total, slot):
        b = lax.broadcasted_iota(jnp.int32, (count, total), 0)
        r = lax.broadcasted_iota(jnp.int32, (count, total), 1)
        segment = 4 * b + k
        return jnp.where((r == slot * (segment // 3) + lax.rem(segment, 3)) & (b < 12), 1.0, 0.0).astype(BF)

    def spread_params():
        lanes = vb.shape[-1]
        segments = vb[...].reshape(-1, lanes)
        total = None
        for k in range(4):
            picked = dot(pick_matrix(k, 16, segments.shape[0], vb.shape[-2]), segments).astype(BF)
            part = dot(picked, place_matrix(k, lanes))
            total = part if total is None else total + part
        prm[...] = total

    def gather_grads():
        lanes = gv.shape[-1]
        low = vg[...].astype(BF)
        total = None
        for k in range(4):
            cut = dot(low, place_matrix(k, lanes), NT).astype(BF)
            part = dot(pick_matrix(k, 16, 16 * gv.shape[-2], gv.shape[-2]), cut, TN)
            total = part if total is None else total + part
        gv[...] = total.astype(BF).reshape(gv.shape)

    def weight(k, cols=ALL):
        block = wa[k, :, :, :, :, :, cols]
        return block.reshape(-1, block.shape[-1])

    def project(g):
        grouped = span(g, group)
        joined = dot(x[...], weight(g))
        q = (joined[:, :group] + prm[0:1, grouped]).astype(BF)
        qkv[g, :, 0:group] = q * jnp.asarray(head**-0.5, BF)
        qkv[g, :, group : 2 * group] = joined[:, group : 2 * group].astype(BF)
        v = (joined[:, 2 * group :] + prm[1:2, grouped]).astype(BF)
        qkv[g, :, 2 * group :] = v
        vt[grouped, :] = v.T

    def attend(g):
        length = len_ref[0]

        def one(h):
            cols = span(h // 2, pair)
            keys = pl.ds(pl.multiple_of(group + (h // 2) * pair, pair), pair)
            lane = lax.broadcasted_iota(jnp.int32, (seq, pair), 1) // head
            masked = jnp.where(lane == lax.rem(h, 2), qkv[g, :, keys], jnp.zeros((), BF))
            scores = dot(masked, qkv[g, :, cols], NT)
            key = lax.broadcasted_iota(jnp.int32, scores.shape, 0)
            scores = jnp.where(key < length, scores, -1000000000.0)
            raised = jnp.exp(scores - jnp.max(scores, axis=0, keepdims=True))
            probs = (raised * (1.0 / jnp.sum(raised, axis=0, keepdims=True))).astype(BF)
            pt[g, h] = probs
            mine = pl.ds(pl.multiple_of(g * group + h * head, head), head)
            ct[mine, :] = dot(vt[mine, :], probs).astype(BF)

        loop(group // head, one)

    def out_proj():
        context = ct[...].T
        bo, g1, c1 = prm[2:3, :], prm[3:4, :], prm[4:5, :]
        w = weight(OUT)

        def tile(i):
            r = span(i, 128)
            h1 = x[r, :].astype(F32) + (h2[r, :] + bo)
            centred = h1 - jnp.mean(h1, -1, keepdims=True)
            inverse = lax.rsqrt(jnp.mean(centred * centred, -1, keepdims=True) + 1e-06)
            normed = centred * inverse
            n1[r, :] = normed
            rs1[r, :] = inverse
            y1b[r, :] = (normed * g1 + c1).astype(BF)

        h2[...] = dot(context, w)
        loop(seq // 128, tile)

    def feed_up(j):
        for t in range(2):
            cols = slice(t * half, (t + 1) * half)
            wide_cols = slice(j * model + t * half, j * model + (t + 1) * half)
            u = dot(y1b[...], weight(IN + j, cols)) + prm[8 + j : 9 + j, cols]
            phi = 0.5 * (1.0 + lax.erf(u * SQRT_HALF))
            act[2 * j + t] = (u * phi).astype(BF).T.reshape(CS, 4, rows, seq)
            dact[:, wide_cols] = (phi + u * (jnp.exp(-0.5 * u * u) * INV_SQRT_TAU)).astype(BF)

    def act_rows(m):
        return act[:, :, m].reshape(-1, seq)

    def feed_down(m):
        w = wd[:, :, :, :, m].reshape(-1, model)
        part = dot(act_rows(m), w, TN)
        if m == 0:
            h2[...] = part + (n1[...] * prm[3:4, :] + prm[4:5, :]) + prm[5:6, :]
        else:
            h2[...] += part

    def vsum(row, value):
        vg[row : row + 1, :] += jnp.sum(value, axis=0, keepdims=True)

    def norm_back(dn, n, inverse):
        return (dn - jnp.mean(dn, -1, keepdims=True) - n * jnp.mean(dn * n, -1, keepdims=True)) * inverse

    def norm_two():
        g2, c2 = prm[6:7, :], prm[7:8, :]

        def tile(i):
            r = span(i, 128)
            h = h2[r, :]
            centred = h - jnp.mean(h, -1, keepdims=True)
            inverse = lax.rsqrt(jnp.mean(centred * centred, -1, keepdims=True) + 1e-06)
            n = centred * inverse
            dcx[r, :] = (n * g2 + c2).astype(BF)
            dy = cot[r, :].astype(F32)
            vsum(6, dy * n)
            vsum(7, dy)
            dh = norm_back(dy * g2, n, inverse)
            h2[r, :] = dh
            low = dh.astype(BF)
            dfb[r, :] = low
            vsum(5, low.astype(F32))

        loop(seq // 128, tile)

    def grad_down(m):
        gd[m] = dot(act_rows(m), dfb[...]).astype(BF).reshape(gd.shape[1:])

    def grad_act(j):
        def tile(t):
            i = 2 * j + t
            cols = span(i, 2 * 4 * rows)
            zz = i // YS
            w = wd[zz // ZL, lax.rem(zz, ZL), lax.rem(i, YS)].reshape(2 * 4 * rows, model)
            du = (dot(dfb[...], w, NT) * dact[:, cols].astype(F32)).astype(BF)
            dact[:, cols] = du
            total = jnp.sum(du.astype(F32), axis=0, keepdims=True)
            if t == 0:
                vg[8 + j : 9 + j, 0:half] = total
            else:
                vg[8 + j : 9 + j, half:] = total

        tile(0)
        tile(1)

    def grad_in(j):
        if j == 0:
            y1t[...] = y1b[...].T

        def tile(i):
            cols = span(i, 256)
            wide_cols = pl.ds(pl.multiple_of(j * model + i * 256, 256), 256)
            g = dot(y1t[...], dact[:, wide_cols]).astype(BF)
            wd[:, :, :, :, j, :, cols] = g.reshape(ZH, ZL, YS, CS, rows, 256)

        loop(model // 256, tile)

    def grad_normed(j):
        def tile(i):
            cols = span(i, half)
            w = wa[IN + j, i].reshape(half, model)
            h2[:, cols] += dot(dact[:, j * model : (j + 1) * model], w, NT)

        loop(2, tile)

    def norm_one_back():
        g1 = prm[3:4, :]

        def tile(i):
            r = span(i, 128)
            dy, n = h2[r, :], n1[r, :]
            vsum(3, dy * n)
            vsum(4, dy)
            dh = norm_back(dy * g1, n, rs1[r, :])
            h2[r, :] = dh
            low = dh.astype(BF)
            dfb[r, :] = low
            vsum(2, low.astype(F32))

        loop(seq // 128, tile)

    def grad_out():
        g = dot(ct[...], dfb[...]).astype(BF)
        go[0] = g.reshape(ZH, ZL, YS, CS, rows, model)

    def grad_context():
        vt[...] = x[...].T
        dcx[...] = dot(dfb[...], weight(OUT), NT).astype(BF)

    def attend_back(g):
        def one(j):
            cols = span(j, pair)
            keys = pl.ds(pl.multiple_of(group + j * pair, pair), pair)
            vals = pl.ds(pl.multiple_of(2 * group + j * pair, pair), pair)
            wide_cols = pl.ds(pl.multiple_of(g * group + j * pair, pair), pair)
            lane = lax.broadcasted_iota(jnp.int32, (seq, pair), 1) // head
            dc = dcx[:, wide_cols]
            q, k, v = qkv[g, :, cols], qkv[g, :, keys], qkv[g, :, vals]
            kt = k.T
            dk, dv, dq = [], [], []
            for e in range(2):
                probs = pt[g, 2 * j + e]
                dv.append(dot(probs, dc))
                dp = dot(jnp.where(lane == e, v, jnp.zeros((), BF)), dc, NT)
                p32 = probs.astype(F32)
                t = p32 * dp
                ds = (t - p32 * jnp.sum(t, axis=0, keepdims=True)).astype(BF)
                dk.append(dot(ds, q))
                dq.append((dot(kt[e * head : (e + 1) * head, :], ds) * head**-0.5).astype(BF))
            qkv[g, :, cols] = jnp.concatenate(dq, axis=0).T
            qkv[g, :, keys] = jnp.where(lane == 0, dk[0], dk[1]).astype(BF)
            qkv[g, :, vals] = jnp.where(lane == 0, dv[0], dv[1]).astype(BF)

        loop(group // pair, one)
        grouped = span(g, group)
        vg[0:1, grouped] = jnp.sum(qkv[g, :, 0:group].astype(F32), axis=0, keepdims=True)
        vg[1:2, grouped] = jnp.sum(qkv[g, :, 2 * group :].astype(F32), axis=0, keepdims=True)

    def grad_qkv(g):
        r = dot(vt[...], qkv[g]).astype(BF)
        wa[IN + g] = r.reshape(ZH, ZL, YS, CS, rows, model)

    def grad_x():
        total = h2[...]
        for g in range(3):
            total = total + dot(qkv[g], weight(g), NT)
        n1[...] = total

    left, right = pl.ds(0, half), pl.ds(half, half)

    def gpiece(k, zi, yy, cc, cols=ALL):
        if k < 4:
            return gd.at[(k, *zi, yy, cc, ALL, cols)]
        if k < 8:
            return wd.at[(*zi, yy, cc, k - 4, ALL, cols)]
        if k < 9:
            return go.at[(0, *zi, yy, cc, ALL, cols)]
        return wa.at[(IN + k - 9, *zi, yy, cc, ALL, cols)]

    every = (ALL, ALL)
    mine = (zh, zl)

    def at_z(zz):
        return (zz // ZL, lax.rem(zz, ZL))

    def r_core(k):
        return remote(gpiece(k, every, ALL, 1 - c), rcore.at[k], r_sent.at[k], rrc.at[k], sibling)

    def r_ya(k):
        return remote(gpiece(k, every, 1 - y, c, left), rya.at[k], r_sent.at[k], rry.at[k, 0], across_y)

    def r_xb(k):
        return remote(gpiece(k, (ALL, 1 - px), ALL, c, right), rxb.at[k], r_sent.at[k], rrx.at[k, 0], across_x)

    def r_za(k, dz):
        piece = gpiece(k, at_z(ahead(dz)), y, c, left)
        return remote(piece, rza.at[k, dz - 1], r_sent.at[k], rrz.at[k, 0], device(ahead(dz), y, c, px))

    def r_yb(k):
        return remote(gpiece(k, (ALL, px), 1 - y, c, right), ryb.at[k], r_sent.at[k], rry.at[k, 1], across_y)

    def r_xa(k):
        return remote(gpiece(k, mine, y, c, left), rxa.at[k], r_sent.at[k], rrx.at[k, 1], across_x)

    def r_zb(k, dz):
        piece = gpiece(k, at_z(ahead(dz)), y, c, right)
        return remote(piece, rzb.at[k, dz - 1], r_sent.at[k], rrz.at[k, 1], device(ahead(dz), y, c, px))

    def r_fb(k):
        return remote(gpiece(k, mine, y, c, right), rfb.at[k], r_sent.at[k], rrf.at[k], across_x)

    same = zl == px

    def to_parity(dz, act_on):
        if dz == 2:
            pl.when(same)(act_on)
        else:
            pl.when(jnp.logical_not(same))(act_on)

    def add_into(ref, *others):
        total = ref[...].astype(F32)
        for other in others:
            total = total + other[...].astype(F32)
        ref[...] = total.astype(BF)

    def n_chunk(k):
        return 0 <= k < CHUNKS

    def r0(k):
        if n_chunk(k):
            r_core(k).start()
        if k == CHUNKS - 1:
            remote(gv.at[:, :, :, 1 - c], rv_core, rv_sent, wrc, sibling).start()

    def r1(k):
        if not n_chunk(k):
            return
        r_core(k).wait_recv()

        def add(i):
            piece = gpiece(k, at_z(i), ALL, c)
            add_into(piece, rcore.at[(k, *at_z(i))])

        loop(ZS, add)
        r_ya(k).start()
        r_xb(k).start()
        if k == CHUNKS - 1:
            remote(gv.at[:, :, :, 1 - c], rv_core, rv_sent, wrc, sibling).wait_recv()
            add_into(gv.at[:, :, :, c], rv_core)
            remote(gv.at[:, :, 1 - y, c], rv_y, rv_sent, wry, across_y).start()

    def v_rz(dz):
        return remote(
            gv.at[(*at_z(ahead(dz)), y, c)], rv_z.at[dz - 1], rv_sent, wrz,
            device(ahead(dz), y, c, px),
        )

    def v_rx():
        return remote(gv.at[(*mine, y, c)], rv_x, rv_sent, wrx, across_x)

    def r2(k):
        if not n_chunk(k):
            return
        r_ya(k).wait_recv()
        add_into(gpiece(k, every, y, c, left), rya.at[k])
        for dz in (1, 2, 3):
            r_za(k, dz).start()
        r_xb(k).wait_recv()
        add_into(gpiece(k, (ALL, px), ALL, c, right), rxb.at[k])
        r_yb(k).start()
        if k == CHUNKS - 1:
            remote(gv.at[:, :, 1 - y, c], rv_y, rv_sent, wry, across_y).wait_recv()
            add_into(gv.at[:, :, y, c], rv_y)
            for dz in (1, 2, 3):
                v_rz(dz).start()

    def r3(k):
        if not n_chunk(k):
            return
        r_yb(k).wait_recv()
        add_into(gpiece(k, (ALL, px), y, c, right), ryb.at[k])
        for dz in (1, 2, 3):
            to_parity(dz, lambda dz=dz: r_zb(k, dz).start())
        drained(rza.at[k], rrz.at[k, 0])
        add_into(gpiece(k, mine, y, c, left), rza.at[k, 0], rza.at[k, 1], rza.at[k, 2])
        r_xa(k).start()
        if k == CHUNKS - 1:
            drained(rv_z, wrz)
            add_into(gv.at[(*mine, y, c)], rv_z.at[0], rv_z.at[1], rv_z.at[2])
            v_rx().start()

    def r4(k):
        if not n_chunk(k):
            return

        @pl.when(same)
        def _():
            drained(rzb.at[k], rrz.at[k, 1])
            add_into(gpiece(k, mine, y, c, right), rzb.at[k, 0], rzb.at[k, 1], rzb.at[k, 2])
            r_fb(k).start()
            fin[k, :, right] = gpiece(k, mine, y, c, right)[...].astype(F32)

        r_xa(k).wait_recv()
        fin[k, :, left] = gpiece(k, mine, y, c, left)[...].astype(F32) + rxa[k].astype(F32)
        if k == CHUNKS - 1:
            v_rx().wait_recv()
            fv[...] = gv[(*mine, y, c)].astype(F32) + rv_x[...].astype(F32)

    def store(src, dst, i=0):
        cp = pltpu.make_async_copy(src, dst, s_store.at[i])
        cp.start()
        return cp

    def r5(k):
        if not n_chunk(k):
            return

        @pl.when(jnp.logical_not(same))
        def _():
            r_fb(k).wait_recv()
            fin[k, :, right] = rfb[k].astype(F32)

        if k < 4:
            store(fin.at[k], gdown_hbm.at[pl.ds(k * rows, rows)])
        elif k < 8:
            store(fin.at[k], gin_hbm.at[:, pl.ds((k - 4) * model, model)])
        elif k < 9:
            store(fin.at[k], gout_hbm)
        else:
            for part in range(3):
                store(
                    fin.at[k, :, pl.ds(part * group, group)],
                    gqkv_hbm.at[:, pl.ds(part * model + (k - 9) * group, group)],
                )

    def sums_sent(k):
        drained(wa.at[0], r_sent.at[k])

    vg[...] = jnp.zeros_like(vg)
    def forward(k):
        if k < 0:
            return
        if k < OUT:
            if k == 0:
                spread_params()
            project(k)
            attend(k)
        elif k < IN:
            out_proj()
        elif k < DOWN:
            feed_up(k - IN)
        else:
            feed_down(k - DOWN)

    lead, lag_y, lag_x, lag_c = LAGS
    for i in range(lead):
        e1(i)
    load_x.wait()
    last = PARTS + lag_y + lag_x + lag_c
    for t in range(last):
        e2(t)
        e1(t + lead)
        e3(t - lag_y)
        e4(t - lag_y - lag_x)
        done = t - lag_y - lag_x - lag_c
        e5(done)
        if done % CUTS == CUTS - 1:
            forward(done // CUTS)
    load_cot.wait()
    norm_two()
    store_out = store(dcx, out_hbm.at[0], 1)
    for k in range(4):
        grad_down(k)
        r0(k)
    r1(0)
    grad_act(0)
    grad_act(1)
    r1(1)
    r2(0)
    grad_act(2)
    grad_act(3)
    r1(2)
    r2(1)
    r3(0)
    for k in range(DOWN, CHUNKS):
        sent(k)
    grad_in(0)
    r0(4)
    grad_in(1)
    r0(5)
    r1(3)
    r2(2)
    r3(1)
    r4(0)
    grad_in(2)
    r0(6)
    grad_in(3)
    r0(7)
    r1(4)
    r2(3)
    r3(2)
    r4(1)
    r5(0)
    grad_normed(0)
    grad_normed(1)
    r1(5)
    r2(4)
    r3(3)
    r4(2)
    r5(1)
    grad_normed(2)
    grad_normed(3)
    norm_one_back()
    r1(6)
    r2(5)
    r3(4)
    r4(3)
    r5(2)
    store_out.wait()
    grad_out()
    r0(8)
    grad_context()
    for k in range(IN, DOWN):
        sent(k)
    r1(7)
    r2(6)
    r3(5)
    r4(4)
    r5(3)
    attend_back(0)
    grad_qkv(0)
    r0(9)
    r1(8)
    r2(7)
    r3(6)
    r4(5)
    r5(4)
    attend_back(1)
    grad_qkv(1)
    r0(10)
    r1(9)
    r2(8)
    r3(7)
    r4(6)
    r5(5)
    attend_back(2)
    grad_qkv(2)
    gather_grads()
    r0(11)
    r1(10)
    r2(9)
    r3(8)
    r4(7)
    r5(6)
    r1(11)
    grad_x()
    store_x = store(n1, gtok_hbm.at[0], 2)
    r2(10)
    r3(9)
    r4(8)
    r5(7)
    r2(11)
    r3(10)
    r4(9)
    r5(8)
    r3(11)
    r4(10)
    r5(9)
    r4(11)
    store_vec = store(fv, gvec_hbm, 3)
    r5(10)
    r5(11)
    for k in range(IN):
        sent(k)
    vec_sent()
    for k in range(CHUNKS):
        sums_sent(k)
    drained(gv, rv_sent)
    drained(fin, s_store.at[0])
    store_vec.wait()
    store_x.wait()


def place_kernel(cuts, *refs):
    count = len(cuts)
    sources, targets, held = refs[:count], refs[count : 2 * count], refs[2 * count : 3 * count]
    sem_in, sem_out = refs[3 * count :]
    moves = []
    for src, dst, mid, parts in zip(sources, targets, held, cuts):
        size = src.shape[-2] // parts
        for j in range(parts):
            at = (slice(None),) * (len(src.shape) - 2) + (pl.ds(j * size, size),)
            i = len(moves)
            moves.append(
                (
                    pltpu.make_async_copy(src.at[at], mid.at[at], sem_in.at[i]),
                    pltpu.make_async_copy(mid.at[at], dst.at[at], sem_out.at[i]),
                )
            )
    for first, _ in moves:
        first.start()
    for first, second in moves:
        first.wait()
        second.start()
    for _, second in moves:
        second.wait()


def fused_layer(tokens, lengths, w_qkv, w_out, w_in, w_down, norms_biases, cotangent):
    seq, model = tokens.shape[1:]
    rows = w_qkv.shape[0]
    hidden = w_in.shape[1]
    half = model // 2
    group = model // 3
    segments = jnp.pad(norms_biases.reshape(3, -1), ((0, 13), (0, 256 - norms_biases.shape[0] // 3)))
    vm, dma = pltpu.VMEM, pltpu.SemaphoreType.DMA
    grid = (ZH, ZL, YS, CS)
    n, m = CHUNKS, PARTS
    scratch = [
        vm((DOWN, *grid, rows, model), BF),
        vm((*grid, 4, rows, model), BF),
        vm((*grid, 16, 256), BF),
        vm((4, *grid, rows, model), BF),
        vm((1, *grid, rows, model), BF),
        vm((*grid, 16, 256), BF),
        vm((n, ZH, ZL, YS, rows, model), BF),
        vm((n, ZH, ZL, rows, half), BF),
        vm((n, ZH, YS, rows, half), BF),
        vm((n, 3, rows, half), BF),
        vm((n, ZH, rows, half), BF),
        vm((n, 3, rows, half), BF),
        vm((n, rows, half), BF),
        vm((n, rows, half), BF),
        vm((ZH, ZL, YS, 16, 256), BF),
        vm((ZH, ZL, 16, 256), BF),
        vm((3, 16, 256), BF),
        vm((16, 256), BF),
        vm((n, rows, model), F32),
        vm((16, 256), F32),
        vm((seq, model), BF),
        vm((seq, model), BF),
        vm((3, seq, model), BF),
        vm((model, seq), BF),
        vm((3, group // (model // HEADS), seq, seq), BF),
        vm((model, seq), BF),
        vm((seq, model), F32),
        vm((seq, model), BF),
        vm((model, seq), BF),
        vm((ZS * YS, CS, 4, rows, seq), BF),
        vm((seq, hidden), BF),
        vm((seq, model), F32),
        vm((seq, model), BF),
        vm((seq, model), BF),
        vm((seq, 1), F32),
        vm((16, model), F32),
        vm((16, model), F32),
        dma((n,)), dma, dma((2,)), dma((4,)),
        dma((m,)), dma((m,)), dma((m,)), dma((m,)), dma((m,)), dma, dma, dma, dma,
        dma((n,)), dma, dma((n,)), dma((n, 2)), dma((n, 2)), dma((n, 2)), dma((n,)), dma, dma, dma, dma,
    ]
    hbm = pl.BlockSpec(memory_space=pl.ANY)
    shape = jax.ShapeDtypeStruct
    outs = pl.pallas_call(
        layer_kernel,
        out_shape=(
            shape(tokens.shape, BF),
            shape(tokens.shape, F32),
            shape(w_qkv.shape, F32),
            shape(w_out.shape, F32),
            shape(w_in.shape, F32),
            shape(w_down.shape, F32),
            shape((16, 256), F32),
        ),
        in_specs=[hbm, pl.BlockSpec(memory_space=pltpu.SMEM)] + [hbm] * 6,
        out_specs=(hbm,) * 7,
        scratch_shapes=scratch,
        compiler_params=pltpu.CompilerParams(
            collective_id=0, has_side_effects=True, vmem_limit_bytes=64 << 20
        ),
        name="layer",
    )(tokens, lengths, w_qkv, w_out, w_in, w_down, segments, cotangent)
    grad_vector = outs[6][:3, : norms_biases.shape[0] // 3].reshape(-1)
    cuts = (2, 4, 1, 1, 1, 1)
    placed = pl.pallas_call(
        functools.partial(place_kernel, cuts),
        out_shape=tuple(shape(o.shape, o.dtype) for o in outs[:6]),
        in_specs=[hbm] * 6,
        out_specs=(hbm,) * 6,
        scratch_shapes=[vm(o.shape, o.dtype) for o in outs[:6]] + [dma((sum(cuts),)), dma((sum(cuts),))],
        name="place",
    )(*outs[:6])
    return (*placed, grad_vector)


def norm_rows(values, gain_row, shift_row):
    average = jnp.mean(values, -1, keepdims=True)
    centred = values - average
    spread = jnp.mean(centred * centred, -1, keepdims=True)
    return centred * lax.rsqrt(spread + 1e-06) * gain_row + shift_row


def gelu_exact(values):
    return jax.nn.gelu(values, approximate=False)


def column_sum(values):
    return jnp.sum(values.astype(jnp.float32), 0)


def split_vector(vector, model_width, hidden_width):
    segments = [
        vector[position * model_width : (position + 1) * model_width] for position in range(8)
    ]
    return segments + [vector[8 * model_width : 8 * model_width + hidden_width]]


def pair_blocks(projected, head_count):
    row_count = projected.shape[0]
    pair_count = head_count // 2
    pair_width = projected.shape[1] // (3 * pair_count)
    return projected.reshape(row_count, 3, pair_count, pair_width).transpose(2, 1, 0, 3)


def unpair_blocks(blocks):
    pair_count = blocks.shape[0]
    row_count = blocks.shape[2]
    pair_width = blocks.shape[3]
    return blocks.transpose(2, 1, 0, 3).reshape(row_count, 3 * pair_count * pair_width)


def pair_scores(head_block, usable, factor):
    row_count = head_block.shape[1]
    queries = head_block[0].reshape(row_count, 2, -1)
    key_rows = head_block[1].reshape(row_count, 2, -1)
    values = head_block[2].reshape(row_count, 2, -1)
    scores = (
        jnp.einsum("qhd,khd->hqk", queries, key_rows, preferred_element_type=jnp.float32) * factor
    )
    return (queries, key_rows, values, jnp.where(usable[None, None, :], scores, -1000000000.0))


def attention_forward(blocks, usable, factor):

    def one_pair(head_block):
        queries, key_rows, values, scores = pair_scores(head_block, usable, factor)
        highest = jnp.max(scores, -1, keepdims=True)
        raised = jnp.exp(scores - highest)
        summed = jnp.sum(raised, -1, keepdims=True)
        attend = (raised / summed).astype(jnp.bfloat16)
        context = jnp.einsum("hqk,khd->qhd", attend, values, preferred_element_type=jnp.float32)
        return (context.reshape(context.shape[0], -1), highest[..., 0] + jnp.log(summed[..., 0]))

    return lax.map(one_pair, blocks)


def attention_backward(blocks, grad_pairs, log_totals, usable, factor):

    def one_pair(pair_inputs):
        head_block, grad_context, log_total = pair_inputs
        queries, key_rows, values, scores = pair_scores(head_block, usable, factor)
        attend = jnp.exp(scores - log_total[..., None])
        row_count = grad_context.shape[0]
        grad_heads = grad_context.reshape(row_count, 2, -1)
        grad_values = jnp.einsum(
            "hqk,qhd->khd",
            attend.astype(jnp.bfloat16),
            grad_heads,
            preferred_element_type=jnp.float32,
        )
        grad_attend = jnp.einsum(
            "qhd,khd->hqk", grad_heads, values, preferred_element_type=jnp.float32
        )
        grad_scores = attend * (grad_attend - jnp.sum(attend * grad_attend, -1, keepdims=True))
        grad_low = grad_scores.astype(jnp.bfloat16)
        grad_queries = (
            jnp.einsum("hqk,khd->qhd", grad_low, key_rows, preferred_element_type=jnp.float32)
            * factor
        )
        grad_keys = (
            jnp.einsum("hqk,qhd->khd", grad_low, queries, preferred_element_type=jnp.float32)
            * factor
        )
        return jnp.stack(
            [
                grad_queries.reshape(row_count, -1),
                grad_keys.reshape(row_count, -1),
                grad_values.reshape(row_count, -1),
            ]
        )

    return lax.map(one_pair, (blocks, grad_pairs, log_totals))


def layer_forward(inputs, length, weights):
    w_qkv, w_out, w_in, w_down, vector = weights
    row_count, model_width = inputs.shape
    hidden_width = w_in.shape[1]
    params = split_vector(vector.astype(jnp.float32), model_width, hidden_width)
    joined_bias = jnp.concatenate([params[0], jnp.zeros((model_width,), jnp.float32), params[1]])
    projected = (jnp.dot(inputs, w_qkv, preferred_element_type=jnp.float32) + joined_bias).astype(
        jnp.bfloat16
    )
    blocks = pair_blocks(projected, HEADS)
    usable = jnp.arange(row_count) < length
    factor = (model_width // HEADS) ** (-0.5)
    context_pairs, log_totals = attention_forward(blocks, usable, factor)
    context = context_pairs.transpose(1, 0, 2).reshape(row_count, model_width).astype(jnp.bfloat16)
    resid_one = inputs.astype(jnp.float32) + (
        jnp.dot(context, w_out, preferred_element_type=jnp.float32) + params[2]
    )
    normed_one = norm_rows(resid_one, params[3], params[4])
    normed_low = normed_one.astype(jnp.bfloat16)
    pre_act = jnp.dot(normed_low, w_in, preferred_element_type=jnp.float32) + params[8]
    activated = gelu_exact(pre_act).astype(jnp.bfloat16)
    resid_two = normed_one + (
        jnp.dot(activated, w_down, preferred_element_type=jnp.float32) + params[5]
    )
    result = norm_rows(resid_two, params[6], params[7])
    saved = (
        params,
        blocks,
        usable,
        factor,
        log_totals,
        context,
        resid_one,
        normed_low,
        pre_act,
        activated,
        resid_two,
    )
    return (result, saved)


def layer_backward(inputs, length, grad_result, weights):
    w_qkv, w_out, w_in, w_down, vector = weights
    unused_result, saved = layer_forward(inputs, length, weights)
    (
        params,
        blocks,
        usable,
        factor,
        log_totals,
        context,
        resid_one,
        normed_low,
        pre_act,
        activated,
        resid_two,
    ) = saved
    row_count, model_width = inputs.shape
    unused_two, norm_two_back = jax.vjp(norm_rows, resid_two, params[6], params[7])
    grad_two, grad_gain_two, grad_shift_two = norm_two_back(grad_result)
    grad_feed = grad_two.astype(jnp.bfloat16)
    grad_down = jnp.einsum("sf,sd->fd", activated, grad_feed, preferred_element_type=jnp.float32)
    grad_act = jnp.einsum("sd,fd->sf", grad_feed, w_down, preferred_element_type=jnp.float32)
    unused_act, gelu_back = jax.vjp(gelu_exact, pre_act)
    grad_pre = gelu_back(grad_act)[0].astype(jnp.bfloat16)
    grad_in = jnp.einsum("sd,sf->df", normed_low, grad_pre, preferred_element_type=jnp.float32)
    grad_normed = grad_two + jnp.einsum(
        "sf,df->sd", grad_pre, w_in, preferred_element_type=jnp.float32
    )
    unused_one, norm_one_back = jax.vjp(norm_rows, resid_one, params[3], params[4])
    grad_one, grad_gain_one, grad_shift_one = norm_one_back(grad_normed)
    grad_attended = grad_one.astype(jnp.bfloat16)
    grad_out = jnp.einsum("sd,se->de", context, grad_attended, preferred_element_type=jnp.float32)
    grad_context = jnp.einsum(
        "se,de->sd", grad_attended, w_out, preferred_element_type=jnp.float32
    ).astype(jnp.bfloat16)
    grad_pairs = grad_context.reshape(row_count, HEADS // 2, -1).transpose(1, 0, 2)
    grad_blocks = attention_backward(blocks, grad_pairs, log_totals, usable, factor)
    grad_projected = unpair_blocks(grad_blocks).astype(jnp.bfloat16)
    grad_qkv = jnp.einsum("sd,se->de", inputs, grad_projected, preferred_element_type=jnp.float32)
    grad_inputs = grad_one + jnp.einsum(
        "se,de->sd", grad_projected, w_qkv, preferred_element_type=jnp.float32
    )
    projected_sums = column_sum(grad_projected)
    grad_vector = jnp.concatenate(
        [
            projected_sums[:model_width],
            projected_sums[2 * model_width :],
            column_sum(grad_attended),
            grad_gain_one,
            grad_shift_one,
            column_sum(grad_feed),
            grad_gain_two,
            grad_shift_two,
            column_sum(grad_pre),
        ]
    )
    return (grad_inputs, (grad_qkv, grad_out, grad_in, grad_down, grad_vector))


def local(tokens, lengths, w_qkv, w_out, w_in, w_down, norms_biases, cotangent):
    weights = (
        lax.all_gather(w_qkv, "wide", axis=0, tiled=True),
        lax.all_gather(w_out, "wide", axis=0, tiled=True),
        lax.all_gather(w_in, "wide", axis=0, tiled=True),
        lax.all_gather(w_down, "wide", axis=0, tiled=True),
        lax.all_gather(norms_biases, "wide", axis=0, tiled=True),
    )

    def forward_one(sequence):
        return layer_forward(sequence[0], sequence[1], weights)[0].astype(jnp.bfloat16)

    output = lax.map(forward_one, (tokens, lengths))
    second_copy = (
        lax.all_gather(w_qkv, "wide", axis=0, tiled=True),
        lax.all_gather(w_out, "wide", axis=0, tiled=True),
        lax.all_gather(w_in, "wide", axis=0, tiled=True),
        lax.all_gather(w_down, "wide", axis=0, tiled=True),
        lax.all_gather(norms_biases, "wide", axis=0, tiled=True),
    )
    running = tuple((jnp.zeros(member.shape, jnp.float32) for member in second_copy))

    def advance(totals, sequence):
        grad_inputs, gradients = layer_backward(
            sequence[0], sequence[1], sequence[2].astype(jnp.float32), second_copy
        )
        return (jax.tree.map(jnp.add, totals, gradients), grad_inputs)

    totals, grad_tokens = lax.scan(advance, running, (tokens, lengths, cotangent))
    owned_rows = (
        lax.psum_scatter(
            totals[0].astype(jnp.bfloat16), "wide", scatter_dimension=0, tiled=True
        ).astype(jnp.float32),
        lax.psum_scatter(
            totals[1].astype(jnp.bfloat16), "wide", scatter_dimension=0, tiled=True
        ).astype(jnp.float32),
        lax.psum_scatter(
            totals[2].astype(jnp.bfloat16), "wide", scatter_dimension=0, tiled=True
        ).astype(jnp.float32),
        lax.psum_scatter(
            totals[3].astype(jnp.bfloat16), "wide", scatter_dimension=0, tiled=True
        ).astype(jnp.float32),
        lax.psum_scatter(
            totals[4].astype(jnp.bfloat16), "wide", scatter_dimension=0, tiled=True
        ).astype(jnp.float32),
    )
    summed_all = (
        lax.psum(owned_rows[0].astype(jnp.bfloat16), "narrow").astype(jnp.float32),
        lax.psum(owned_rows[1].astype(jnp.bfloat16), "narrow").astype(jnp.float32),
        lax.psum(owned_rows[2].astype(jnp.bfloat16), "narrow").astype(jnp.float32),
        lax.psum(owned_rows[3].astype(jnp.bfloat16), "narrow").astype(jnp.float32),
        lax.psum(owned_rows[4].astype(jnp.bfloat16), "narrow").astype(jnp.float32),
    )
    return (
        output,
        grad_tokens,
        summed_all[0],
        summed_all[1],
        summed_all[2],
        summed_all[3],
        summed_all[4],
    )


def solution(mesh):
    in_specs = (
        P(("wide", "narrow"), None, None),
        P(("wide", "narrow")),
        P("wide", None),
        P("wide", None),
        P("wide", None),
        P("wide", None),
        P("wide"),
        P(("wide", "narrow"), None, None),
    )
    out_specs = (
        P(("wide", "narrow"), None, None),
        P(("wide", "narrow"), None, None),
        P("wide", None),
        P("wide", None),
        P("wide", None),
        P("wide", None),
        P("wide"),
    )
    chips = (ZS * YS * CS, 2)
    fused = tuple(mesh.shape[axis] for axis in ("wide", "narrow")) == chips
    step = fused_layer if fused else local
    return jax.shard_map(step, mesh=mesh, in_specs=in_specs, out_specs=out_specs, check_vma=False)
```

```python
import functools

import jax
import jax.numpy as jnp
import numpy as np
from jax import lax
from jax.experimental import pallas as pl
from jax.experimental.pallas import tpu as pltpu
from jax.sharding import PartitionSpec as P

HEADS = 12
MESH = pl.DeviceIdType.MESH
BF = jnp.bfloat16
F32 = jnp.float32
NT = (((1,), (1,)), ((), ()))
TN = (((0,), (0,)), ((), ()))
ZH, ZL, YS, CS = 2, 2, 2, 2
ZS = ZH * ZL
QKV, OUT, IN, DOWN, CHUNKS = 0, 3, 4, 8, 12
RING = 8
(
    S_E1, S_EO, S_E2, S_E3, S_E4, S_E5, S_R0, S_R1, S_R2A, S_R2B, S_R3A,
    S_R3B, S_R4A, S_R4B, S_R5, S_SPREAD, S_PROJECT, S_ATTEND, S_OUT, S_UP, S_DOWN, S_NORM2,
    S_GDOWN, S_GACT, S_GIN, S_GNORM, S_NORM1, S_GOUT, S_GCTX, S_ABACK, S_GQKV, S_GGRADS, S_GX,
) = range(33)
GATHERED = (
    (0, 0, 384), (0, 384, 384), (1, 0, 384), (1, 384, 384), (2, 0, 384), (2, 384, 384), (3, 0, 384), (3, 384, 384),
    (4, 0, 384), (4, 384, 384), (5, 0, 384), (5, 384, 384), (6, 0, 384), (6, 384, 384), (7, 0, 384), (7, 384, 384),
    (8, 0, 384), (8, 384, 384), (9, 0, 384), (9, 384, 384), (10, 0, 384), (10, 384, 384), (11, 0, 384), (11, 384, 384),
)
SUMMED = (
    (0, 0, 384), (1, 0, 384), (2, 0, 384), (3, 0, 384), (4, 0, 384), (5, 0, 384), (6, 0, 384), (7, 0, 384),
    (8, 0, 384), (9, 0, 384), (10, 0, 384), (11, 0, 384),
)
ORDER = (
    (S_E1, 0), (S_E1, 1), (S_E1, 2), (S_EO, 0), (S_EO, 1), (S_EO, 2), (S_EO, 3), (S_EO, 4), (S_EO, 5), (S_E2, 0),
    (S_E1, 3), (S_EO, 6), (S_E2, 1), (S_E1, 4), (S_EO, 7), (S_E3, 0), (S_E2, 2), (S_E1, 5), (S_EO, 8), (S_E3, 1),
    (S_E2, 3), (S_E1, 6), (S_E4, 0), (S_EO, 9), (S_E3, 2), (S_E5, 0), (S_E2, 4), (S_E1, 7), (S_E4, 1), (S_EO, 10),
    (S_E3, 3), (S_E5, 1), (S_SPREAD, 0), (S_E2, 5), (S_E1, 8), (S_E4, 2), (S_EO, 11), (S_PROJECT, 0), (S_E3, 4), (S_E5, 2),
    (S_E2, 6), (S_E1, 9), (S_E4, 3), (S_EO, 12), (S_ATTEND, 0), (S_E2, 7), (S_E1, 10), (S_E3, 5), (S_E4, 4), (S_E5, 3),
    (S_EO, 13), (S_ATTEND, 1), (S_E2, 8), (S_E1, 11), (S_E3, 6), (S_E5, 4), (S_EO, 14), (S_PROJECT, 1), (S_E3, 7), (S_E4, 5),
    (S_E2, 9), (S_E1, 12), (S_EO, 15), (S_E5, 5), (S_ATTEND, 2), (S_E2, 10), (S_E1, 13), (S_E3, 8), (S_E4, 6), (S_E4, 7),
    (S_EO, 16), (S_ATTEND, 3), (S_E2, 11), (S_E1, 14), (S_E3, 9), (S_E5, 6), (S_E5, 7), (S_EO, 17), (S_PROJECT, 2), (S_E3, 10),
    (S_E2, 12), (S_E1, 15), (S_E4, 8), (S_EO, 18), (S_ATTEND, 4), (S_E2, 13), (S_E1, 16), (S_E3, 11), (S_E4, 9), (S_E4, 10),
    (S_E5, 8), (S_EO, 19), (S_ATTEND, 5), (S_E2, 14), (S_E1, 17), (S_E3, 12), (S_E5, 9), (S_E5, 10), (S_EO, 20), (S_OUT, 0),
    (S_E2, 15), (S_E1, 18), (S_E3, 13), (S_E4, 11), (S_EO, 21), (S_E3, 14), (S_E2, 16), (S_E1, 19), (S_E4, 12), (S_E5, 11),
    (S_EO, 22), (S_UP, 0), (S_E5, 12), (S_E2, 17), (S_E1, 20), (S_E3, 15), (S_E4, 13), (S_EO, 23), (S_UP, 1), (S_E2, 18),
    (S_E1, 21), (S_E3, 16), (S_E4, 14), (S_E5, 13), (S_UP, 2), (S_E4, 15), (S_E2, 19), (S_E1, 22), (S_E3, 17), (S_E5, 14),
    (S_E5, 15), (S_UP, 3), (S_E2, 20), (S_E1, 23), (S_E3, 18), (S_E4, 16), (S_E4, 17), (S_E2, 21), (S_E3, 19), (S_E5, 16),
    (S_E5, 17), (S_DOWN, 0), (S_E2, 22), (S_E3, 20), (S_E4, 18), (S_E3, 21), (S_E4, 19), (S_E2, 23), (S_E5, 18), (S_E5, 19),
    (S_DOWN, 1), (S_E3, 22), (S_E4, 20), (S_E4, 21), (S_E5, 20), (S_E3, 23), (S_E5, 21), (S_DOWN, 2), (S_E4, 22), (S_E5, 22),
    (S_E4, 23), (S_E5, 23), (S_DOWN, 3), (S_NORM2, 0), (S_GDOWN, 0), (S_R0, 0), (S_GACT, 0), (S_GACT, 1), (S_R1, 0), (S_GACT, 2),
    (S_GACT, 3), (S_GDOWN, 1), (S_R0, 1), (S_GDOWN, 2), (S_R0, 2), (S_GDOWN, 3), (S_R0, 3), (S_R1, 1), (S_GIN, 0), (S_R0, 4),
    (S_R2A, 0), (S_R2B, 0), (S_R1, 2), (S_GIN, 1), (S_R0, 5), (S_GIN, 2), (S_R0, 6), (S_GIN, 3), (S_R0, 7), (S_R2A, 1),
    (S_R2B, 1), (S_R1, 3), (S_GNORM, 0), (S_R3A, 0), (S_R3B, 0), (S_GNORM, 1), (S_R2B, 2), (S_GNORM, 2), (S_R2A, 2), (S_R1, 4),
    (S_GNORM, 3), (S_R2B, 3), (S_R3A, 1), (S_R3B, 1), (S_R4A, 0), (S_NORM1, 0), (S_R4B, 0), (S_GOUT, 0), (S_R0, 8), (S_R2A, 3),
    (S_R1, 5), (S_R2B, 4), (S_R3A, 2), (S_R3B, 2), (S_R4A, 1), (S_GCTX, 0), (S_R5, 0), (S_R4B, 1), (S_ABACK, 0), (S_R2A, 4),
    (S_R1, 6), (S_R2B, 5), (S_R3A, 3), (S_R3B, 3), (S_R4A, 2), (S_ABACK, 1), (S_R4B, 2), (S_R5, 1), (S_GQKV, 0), (S_R0, 9),
    (S_R2A, 5), (S_R1, 7), (S_R2B, 6), (S_R3A, 4), (S_R3B, 4), (S_R4A, 3), (S_ABACK, 2), (S_R4B, 3), (S_R5, 2), (S_ABACK, 3),
    (S_R2A, 6), (S_R1, 8), (S_R2B, 7), (S_R3A, 5), (S_R3B, 5), (S_R4A, 4), (S_GQKV, 1), (S_R0, 10), (S_R5, 3), (S_ABACK, 4),
    (S_R4B, 4), (S_R2A, 7), (S_R1, 9), (S_ABACK, 5), (S_R2B, 8), (S_R3A, 6), (S_R3B, 6), (S_R4A, 5), (S_R5, 4), (S_GQKV, 2),
    (S_R4B, 5), (S_GGRADS, 0), (S_R0, 11), (S_R2A, 8), (S_R1, 10), (S_GX, 0), (S_R2B, 9), (S_R3A, 7), (S_R3B, 7), (S_R4A, 6),
    (S_GX, 1), (S_R5, 5), (S_R4B, 6), (S_GX, 2), (S_R2A, 9), (S_R1, 11), (S_R2B, 10), (S_R3A, 8), (S_R3B, 8), (S_R4A, 7),
    (S_R5, 6), (S_R4B, 7), (S_R2A, 10), (S_R2B, 11), (S_R3A, 9), (S_R3B, 9), (S_R4A, 8), (S_R5, 7), (S_R4B, 8), (S_R4A, 9),
    (S_R2A, 11), (S_R3A, 10), (S_R3B, 10), (S_R5, 8), (S_R3B, 11), (S_R4B, 9), (S_R4A, 10), (S_R3A, 11), (S_R5, 9), (S_R4B, 10),
    (S_R4A, 11), (S_R4B, 11), (S_R5, 10), (S_R5, 11),
)
SQRT_HALF = 0.7071067811865476
INV_SQRT_TAU = 0.3989422804014327


def dot(left, right, dims=None):
    if dims is None:
        return jnp.dot(left, right, preferred_element_type=F32)
    return lax.dot_general(left, right, dims, preferred_element_type=F32)


def loop(count, body):
    def step(index, carry):
        body(index)
        return carry

    lax.fori_loop(0, count, step, 0)


def span(index, size):
    return pl.ds(pl.multiple_of(index * size, size), size)


def layer_kernel(
    x_hbm, len_ref, wqkv_hbm, wout_hbm, win_hbm, wdown_hbm, vec_hbm, cot_hbm,
    out_hbm, gtok_hbm, gqkv_hbm, gout_hbm, gin_hbm, gdown_hbm, gvec_hbm,
    wa, wd, vb, gd, go, gv, rcore, rya, rxb, rza, ryb, rzb, rxa, rfb, rv_core, rv_y, rv_z, rv_x, fin, vec,
    x, cot, qkv, vt, pt, ct, n1, y1b, y1t, act, dact, h2, dfb, dcx, rs1, prm, vg,
    s_load, s_io, s_store,
    g_sent, grz, gry, grx, grc, v_sent, vrz, vry, vrc,
    r_sent, rv_sent, rrc, rry, rrx, rrz, rrf, wrc, wry, wrz, wrx,
):
    seq, model = x.shape
    rows = wa.shape[-2]
    hidden = dact.shape[1]
    pair = 2 * (model // HEADS)
    head = model // HEADS
    group = model // 3
    half = model // 2
    wide = lax.axis_index("wide")
    px = lax.axis_index("narrow")
    c = lax.rem(wide, CS)
    y = lax.rem(wide // CS, YS)
    z = wide // (CS * YS)
    zl = lax.rem(z, ZL)
    zh = z // ZL

    def device(zz, yy, cc, xx):
        return ((zz * YS + yy) * CS + cc, xx)

    sibling = device(z, y, 1 - c, px)
    across_y = device(z, 1 - y, c, px)
    across_x = device(z, y, c, 1 - px)

    def ahead(dz):
        return lax.rem(z + dz, ZS)

    def behind(dz):
        return lax.rem(z + ZS - dz, ZS)

    def remote(src, dst, send, recv, where):
        return pltpu.make_async_remote_copy(
            src_ref=src, dst_ref=dst, send_sem=send, recv_sem=recv, device_id=where, device_id_type=MESH
        )

    ALL = slice(None)

    def drained(ref, sem):
        pltpu.make_async_copy(ref, ref, sem).wait()

    def rows_of(count, cols):
        return x.at[pl.ds(0, count), pl.ds(0, cols)]

    def load(src, dst, sem):
        cp = pltpu.make_async_copy(src, dst, sem)
        cp.start()
        return cp

    load_vec = load(vec_hbm, vec, s_io.at[2])
    load_x = load(x_hbm.at[0], x, s_io.at[0])
    for k in range(CHUNKS):
        if k < OUT:
            for part in range(3):
                load(
                    wqkv_hbm.at[:, pl.ds(part * model + k * group, group)],
                    wa.at[k, zh, zl, y, c, :, pl.ds(part * group, group)],
                    s_load.at[k],
                )
        elif k < IN:
            load(wout_hbm, wa.at[k, zh, zl, y, c], s_load.at[k])
        elif k < DOWN:
            load(win_hbm.at[:, pl.ds((k - IN) * model, model)], wa.at[k, zh, zl, y, c], s_load.at[k])
        else:
            load(wdown_hbm.at[pl.ds((k - DOWN) * rows, rows)], wd.at[zh, zl, y, c, k - DOWN], s_load.at[k])
    load_cot = load(cot_hbm.at[0], cot, s_io.at[1])

    barrier = pltpu.get_barrier_semaphore()
    for where in (sibling, across_y, across_x, *(device(ahead(dz), y, c, px) for dz in (1, 2, 3))):
        pl.semaphore_signal(barrier, inc=1, device_id=where, device_id_type=MESH)
    pl.semaphore_wait(barrier, 6)

    third = rows // 3
    kept = pl.ds(pl.multiple_of(px * third, third), 2 * third)
    given = pl.ds(pl.multiple_of(px * 2 * third, third), third)
    taken = pl.ds(pl.multiple_of((1 - px) * 2 * third, third), third)

    def wcut(i, zz, yy, cc, r=ALL):
        k, first, count = GATHERED[i]
        cols = pl.ds(first, count)
        zi = (ALL, ALL) if zz is None else (zz // ZL, lax.rem(zz, ZL))
        if k < DOWN:
            return wa.at[(k, *zi, yy, cc, r, cols)]
        return wd.at[(*zi, yy, cc, k - DOWN, r, cols)]

    def g_z(i, dz, source):
        piece = wcut(i, source, y, c, kept)
        return remote(piece, piece, g_sent.at[i], grz.at[i], device(ahead(dz), y, c, px))

    def g_y(i, dz, column):
        piece = wcut(i, behind(dz), column, c, kept)
        return remote(piece, piece, g_sent.at[i], gry.at[i], across_y)

    def g_x1(i, dz, r):
        piece = wcut(i, behind(dz), y, c, r)
        return remote(piece, piece, g_sent.at[i], grx.at[i], across_x)

    def g_x2(i, r):
        piece = wcut(i, None, 1 - y, c, r)
        return remote(piece, piece, g_sent.at[i], grx.at[i], across_x)

    def g_core(i, core):
        piece = wcut(i, None, ALL, core)
        return remote(piece, piece, g_sent.at[i], grc.at[i], sibling)

    def v_z(dz, source):
        piece = vb.at[source // ZL, lax.rem(source, ZL), y, c]
        return remote(piece, piece, v_sent, vrz, device(ahead(dz), y, c, px))

    def v_y(column):
        piece = vb.at[:, :, column, c]
        return remote(piece, piece, v_sent, vry, across_y)

    def v_core(core):
        piece = vb.at[:, :, :, core]
        return remote(piece, piece, v_sent, vrc, sibling)

    loaded = set()

    def own(k):
        if k not in loaded:
            loaded.add(k)
            drained(rows_of(rows, model), s_load.at[k])

    def e1(i):
        own(GATHERED[i][0])
        for dz in (1, 2, 3):
            g_z(i, dz, z).start()
        if i == 1:
            load_vec.wait()
            segment = vec.shape[0] // 3
            row = vec[...].astype(F32).reshape(1, -1)
            vb[zh, zl, y, c] = jnp.zeros(vb.shape[-2:], BF)
            for s in range(3):
                vb[zh, zl, y, c, s : s + 1, 0:segment] = row[:, s * segment : (s + 1) * segment].astype(BF)
            for dz in (1, 2, 3):
                v_z(dz, z).start()

    def eo(i):
        own(GATHERED[i][0])
        g_y(i, 0, y).start()

    def e2(i):
        if i == 1:
            drained(rv_z, vrz)
            v_y(y).start()
        drained(rows_of(3 * 2 * third, GATHERED[i][2]), grz.at[i])
        for dz in (1, 2, 3):
            g_y(i, dz, y).start()
            g_x1(i, dz, given).start()

    def e3(i):
        if i == 1:
            v_y(1 - y).wait_recv()
            v_core(c).start()
        drained(rows_of(ZS * 2 * third, GATHERED[i][2]), gry.at[i])
        g_x2(i, given).start()

    def e4(i):
        drained(rows_of((ZS + ZS - 1) * third, GATHERED[i][2]), grx.at[i])
        g_core(i, c).start()

    def e5(i):
        if i == 1:
            v_core(1 - c).wait_recv()
        g_core(i, 1 - c).wait_recv()

    def sent(*chunks):
        count = (3 + ZS) * 2 * third + (2 * ZS - 1) * third + ZS * YS * rows
        for i, (k, _, cols) in enumerate(GATHERED):
            if k in chunks:
                drained(qkv.at[:, pl.ds(0, count // 3), pl.ds(0, cols)], g_sent.at[i])

    def vec_sent():
        drained(x.at[pl.ds(0, 80)], v_sent)

    def place_matrix(k, lanes):
        i = lax.broadcasted_iota(jnp.int32, (lanes, model), 0)
        j = lax.broadcasted_iota(jnp.int32, (lanes, model), 1)
        quarter = model // 4
        return jnp.where((i < quarter) & (j == i + k * quarter), 1.0, 0.0).astype(BF)

    def pick_matrix(k, count, total, slot):
        b = lax.broadcasted_iota(jnp.int32, (count, total), 0)
        r = lax.broadcasted_iota(jnp.int32, (count, total), 1)
        segment = 4 * b + k
        return jnp.where((r == slot * (segment // 3) + lax.rem(segment, 3)) & (b < 12), 1.0, 0.0).astype(BF)

    def spread_params(_):
        lanes = vb.shape[-1]
        segments = vb[...].reshape(-1, lanes)
        total = None
        for k in range(4):
            picked = dot(pick_matrix(k, 16, segments.shape[0], vb.shape[-2]), segments).astype(BF)
            part = dot(picked, place_matrix(k, lanes))
            total = part if total is None else total + part
        prm[...] = total

    def gather_grads(_):
        lanes = gv.shape[-1]
        low = vg[...].astype(BF)
        total = None
        for k in range(4):
            cut = dot(low, place_matrix(k, lanes), NT).astype(BF)
            part = dot(pick_matrix(k, 16, 16 * gv.shape[-2], gv.shape[-2]), cut, TN)
            total = part if total is None else total + part
        gv[...] = total.astype(BF).reshape(gv.shape)

    def weight(k, cols=ALL):
        block = wa[k, :, :, :, :, :, cols]
        return block.reshape(-1, block.shape[-1])

    def project(g):
        grouped = span(g, group)
        joined = dot(x[...], weight(g))
        q = (joined[:, :group] + prm[0:1, grouped]).astype(BF)
        qkv[g, :, 0:group] = q * jnp.asarray(head**-0.5, BF)
        qkv[g, :, group : 2 * group] = joined[:, group : 2 * group].astype(BF)
        v = (joined[:, 2 * group :] + prm[1:2, grouped]).astype(BF)
        qkv[g, :, 2 * group :] = v
        vt[grouped, :] = v.T

    def attend(half_group):
        g, first = half_group // 2, half_group % 2 * 2
        length = len_ref[0]

        def one(i):
            h = first + i
            cols = span(first // 2, pair)
            keys = pl.ds(group + (first // 2) * pair, pair)
            lane = lax.broadcasted_iota(jnp.int32, (seq, pair), 1) // head
            masked = jnp.where(lane == lax.rem(h, 2), qkv[g, :, keys], jnp.zeros((), BF))
            scores = dot(masked, qkv[g, :, cols], NT)
            key = lax.broadcasted_iota(jnp.int32, scores.shape, 0)
            scores = jnp.where(key < length, scores, -1000000000.0)
            raised = jnp.exp(scores - jnp.max(scores, axis=0, keepdims=True))
            probs = (raised * (1.0 / jnp.sum(raised, axis=0, keepdims=True))).astype(BF)
            pt[g, h] = probs
            mine = pl.ds(pl.multiple_of(g * group + h * head, head), head)
            ct[mine, :] = dot(vt[mine, :], probs).astype(BF)

        loop(2, one)

    def out_proj(_):
        context = ct[...].T
        bo, g1, c1 = prm[2:3, :], prm[3:4, :], prm[4:5, :]
        w = weight(OUT)

        def tile(i):
            r = span(i, 128)
            h1 = x[r, :].astype(F32) + (h2[r, :] + bo)
            centred = h1 - jnp.mean(h1, -1, keepdims=True)
            inverse = lax.rsqrt(jnp.mean(centred * centred, -1, keepdims=True) + 1e-06)
            normed = centred * inverse
            n1[r, :] = normed
            rs1[r, :] = inverse
            y1b[r, :] = (normed * g1 + c1).astype(BF)

        h2[...] = dot(context, w)
        loop(seq // 128, tile)

    def feed_up(j):
        for t in range(2):
            cols = slice(t * half, (t + 1) * half)
            wide_cols = slice(j * model + t * half, j * model + (t + 1) * half)
            u = dot(y1b[...], weight(IN + j, cols)) + prm[8 + j : 9 + j, cols]
            phi = 0.5 * (1.0 + lax.erf(u * SQRT_HALF))
            act[2 * j + t] = (u * phi).astype(BF).T.reshape(CS, 4, rows, seq)
            dact[:, wide_cols] = (phi + u * (jnp.exp(-0.5 * u * u) * INV_SQRT_TAU)).astype(BF)

    def act_rows(m):
        return act[:, :, m].reshape(-1, seq)

    def feed_down(m):
        w = wd[:, :, :, :, m].reshape(-1, model)
        part = dot(act_rows(m), w, TN)
        if m == 0:
            h2[...] = part + (n1[...] * prm[3:4, :] + prm[4:5, :]) + prm[5:6, :]
        else:
            h2[...] += part

    def vsum(row, value):
        vg[row : row + 1, :] += jnp.sum(value, axis=0, keepdims=True)

    def norm_back(dn, n, inverse):
        return (dn - jnp.mean(dn, -1, keepdims=True) - n * jnp.mean(dn * n, -1, keepdims=True)) * inverse

    def norm_two(_):
        g2, c2 = prm[6:7, :], prm[7:8, :]

        def tile(i):
            r = span(i, 128)
            h = h2[r, :]
            centred = h - jnp.mean(h, -1, keepdims=True)
            inverse = lax.rsqrt(jnp.mean(centred * centred, -1, keepdims=True) + 1e-06)
            n = centred * inverse
            dcx[r, :] = (n * g2 + c2).astype(BF)
            dy = cot[r, :].astype(F32)
            vsum(6, dy * n)
            vsum(7, dy)
            dh = norm_back(dy * g2, n, inverse)
            h2[r, :] = dh
            low = dh.astype(BF)
            dfb[r, :] = low
            vsum(5, low.astype(F32))

        loop(seq // 128, tile)
        store_out.append(store(dcx, out_hbm.at[0], 1))

    def grad_down(m):
        gd[m] = dot(act_rows(m), dfb[...]).astype(BF).reshape(gd.shape[1:])

    def grad_act(j):
        def tile(t):
            i = 2 * j + t
            cols = span(i, 2 * 4 * rows)
            zz = i // YS
            w = wd[zz // ZL, lax.rem(zz, ZL), lax.rem(i, YS)].reshape(2 * 4 * rows, model)
            du = (dot(dfb[...], w, NT) * dact[:, cols].astype(F32)).astype(BF)
            dact[:, cols] = du
            total = jnp.sum(du.astype(F32), axis=0, keepdims=True)
            vg[8 + j : 9 + j, t * half : (t + 1) * half] = total

        tile(0)
        tile(1)

    def grad_in(j):
        if j == 0:
            sent(*range(DOWN, CHUNKS))
            y1t[...] = y1b[...].T
        g = dot(y1t[...], dact[:, j * model : (j + 1) * model]).astype(BF)
        wd[:, :, :, :, j] = g.reshape(ZH, ZL, YS, CS, rows, model)

    def grad_normed(j):
        h2[...] += dot(dact[:, j * model : (j + 1) * model], weight(IN + j), NT)

    def norm_one_back(_):
        g1 = prm[3:4, :]

        def tile(i):
            r = span(i, 128)
            dy, n = h2[r, :], n1[r, :]
            vsum(3, dy * n)
            vsum(4, dy)
            dh = norm_back(dy * g1, n, rs1[r, :])
            h2[r, :] = dh
            low = dh.astype(BF)
            dfb[r, :] = low
            vsum(2, low.astype(F32))

        loop(seq // 128, tile)

    def grad_out(_):
        g = dot(ct[...], dfb[...]).astype(BF)
        go[0] = g.reshape(ZH, ZL, YS, CS, rows, model)

    def grad_context(_):
        store_out.pop().wait()
        vt[...] = x[...].T
        dcx[...] = dot(dfb[...], weight(OUT), NT).astype(BF)

    def attend_back(half_group):
        g, j = half_group // 2, half_group % 2
        cols = span(j, pair)
        keys = pl.ds(group + j * pair, pair)
        vals = pl.ds(2 * group + j * pair, pair)
        lane = lax.broadcasted_iota(jnp.int32, (seq, pair), 1) // head
        dc = dcx[:, pl.ds(g * group + j * pair, pair)]
        q, k, v = qkv[g, :, cols], qkv[g, :, keys], qkv[g, :, vals]
        kt = k.T
        dk, dv, dq = [], [], []
        for e in range(2):
            probs = pt[g, 2 * j + e]
            dv.append(dot(probs, dc))
            dp = dot(jnp.where(lane == e, v, jnp.zeros((), BF)), dc, NT)
            p32 = probs.astype(F32)
            t = p32 * dp
            ds = (t - p32 * jnp.sum(t, axis=0, keepdims=True)).astype(BF)
            dk.append(dot(ds, q))
            dq.append((dot(kt[e * head : (e + 1) * head, :], ds) * head**-0.5).astype(BF))
        dv = jnp.where(lane == 0, dv[0], dv[1]).astype(BF)
        dq = jnp.concatenate(dq, axis=0).T
        qkv[g, :, cols] = dq
        qkv[g, :, keys] = jnp.where(lane == 0, dk[0], dk[1]).astype(BF)
        qkv[g, :, vals] = dv
        place = pl.ds(g * group + j * pair, pair)
        vg[0:1, place] = jnp.sum(dq.astype(F32), axis=0, keepdims=True)
        vg[1:2, place] = jnp.sum(dv.astype(F32), axis=0, keepdims=True)

    def grad_qkv(g):
        if g == 0:
            sent(*range(IN, DOWN))
        r = dot(vt[...], qkv[g]).astype(BF)
        wa[IN + g] = r.reshape(ZH, ZL, YS, CS, rows, model)

    def grad_x(g):
        before = h2 if g == 0 else n1
        n1[...] = before[...] + dot(qkv[g], weight(g), NT)
        if g == 2:
            store_x.append(store(n1, gtok_hbm.at[0], 2))

    last = len(SUMMED) - 1
    every = (ALL, ALL)
    mine = (zh, zl)

    def at_z(zz):
        return (zz // ZL, lax.rem(zz, ZL))

    def gpiece(k, zi, yy, cc, cols=ALL):
        if k < 4:
            return gd.at[(k, *zi, yy, cc, ALL, cols)]
        if k < 8:
            return wd.at[(*zi, yy, cc, k - 4, ALL, cols)]
        if k < 9:
            return go.at[(0, *zi, yy, cc, ALL, cols)]
        return wa.at[(IN + k - 9, *zi, yy, cc, ALL, cols)]

    def left(i):
        return pl.ds(SUMMED[i][1], SUMMED[i][2])

    def right(i):
        return pl.ds(half + SUMMED[i][1], SUMMED[i][2])

    def near(i):
        return left(i)

    def both(i):
        return (ALL,) if SUMMED[i][2] == half else (left(i), right(i))

    def r_core(i, cols):
        k = SUMMED[i][0]
        return remote(
            gpiece(k, every, ALL, 1 - c, cols), rcore.at[k % RING, :, :, :, :, cols], r_sent.at[i], rrc.at[i], sibling
        )

    def r_ya(i):
        k = SUMMED[i][0]
        src, dst = gpiece(k, every, 1 - y, c, left(i)), rya.at[k, :, :, :, near(i)]
        return remote(src, dst, r_sent.at[i], rry.at[i, 0], across_y)

    def r_xb(i):
        k = SUMMED[i][0]
        src, dst = gpiece(k, (ALL, 1 - px), ALL, c, right(i)), rxb.at[k, :, :, :, near(i)]
        return remote(src, dst, r_sent.at[i], rrx.at[i, 0], across_x)

    def r_za(i, dz):
        k = SUMMED[i][0]
        src, dst = gpiece(k, at_z(ahead(dz)), y, c, left(i)), rza.at[k, dz - 1, :, near(i)]
        return remote(src, dst, r_sent.at[i], rrz.at[i, 0], device(ahead(dz), y, c, px))

    def r_yb(i):
        k = SUMMED[i][0]
        src, dst = gpiece(k, (ALL, px), 1 - y, c, right(i)), ryb.at[k, :, :, near(i)]
        return remote(src, dst, r_sent.at[i], rry.at[i, 1], across_y)

    def r_xa(i):
        k = SUMMED[i][0]
        src, dst = gpiece(k, mine, y, c, left(i)), rxa.at[k, :, near(i)]
        return remote(src, dst, r_sent.at[i], rrx.at[i, 1], across_x)

    def r_zb(i, dz):
        k = SUMMED[i][0]
        src, dst = gpiece(k, at_z(ahead(dz)), y, c, right(i)), rzb.at[k, dz - 1, :, near(i)]
        return remote(src, dst, r_sent.at[i], rrz.at[i, 1], device(ahead(dz), y, c, px))

    def r_fb(i):
        k = SUMMED[i][0]
        return remote(
            gpiece(k, mine, y, c, right(i)), rfb.at[k, :, near(i)], r_sent.at[i], rrf.at[i], across_x
        )

    v_rc = remote(gv.at[:, :, :, 1 - c], rv_core, rv_sent, wrc, sibling)
    v_ry = remote(gv.at[:, :, 1 - y, c], rv_y, rv_sent, wry, across_y)
    v_rx = remote(gv.at[(*mine, y, c)], rv_x, rv_sent, wrx, across_x)

    def v_rz(dz):
        where = device(ahead(dz), y, c, px)
        return remote(gv.at[(*at_z(ahead(dz)), y, c)], rv_z.at[dz - 1], rv_sent, wrz, where)

    same = zl == px

    def add_into(ref, *others):
        if len(others) == 1:
            ref[...] += others[0][...]
            return
        total = ref[...].astype(F32)
        for other in others:
            total = total + other[...].astype(F32)
        ref[...] = total.astype(BF)

    def r0(i):
        for cols in both(i):
            r_core(i, cols).start()
        if i == last:
            v_rc.start()

    def r1(i):
        k, _, width = SUMMED[i]
        drained(wa.at[0, :, :, :, 0, :, pl.ds(0, 2 * width)], rrc.at[i])

        def add(zz):
            for cols in both(i):
                add_into(gpiece(k, at_z(zz), ALL, c, cols), rcore.at[(k % RING, *at_z(zz), ALL, ALL, cols)])

        loop(ZS, add)
        r_ya(i).start()
        r_xb(i).start()
        if i == last:
            v_rc.wait_recv()
            add_into(gv.at[:, :, :, c], rv_core)
            v_ry.start()

    def r2a(i):
        k = SUMMED[i][0]
        r_ya(i).wait_recv()
        add_into(gpiece(k, every, y, c, left(i)), rya.at[k, :, :, :, near(i)])
        for dz in (1, 2, 3):
            r_za(i, dz).start()
        if i == last:
            v_ry.wait_recv()
            add_into(gv.at[:, :, y, c], rv_y)
            for dz in (1, 2, 3):
                v_rz(dz).start()

    def r2b(i):
        k = SUMMED[i][0]
        r_xb(i).wait_recv()
        add_into(gpiece(k, (ALL, px), ALL, c, right(i)), rxb.at[k, :, :, :, near(i)])
        r_yb(i).start()

    def r3a(i):
        k = SUMMED[i][0]
        drained(rza.at[k, :, :, near(i)], rrz.at[i, 0])
        add_into(gpiece(k, mine, y, c, left(i)), *(rza.at[k, dz, :, near(i)] for dz in range(3)))
        r_xa(i).start()
        if i == last:
            drained(rv_z, wrz)
            add_into(gv.at[(*mine, y, c)], rv_z.at[0], rv_z.at[1], rv_z.at[2])
            v_rx.start()

    def r3b(i):
        k = SUMMED[i][0]
        r_yb(i).wait_recv()
        add_into(gpiece(k, (ALL, px), y, c, right(i)), ryb.at[k, :, :, near(i)])
        pl.when(same)(lambda: r_zb(i, 2).start())

        @pl.when(jnp.logical_not(same))
        def _():
            r_zb(i, 1).start()
            r_zb(i, 3).start()

    def r4a(i):
        k = SUMMED[i][0]
        r_xa(i).wait_recv()
        fin[k, :, left(i)] = gpiece(k, mine, y, c, left(i))[...].astype(F32) + rxa[k, :, near(i)].astype(F32)
        if i == last:
            v_rx.wait_recv()
            store_vec.append(store(gv.at[(*mine, y, c)], gvec_hbm.at[0], 3))
            store_vec.append(store(rv_x, gvec_hbm.at[1], 4))
        settle(k)

    def r4b(i):
        k = SUMMED[i][0]

        @pl.when(same)
        def _():
            drained(rzb.at[k, :, :, near(i)], rrz.at[i, 1])
            piece = gpiece(k, mine, y, c, right(i))
            add_into(piece, *(rzb.at[k, dz, :, near(i)] for dz in range(3)))
            r_fb(i).start()
            fin[k, :, right(i)] = piece[...].astype(F32)

    def r5(i):
        k = SUMMED[i][0]

        @pl.when(jnp.logical_not(same))
        def _():
            r_fb(i).wait_recv()
            fin[k, :, right(i)] = rfb[k, :, near(i)].astype(F32)

        settle(k)

    store_out, store_x, store_vec = [], [], []
    open_ends = {k: 2 * sum(part[0] == k for part in SUMMED) for k in range(CHUNKS)}

    def store(src, dst, i=0):
        cp = pltpu.make_async_copy(src, dst, s_store.at[i])
        cp.start()
        return cp

    def settle(k):
        open_ends[k] -= 1
        if open_ends[k]:
            return
        if k < 4:
            store(fin.at[k], gdown_hbm.at[pl.ds(k * rows, rows)])
        elif k < 8:
            store(fin.at[k], gin_hbm.at[:, pl.ds((k - 4) * model, model)])
        elif k < 9:
            store(fin.at[k], gout_hbm)
        else:
            for part in range(3):
                store(
                    fin.at[k, :, pl.ds(part * group, group)],
                    gqkv_hbm.at[:, pl.ds(part * model + (k - 9) * group, group)],
                )

    steps = (
        e1, eo, e2, e3, e4, e5,
        r0, r1, r2a, r2b, r3a, r3b,
        r4a, r4b, r5, spread_params, project, attend,
        out_proj, feed_up, feed_down, norm_two, grad_down, grad_act,
        grad_in, grad_normed, norm_one_back, grad_out, grad_context, attend_back,
        grad_qkv, gather_grads, grad_x,
    )
    vg[...] = jnp.zeros_like(vg)
    for step, i in ORDER:
        if step == S_PROJECT and i == 0:
            load_x.wait()
        if step == S_NORM2:
            load_cot.wait()
        steps[step](i)
    sent(*range(IN))
    vec_sent()
    for i, (_, _, width) in enumerate(SUMMED):
        drained(wa.at[0, :, :, :, :, :, pl.ds(0, 2 * width)], r_sent.at[i])
    drained(gv, rv_sent)
    drained(fin, s_store.at[0])
    for cp in (*store_vec, *store_x):
        cp.wait()


def place_kernel(cuts, *refs):
    count = len(cuts)
    sources, targets, held = refs[: count + 1], refs[count + 1 : 2 * count + 2], refs[2 * count + 2 : 3 * count + 3]
    vector, sem_in, sem_out = refs[3 * count + 3 :]
    first = pltpu.make_async_copy(sources[count], held[count], sem_in.at[sum(cuts)])
    first.start()
    moves = []
    for src, dst, mid, parts in zip(sources, targets, held, cuts):
        size = src.shape[-2] // parts
        for j in range(parts):
            at = (slice(None),) * (len(src.shape) - 2) + (pl.ds(j * size, size),)
            i = len(moves)
            moves.append(
                (
                    pltpu.make_async_copy(src.at[at], mid.at[at], sem_in.at[i]),
                    pltpu.make_async_copy(mid.at[at], dst.at[at], sem_out.at[i]),
                )
            )
    for into, _ in moves:
        into.start()
    first.wait()
    segment = vector.shape[0] // 3
    total = held[count][0].astype(F32) + held[count][1].astype(F32)
    vector[...] = jnp.concatenate([total[s : s + 1, 0:segment] for s in range(3)], axis=1).reshape(-1)
    last = pltpu.make_async_copy(vector, targets[count], sem_out.at[sum(cuts)])
    last.start()
    for into, out in moves:
        into.wait()
        out.start()
    for _, out in moves:
        out.wait()
    last.wait()


def fused_layer(tokens, lengths, w_qkv, w_out, w_in, w_down, norms_biases, cotangent):
    seq, model = tokens.shape[1:]
    rows = w_qkv.shape[0]
    hidden = w_in.shape[1]
    half = model // 2
    group = model // 3
    vm, dma = pltpu.VMEM, pltpu.SemaphoreType.DMA
    grid = (ZH, ZL, YS, CS)
    n, m, u = CHUNKS, len(GATHERED), len(SUMMED)
    scratch = [
        vm((DOWN, *grid, rows, model), BF),
        vm((*grid, 4, rows, model), BF),
        vm((*grid, 16, 256), BF),
        vm((4, *grid, rows, model), BF),
        vm((1, *grid, rows, model), BF),
        vm((*grid, 16, 256), BF),
        vm((RING, ZH, ZL, YS, rows, model), BF),
        vm((n, ZH, ZL, rows, half), BF),
        vm((n, ZH, YS, rows, half), BF),
        vm((n, 3, rows, half), BF),
        vm((n, ZH, rows, half), BF),
        vm((n, 3, rows, half), BF),
        vm((n, rows, half), BF),
        vm((n, rows, half), BF),
        vm((ZH, ZL, YS, 16, 256), BF),
        vm((ZH, ZL, 16, 256), BF),
        vm((3, 16, 256), BF),
        vm((16, 256), BF),
        vm((n, rows, model), F32),
        vm(norms_biases.shape, BF),
        vm((seq, model), BF),
        vm((seq, model), BF),
        vm((3, seq, model), BF),
        vm((model, seq), BF),
        vm((3, group // (model // HEADS), seq, seq), BF),
        vm((model, seq), BF),
        vm((seq, model), F32),
        vm((seq, model), BF),
        vm((model, seq), BF),
        vm((ZS * YS, CS, 4, rows, seq), BF),
        vm((seq, hidden), BF),
        vm((seq, model), F32),
        vm((seq, model), BF),
        vm((seq, model), BF),
        vm((seq, 1), F32),
        vm((16, model), F32),
        vm((16, model), F32),
        dma((n,)), dma((3,)), dma((5,)),
        dma((m,)), dma((m,)), dma((m,)), dma((m,)), dma((m,)), dma, dma, dma, dma,
        dma((u,)), dma, dma((u,)), dma((u, 2)), dma((u, 2)), dma((u, 2)), dma((u,)), dma, dma, dma, dma,
    ]
    hbm = pl.BlockSpec(memory_space=pl.ANY)
    shape = jax.ShapeDtypeStruct
    outs = pl.pallas_call(
        layer_kernel,
        out_shape=(
            shape(tokens.shape, BF),
            shape(tokens.shape, F32),
            shape(w_qkv.shape, F32),
            shape(w_out.shape, F32),
            shape(w_in.shape, F32),
            shape(w_down.shape, F32),
            shape((2, 16, 256), BF),
        ),
        in_specs=[hbm, pl.BlockSpec(memory_space=pltpu.SMEM)] + [hbm] * 6,
        out_specs=(hbm,) * 7,
        scratch_shapes=scratch,
        compiler_params=pltpu.CompilerParams(
            collective_id=0, has_side_effects=True, vmem_limit_bytes=64 << 20
        ),
        name="layer",
    )(tokens, lengths, w_qkv, w_out, w_in, w_down, norms_biases, cotangent)
    cuts = (1, 2, 1, 1, 1, 1)
    *placed, grad_vector = pl.pallas_call(
        functools.partial(place_kernel, cuts),
        out_shape=(*(shape(o.shape, o.dtype) for o in outs[:6]), shape(norms_biases.shape, F32)),
        in_specs=[hbm] * 7,
        out_specs=(hbm,) * 7,
        scratch_shapes=[vm(o.shape, o.dtype) for o in outs]
        + [vm(norms_biases.shape, F32), dma((sum(cuts) + 1,)), dma((sum(cuts) + 1,))],
        name="place",
    )(*outs)
    return (*placed, grad_vector)


def norm_rows(values, gain_row, shift_row):
    average = jnp.mean(values, -1, keepdims=True)
    centred = values - average
    spread = jnp.mean(centred * centred, -1, keepdims=True)
    return centred * lax.rsqrt(spread + 1e-06) * gain_row + shift_row


def gelu_exact(values):
    return jax.nn.gelu(values, approximate=False)


def column_sum(values):
    return jnp.sum(values.astype(jnp.float32), 0)


def split_vector(vector, model_width, hidden_width):
    segments = [
        vector[position * model_width : (position + 1) * model_width] for position in range(8)
    ]
    return segments + [vector[8 * model_width : 8 * model_width + hidden_width]]


def pair_blocks(projected, head_count):
    row_count = projected.shape[0]
    pair_count = head_count // 2
    pair_width = projected.shape[1] // (3 * pair_count)
    return projected.reshape(row_count, 3, pair_count, pair_width).transpose(2, 1, 0, 3)


def unpair_blocks(blocks):
    pair_count = blocks.shape[0]
    row_count = blocks.shape[2]
    pair_width = blocks.shape[3]
    return blocks.transpose(2, 1, 0, 3).reshape(row_count, 3 * pair_count * pair_width)


def pair_scores(head_block, usable, factor):
    row_count = head_block.shape[1]
    queries = head_block[0].reshape(row_count, 2, -1)
    key_rows = head_block[1].reshape(row_count, 2, -1)
    values = head_block[2].reshape(row_count, 2, -1)
    scores = (
        jnp.einsum("qhd,khd->hqk", queries, key_rows, preferred_element_type=jnp.float32) * factor
    )
    return (queries, key_rows, values, jnp.where(usable[None, None, :], scores, -1000000000.0))


def attention_forward(blocks, usable, factor):

    def one_pair(head_block):
        queries, key_rows, values, scores = pair_scores(head_block, usable, factor)
        highest = jnp.max(scores, -1, keepdims=True)
        raised = jnp.exp(scores - highest)
        summed = jnp.sum(raised, -1, keepdims=True)
        attend = (raised / summed).astype(jnp.bfloat16)
        context = jnp.einsum("hqk,khd->qhd", attend, values, preferred_element_type=jnp.float32)
        return (context.reshape(context.shape[0], -1), highest[..., 0] + jnp.log(summed[..., 0]))

    return lax.map(one_pair, blocks)


def attention_backward(blocks, grad_pairs, log_totals, usable, factor):

    def one_pair(pair_inputs):
        head_block, grad_context, log_total = pair_inputs
        queries, key_rows, values, scores = pair_scores(head_block, usable, factor)
        attend = jnp.exp(scores - log_total[..., None])
        row_count = grad_context.shape[0]
        grad_heads = grad_context.reshape(row_count, 2, -1)
        grad_values = jnp.einsum(
            "hqk,qhd->khd",
            attend.astype(jnp.bfloat16),
            grad_heads,
            preferred_element_type=jnp.float32,
        )
        grad_attend = jnp.einsum(
            "qhd,khd->hqk", grad_heads, values, preferred_element_type=jnp.float32
        )
        grad_scores = attend * (grad_attend - jnp.sum(attend * grad_attend, -1, keepdims=True))
        grad_low = grad_scores.astype(jnp.bfloat16)
        grad_queries = (
            jnp.einsum("hqk,khd->qhd", grad_low, key_rows, preferred_element_type=jnp.float32)
            * factor
        )
        grad_keys = (
            jnp.einsum("hqk,qhd->khd", grad_low, queries, preferred_element_type=jnp.float32)
            * factor
        )
        return jnp.stack(
            [
                grad_queries.reshape(row_count, -1),
                grad_keys.reshape(row_count, -1),
                grad_values.reshape(row_count, -1),
            ]
        )

    return lax.map(one_pair, (blocks, grad_pairs, log_totals))


def layer_forward(inputs, length, weights):
    w_qkv, w_out, w_in, w_down, vector = weights
    row_count, model_width = inputs.shape
    hidden_width = w_in.shape[1]
    params = split_vector(vector.astype(jnp.float32), model_width, hidden_width)
    joined_bias = jnp.concatenate([params[0], jnp.zeros((model_width,), jnp.float32), params[1]])
    projected = (jnp.dot(inputs, w_qkv, preferred_element_type=jnp.float32) + joined_bias).astype(
        jnp.bfloat16
    )
    blocks = pair_blocks(projected, HEADS)
    usable = jnp.arange(row_count) < length
    factor = (model_width // HEADS) ** (-0.5)
    context_pairs, log_totals = attention_forward(blocks, usable, factor)
    context = context_pairs.transpose(1, 0, 2).reshape(row_count, model_width).astype(jnp.bfloat16)
    resid_one = inputs.astype(jnp.float32) + (
        jnp.dot(context, w_out, preferred_element_type=jnp.float32) + params[2]
    )
    normed_one = norm_rows(resid_one, params[3], params[4])
    normed_low = normed_one.astype(jnp.bfloat16)
    pre_act = jnp.dot(normed_low, w_in, preferred_element_type=jnp.float32) + params[8]
    activated = gelu_exact(pre_act).astype(jnp.bfloat16)
    resid_two = normed_one + (
        jnp.dot(activated, w_down, preferred_element_type=jnp.float32) + params[5]
    )
    result = norm_rows(resid_two, params[6], params[7])
    saved = (
        params,
        blocks,
        usable,
        factor,
        log_totals,
        context,
        resid_one,
        normed_low,
        pre_act,
        activated,
        resid_two,
    )
    return (result, saved)


def layer_backward(inputs, length, grad_result, weights):
    w_qkv, w_out, w_in, w_down, vector = weights
    unused_result, saved = layer_forward(inputs, length, weights)
    (
        params,
        blocks,
        usable,
        factor,
        log_totals,
        context,
        resid_one,
        normed_low,
        pre_act,
        activated,
        resid_two,
    ) = saved
    row_count, model_width = inputs.shape
    unused_two, norm_two_back = jax.vjp(norm_rows, resid_two, params[6], params[7])
    grad_two, grad_gain_two, grad_shift_two = norm_two_back(grad_result)
    grad_feed = grad_two.astype(jnp.bfloat16)
    grad_down = jnp.einsum("sf,sd->fd", activated, grad_feed, preferred_element_type=jnp.float32)
    grad_act = jnp.einsum("sd,fd->sf", grad_feed, w_down, preferred_element_type=jnp.float32)
    unused_act, gelu_back = jax.vjp(gelu_exact, pre_act)
    grad_pre = gelu_back(grad_act)[0].astype(jnp.bfloat16)
    grad_in = jnp.einsum("sd,sf->df", normed_low, grad_pre, preferred_element_type=jnp.float32)
    grad_normed = grad_two + jnp.einsum(
        "sf,df->sd", grad_pre, w_in, preferred_element_type=jnp.float32
    )
    unused_one, norm_one_back = jax.vjp(norm_rows, resid_one, params[3], params[4])
    grad_one, grad_gain_one, grad_shift_one = norm_one_back(grad_normed)
    grad_attended = grad_one.astype(jnp.bfloat16)
    grad_out = jnp.einsum("sd,se->de", context, grad_attended, preferred_element_type=jnp.float32)
    grad_context = jnp.einsum(
        "se,de->sd", grad_attended, w_out, preferred_element_type=jnp.float32
    ).astype(jnp.bfloat16)
    grad_pairs = grad_context.reshape(row_count, HEADS // 2, -1).transpose(1, 0, 2)
    grad_blocks = attention_backward(blocks, grad_pairs, log_totals, usable, factor)
    grad_projected = unpair_blocks(grad_blocks).astype(jnp.bfloat16)
    grad_qkv = jnp.einsum("sd,se->de", inputs, grad_projected, preferred_element_type=jnp.float32)
    grad_inputs = grad_one + jnp.einsum(
        "se,de->sd", grad_projected, w_qkv, preferred_element_type=jnp.float32
    )
    projected_sums = column_sum(grad_projected)
    grad_vector = jnp.concatenate(
        [
            projected_sums[:model_width],
            projected_sums[2 * model_width :],
            column_sum(grad_attended),
            grad_gain_one,
            grad_shift_one,
            column_sum(grad_feed),
            grad_gain_two,
            grad_shift_two,
            column_sum(grad_pre),
        ]
    )
    return (grad_inputs, (grad_qkv, grad_out, grad_in, grad_down, grad_vector))


def local(tokens, lengths, w_qkv, w_out, w_in, w_down, norms_biases, cotangent):
    weights = (
        lax.all_gather(w_qkv, "wide", axis=0, tiled=True),
        lax.all_gather(w_out, "wide", axis=0, tiled=True),
        lax.all_gather(w_in, "wide", axis=0, tiled=True),
        lax.all_gather(w_down, "wide", axis=0, tiled=True),
        lax.all_gather(norms_biases, "wide", axis=0, tiled=True),
    )

    def forward_one(sequence):
        return layer_forward(sequence[0], sequence[1], weights)[0].astype(jnp.bfloat16)

    output = lax.map(forward_one, (tokens, lengths))
    second_copy = (
        lax.all_gather(w_qkv, "wide", axis=0, tiled=True),
        lax.all_gather(w_out, "wide", axis=0, tiled=True),
        lax.all_gather(w_in, "wide", axis=0, tiled=True),
        lax.all_gather(w_down, "wide", axis=0, tiled=True),
        lax.all_gather(norms_biases, "wide", axis=0, tiled=True),
    )
    running = tuple((jnp.zeros(member.shape, jnp.float32) for member in second_copy))

    def advance(totals, sequence):
        grad_inputs, gradients = layer_backward(
            sequence[0], sequence[1], sequence[2].astype(jnp.float32), second_copy
        )
        return (jax.tree.map(jnp.add, totals, gradients), grad_inputs)

    totals, grad_tokens = lax.scan(advance, running, (tokens, lengths, cotangent))
    owned_rows = (
        lax.psum_scatter(
            totals[0].astype(jnp.bfloat16), "wide", scatter_dimension=0, tiled=True
        ).astype(jnp.float32),
        lax.psum_scatter(
            totals[1].astype(jnp.bfloat16), "wide", scatter_dimension=0, tiled=True
        ).astype(jnp.float32),
        lax.psum_scatter(
            totals[2].astype(jnp.bfloat16), "wide", scatter_dimension=0, tiled=True
        ).astype(jnp.float32),
        lax.psum_scatter(
            totals[3].astype(jnp.bfloat16), "wide", scatter_dimension=0, tiled=True
        ).astype(jnp.float32),
        lax.psum_scatter(
            totals[4].astype(jnp.bfloat16), "wide", scatter_dimension=0, tiled=True
        ).astype(jnp.float32),
    )
    summed_all = (
        lax.psum(owned_rows[0].astype(jnp.bfloat16), "narrow").astype(jnp.float32),
        lax.psum(owned_rows[1].astype(jnp.bfloat16), "narrow").astype(jnp.float32),
        lax.psum(owned_rows[2].astype(jnp.bfloat16), "narrow").astype(jnp.float32),
        lax.psum(owned_rows[3].astype(jnp.bfloat16), "narrow").astype(jnp.float32),
        lax.psum(owned_rows[4].astype(jnp.bfloat16), "narrow").astype(jnp.float32),
    )
    return (
        output,
        grad_tokens,
        summed_all[0],
        summed_all[1],
        summed_all[2],
        summed_all[3],
        summed_all[4],
    )


def solution(mesh):
    in_specs = (
        P(("wide", "narrow"), None, None),
        P(("wide", "narrow")),
        P("wide", None),
        P("wide", None),
        P("wide", None),
        P("wide", None),
        P("wide"),
        P(("wide", "narrow"), None, None),
    )
    out_specs = (
        P(("wide", "narrow"), None, None),
        P(("wide", "narrow"), None, None),
        P("wide", None),
        P("wide", None),
        P("wide", None),
        P("wide", None),
        P("wide"),
    )
    chips = (ZS * YS * CS, 2)
    fused = tuple(mesh.shape[axis] for axis in ("wide", "narrow")) == chips
    step = fused_layer if fused else local
    return jax.shard_map(step, mesh=mesh, in_specs=in_specs, out_specs=out_specs, check_vma=False)
```

```python
import functools

import jax
import jax.numpy as jnp
import numpy as np
from jax import lax
from jax.experimental import pallas as pl
from jax.experimental.pallas import tpu as pltpu
from jax.sharding import PartitionSpec as P

HEADS = 12
MESH = pl.DeviceIdType.MESH
BF = jnp.bfloat16
F32 = jnp.float32
NT = (((1,), (1,)), ((), ()))
TN = (((0,), (0,)), ((), ()))
ZH, ZL, YS, CS = 2, 2, 2, 2
ZS = ZH * ZL
QKV, OUT, IN, DOWN, CHUNKS = 0, 3, 4, 8, 12
RING = 8
(
    S_E1, S_EO, S_E2, S_E3, S_E4, S_E5, S_R0, S_R1, S_R2A, S_R2B, S_R3A,
    S_R3B, S_R4A, S_R4B, S_R5, S_SPREAD, S_PROJECT, S_ATTEND, S_OUT, S_UP, S_DOWN, S_NORM2,
    S_GDOWN, S_GACT, S_GIN, S_GNORM, S_NORM1, S_GOUT, S_GCTX, S_ABACK, S_GQKV, S_GGRADS, S_GX,
) = range(33)
GATHERED = (
    (0, 0, 384), (0, 384, 384), (1, 0, 384), (1, 384, 384), (2, 0, 384), (2, 384, 384), (3, 0, 384), (3, 384, 384),
    (4, 0, 384), (4, 384, 384), (5, 0, 384), (5, 384, 384), (6, 0, 384), (6, 384, 384), (7, 0, 384), (7, 384, 384),
    (8, 0, 384), (8, 384, 384), (9, 0, 384), (9, 384, 384), (10, 0, 384), (10, 384, 384), (11, 0, 384), (11, 384, 384),
)
SUMMED = (
    (0, 0, 384), (1, 0, 384), (2, 0, 384), (3, 0, 384), (4, 0, 384), (5, 0, 384), (6, 0, 384), (7, 0, 384),
    (8, 0, 384), (9, 0, 384), (10, 0, 384), (11, 0, 384),
)
ORDER = (
    (S_EO, 0), (S_E1, 0), (S_EO, 1), (S_E1, 1), (S_E1, 2), (S_EO, 2), (S_EO, 3), (S_E1, 3), (S_EO, 4), (S_EO, 5),
    (S_E2, 0), (S_E1, 4), (S_EO, 6), (S_E2, 1), (S_E1, 5), (S_EO, 7), (S_E3, 0), (S_E2, 2), (S_E1, 6), (S_EO, 8),
    (S_E3, 1), (S_E2, 3), (S_E4, 0), (S_E1, 7), (S_EO, 9), (S_E5, 0), (S_E3, 2), (S_E2, 4), (S_E4, 1), (S_E1, 8),
    (S_EO, 10), (S_E5, 1), (S_E3, 3), (S_SPREAD, 0), (S_E4, 2), (S_E2, 5), (S_E1, 9), (S_EO, 11), (S_PROJECT, 0), (S_E5, 2),
    (S_E3, 4), (S_E4, 3), (S_E2, 6), (S_E1, 10), (S_EO, 12), (S_ATTEND, 0), (S_E5, 3), (S_E4, 4), (S_E3, 5), (S_E3, 6),
    (S_E2, 7), (S_E2, 8), (S_E1, 11), (S_E1, 12), (S_E5, 4), (S_EO, 13), (S_EO, 14), (S_PROJECT, 1), (S_E2, 9), (S_E4, 5),
    (S_E1, 13), (S_EO, 15), (S_ATTEND, 1), (S_E5, 5), (S_E4, 6), (S_E3, 7), (S_E3, 8), (S_E2, 10), (S_E1, 14), (S_E2, 11),
    (S_E1, 15), (S_E5, 6), (S_EO, 16), (S_EO, 17), (S_PROJECT, 2), (S_E3, 9), (S_E4, 7), (S_E2, 12), (S_E1, 16), (S_EO, 18),
    (S_ATTEND, 2), (S_E5, 7), (S_E4, 8), (S_E4, 9), (S_E3, 10), (S_E3, 11), (S_E2, 13), (S_E2, 14), (S_E1, 17), (S_E5, 8),
    (S_E1, 18), (S_E5, 9), (S_E3, 12), (S_EO, 19), (S_EO, 20), (S_OUT, 0), (S_E4, 10), (S_E3, 13), (S_E4, 11), (S_E2, 15),
    (S_E2, 16), (S_E5, 10), (S_E1, 19), (S_E1, 20), (S_E5, 11), (S_E3, 14), (S_EO, 21), (S_EO, 22), (S_UP, 0), (S_E4, 12),
    (S_E2, 17), (S_E4, 13), (S_E3, 15), (S_E1, 21), (S_E5, 12), (S_E2, 18), (S_E5, 13), (S_E1, 22), (S_EO, 23), (S_UP, 1),
    (S_E4, 14), (S_E3, 16), (S_E2, 19), (S_E1, 23), (S_UP, 2), (S_E5, 14), (S_E4, 15), (S_E3, 17), (S_E2, 20), (S_E3, 18),
    (S_E4, 16), (S_E5, 15), (S_UP, 3), (S_E5, 16), (S_E4, 17), (S_E3, 19), (S_E2, 21), (S_E2, 22), (S_E5, 17), (S_E3, 20),
    (S_E4, 18), (S_DOWN, 0), (S_E4, 19), (S_E5, 18), (S_E2, 23), (S_E3, 21), (S_E5, 19), (S_DOWN, 1), (S_E3, 22), (S_E4, 20),
    (S_E3, 23), (S_E5, 20), (S_E4, 21), (S_E4, 22), (S_E5, 21), (S_DOWN, 2), (S_E5, 22), (S_E4, 23), (S_E5, 23), (S_DOWN, 3),
    (S_NORM2, 0), (S_GDOWN, 0), (S_R0, 0), (S_GDOWN, 1), (S_GACT, 0), (S_R1, 0), (S_R0, 1), (S_GDOWN, 2), (S_GDOWN, 3), (S_R0, 2),
    (S_R0, 3), (S_R1, 1), (S_GACT, 1), (S_GACT, 2), (S_GACT, 3), (S_R2A, 0), (S_R1, 3), (S_GNORM, 0), (S_R1, 2), (S_GIN, 0),
    (S_R2A, 1), (S_GIN, 1), (S_R2B, 1), (S_R2B, 0), (S_R0, 4), (S_GNORM, 1), (S_R2A, 3), (S_GIN, 2), (S_GIN, 3), (S_R2B, 3),
    (S_R0, 5), (S_R2A, 2), (S_GNORM, 2), (S_GNORM, 3), (S_R0, 6), (S_R0, 7), (S_R1, 4), (S_R3B, 1), (S_NORM1, 0), (S_GOUT, 0),
    (S_R1, 6), (S_R3B, 0), (S_R0, 8), (S_R3B, 3), (S_R1, 5), (S_GCTX, 0), (S_R3A, 3), (S_R1, 8), (S_R2A, 4), (S_ABACK, 0),
    (S_R2A, 6), (S_ABACK, 1), (S_R2A, 5), (S_R1, 7), (S_R2B, 2), (S_GQKV, 0), (S_R2B, 5), (S_R3A, 2), (S_R4B, 3), (S_R2A, 8),
    (S_ABACK, 2), (S_R2A, 7), (S_R0, 9), (S_R2B, 4), (S_GQKV, 1), (S_R3B, 2), (S_R2B, 7), (S_R2B, 8), (S_GQKV, 2), (S_R1, 9),
    (S_R2B, 6), (S_R3B, 5), (S_R3A, 5), (S_GX, 0), (S_R0, 10), (S_R3A, 1), (S_R4A, 3), (S_R3B, 4), (S_GGRADS, 0), (S_R4B, 0),
    (S_R3A, 8), (S_R3B, 8), (S_R0, 11), (S_R3B, 7), (S_GX, 1), (S_R2B, 9), (S_R1, 11), (S_R2A, 9), (S_R3B, 6), (S_R5, 0),
    (S_R1, 10), (S_R3A, 6), (S_GX, 2), (S_R3A, 7), (S_R3B, 9), (S_R4B, 7), (S_R2A, 11), (S_R2B, 11), (S_R5, 3), (S_R3A, 4),
    (S_R4B, 8), (S_R4A, 2), (S_R4A, 1), (S_R4B, 1), (S_R3A, 0), (S_R4B, 5), (S_R2B, 10), (S_R2A, 10), (S_R4B, 4), (S_R3A, 9),
    (S_R4B, 2), (S_R3B, 11), (S_R4A, 5), (S_R4B, 9), (S_R5, 1), (S_R4A, 0), (S_R4A, 7), (S_R3B, 10), (S_R4A, 4), (S_R3A, 11),
    (S_R5, 9), (S_R3A, 10), (S_R4A, 8), (S_R4A, 9), (S_R4B, 6), (S_R5, 4), (S_R4A, 11), (S_R5, 7), (S_R4B, 11), (S_R5, 2),
    (S_R5, 6), (S_R5, 8), (S_R4B, 10), (S_R4A, 10), (S_R5, 5), (S_R4A, 6), (S_R5, 11), (S_R5, 10),
)
SQRT_HALF = 0.7071067811865476
INV_SQRT_TAU = 0.3989422804014327


def dot(left, right, dims=None):
    if dims is None:
        return jnp.dot(left, right, preferred_element_type=F32)
    return lax.dot_general(left, right, dims, preferred_element_type=F32)


def loop(count, body):
    def step(index, carry):
        body(index)
        return carry

    lax.fori_loop(0, count, step, 0)


def span(index, size):
    return pl.ds(pl.multiple_of(index * size, size), size)


def layer_kernel(
    x_hbm, len_ref, wqkv_hbm, wout_hbm, win_hbm, wdown_hbm, vec_hbm, cot_hbm,
    out_hbm, gtok_hbm, gqkv_hbm, gout_hbm, gin_hbm, gdown_hbm, gvec_hbm,
    wa, wd, vb, gd, go, gv, rcore, rya, rxb, rza, ryb, rzb, rxa, rfb, rv_core, rv_y, rv_z, rv_x, fin, vec,
    x, cot, qkv, vt, pt, ct, n1, y1b, y1t, act, dact, h2, dfb, dcx, rs1, prm, vg,
    s_load, s_io, s_store,
    g_sent, grz, gry, grx, grc, v_sent, vrz, vry, vrc,
    r_sent, rv_sent, rrc, rry, rrx, rrz, rrf, wrc, wry, wrz, wrx,
):
    seq, model = x.shape
    rows = wa.shape[-2]
    hidden = dact.shape[1]
    pair = 2 * (model // HEADS)
    head = model // HEADS
    group = model // 3
    half = model // 2
    wide = lax.axis_index("wide")
    px = lax.axis_index("narrow")
    c = lax.rem(wide, CS)
    y = lax.rem(wide // CS, YS)
    z = wide // (CS * YS)
    zl = lax.rem(z, ZL)
    zh = z // ZL

    def device(zz, yy, cc, xx):
        return ((zz * YS + yy) * CS + cc, xx)

    sibling = device(z, y, 1 - c, px)
    across_y = device(z, 1 - y, c, px)
    across_x = device(z, y, c, 1 - px)

    def ahead(dz):
        return lax.rem(z + dz, ZS)

    def behind(dz):
        return lax.rem(z + ZS - dz, ZS)

    def remote(src, dst, send, recv, where):
        return pltpu.make_async_remote_copy(
            src_ref=src, dst_ref=dst, send_sem=send, recv_sem=recv, device_id=where, device_id_type=MESH
        )

    ALL = slice(None)

    def drained(ref, sem):
        pltpu.make_async_copy(ref, ref, sem).wait()

    def rows_of(count, cols):
        return x.at[pl.ds(0, count), pl.ds(0, cols)]

    def load(src, dst, sem):
        cp = pltpu.make_async_copy(src, dst, sem)
        cp.start()
        return cp

    load_vec = load(vec_hbm, vec, s_io.at[2])
    load_x = load(x_hbm.at[0], x, s_io.at[0])
    for k in range(CHUNKS):
        if k < OUT:
            for part in range(3):
                load(
                    wqkv_hbm.at[:, pl.ds(part * model + k * group, group)],
                    wa.at[k, zh, zl, y, c, :, pl.ds(part * group, group)],
                    s_load.at[k],
                )
        elif k < IN:
            load(wout_hbm, wa.at[k, zh, zl, y, c], s_load.at[k])
        elif k < DOWN:
            load(win_hbm.at[:, pl.ds((k - IN) * model, model)], wa.at[k, zh, zl, y, c], s_load.at[k])
        else:
            load(wdown_hbm.at[pl.ds((k - DOWN) * rows, rows)], wd.at[zh, zl, y, c, k - DOWN], s_load.at[k])
    load_cot = load(cot_hbm.at[0], cot, s_io.at[1])

    barrier = pltpu.get_barrier_semaphore()
    for where in (sibling, across_y, across_x, *(device(ahead(dz), y, c, px) for dz in (1, 2, 3))):
        pl.semaphore_signal(barrier, inc=1, device_id=where, device_id_type=MESH)
    pl.semaphore_wait(barrier, 6)

    third = rows // 3
    kept = pl.ds(pl.multiple_of(px * third, third), 2 * third)
    given = pl.ds(pl.multiple_of(px * 2 * third, third), third)
    taken = pl.ds(pl.multiple_of((1 - px) * 2 * third, third), third)

    def wcut(i, zz, yy, cc, r=ALL):
        k, first, count = GATHERED[i]
        cols = pl.ds(first, count)
        zi = (ALL, ALL) if zz is None else (zz // ZL, lax.rem(zz, ZL))
        if k < DOWN:
            return wa.at[(k, *zi, yy, cc, r, cols)]
        return wd.at[(*zi, yy, cc, k - DOWN, r, cols)]

    def g_z(i, dz, source):
        piece = wcut(i, source, y, c, kept)
        return remote(piece, piece, g_sent.at[i], grz.at[i], device(ahead(dz), y, c, px))

    def g_y(i, dz, column):
        piece = wcut(i, behind(dz), column, c, kept)
        return remote(piece, piece, g_sent.at[i], gry.at[i], across_y)

    def g_x1(i, dz, r):
        piece = wcut(i, behind(dz), y, c, r)
        return remote(piece, piece, g_sent.at[i], grx.at[i], across_x)

    def g_x2(i, r):
        piece = wcut(i, None, 1 - y, c, r)
        return remote(piece, piece, g_sent.at[i], grx.at[i], across_x)

    def g_core(i, core):
        piece = wcut(i, None, ALL, core)
        return remote(piece, piece, g_sent.at[i], grc.at[i], sibling)

    def v_z(dz, source):
        piece = vb.at[source // ZL, lax.rem(source, ZL), y, c]
        return remote(piece, piece, v_sent, vrz, device(ahead(dz), y, c, px))

    def v_y(column):
        piece = vb.at[:, :, column, c]
        return remote(piece, piece, v_sent, vry, across_y)

    def v_core(core):
        piece = vb.at[:, :, :, core]
        return remote(piece, piece, v_sent, vrc, sibling)

    loaded = set()

    def own(k):
        if k not in loaded:
            loaded.add(k)
            drained(rows_of(rows, model), s_load.at[k])

    def e1(i):
        own(GATHERED[i][0])
        for dz in (1, 2, 3):
            g_z(i, dz, z).start()
        if i == 1:
            load_vec.wait()
            segment = vec.shape[0] // 3
            row = vec[...].astype(F32).reshape(1, -1)
            vb[zh, zl, y, c] = jnp.zeros(vb.shape[-2:], BF)
            for s in range(3):
                vb[zh, zl, y, c, s : s + 1, 0:segment] = row[:, s * segment : (s + 1) * segment].astype(BF)
            for dz in (1, 2, 3):
                v_z(dz, z).start()

    def eo(i):
        own(GATHERED[i][0])
        g_y(i, 0, y).start()

    def e2(i):
        if i == 1:
            drained(rv_z, vrz)
            v_y(y).start()
        drained(rows_of(3 * 2 * third, GATHERED[i][2]), grz.at[i])
        for dz in (1, 2, 3):
            g_y(i, dz, y).start()
            g_x1(i, dz, given).start()

    def e3(i):
        if i == 1:
            v_y(1 - y).wait_recv()
            v_core(c).start()
        drained(rows_of(ZS * 2 * third, GATHERED[i][2]), gry.at[i])
        g_x2(i, given).start()

    def e4(i):
        drained(rows_of((ZS + ZS - 1) * third, GATHERED[i][2]), grx.at[i])
        g_core(i, c).start()

    def e5(i):
        if i == 1:
            v_core(1 - c).wait_recv()
        g_core(i, 1 - c).wait_recv()

    def sent(*chunks):
        count = (3 + ZS) * 2 * third + (2 * ZS - 1) * third + ZS * YS * rows
        for i, (k, _, cols) in enumerate(GATHERED):
            if k in chunks:
                drained(qkv.at[:, pl.ds(0, count // 3), pl.ds(0, cols)], g_sent.at[i])

    def vec_sent():
        drained(x.at[pl.ds(0, 80)], v_sent)

    def place_matrix(k, lanes):
        i = lax.broadcasted_iota(jnp.int32, (lanes, model), 0)
        j = lax.broadcasted_iota(jnp.int32, (lanes, model), 1)
        quarter = model // 4
        return jnp.where((i < quarter) & (j == i + k * quarter), 1.0, 0.0).astype(BF)

    def pick_matrix(k, count, total, slot):
        b = lax.broadcasted_iota(jnp.int32, (count, total), 0)
        r = lax.broadcasted_iota(jnp.int32, (count, total), 1)
        segment = 4 * b + k
        return jnp.where((r == slot * (segment // 3) + lax.rem(segment, 3)) & (b < 12), 1.0, 0.0).astype(BF)

    def spread_params(_):
        lanes = vb.shape[-1]
        segments = vb[...].reshape(-1, lanes)
        total = None
        for k in range(4):
            picked = dot(pick_matrix(k, 16, segments.shape[0], vb.shape[-2]), segments).astype(BF)
            part = dot(picked, place_matrix(k, lanes))
            total = part if total is None else total + part
        prm[...] = total

    def gather_grads(_):
        lanes = gv.shape[-1]
        low = vg[...].astype(BF)
        total = None
        for k in range(4):
            cut = dot(low, place_matrix(k, lanes), NT).astype(BF)
            part = dot(pick_matrix(k, 16, 16 * gv.shape[-2], gv.shape[-2]), cut, TN)
            total = part if total is None else total + part
        gv[...] = total.astype(BF).reshape(gv.shape)

    def weight(k, cols=ALL):
        block = wa[k, :, :, :, :, :, cols]
        return block.reshape(-1, block.shape[-1])

    def project(g):
        grouped = span(g, group)

        def tile(part):
            cols = span(part, group)
            bias = jnp.where(part == 0, prm[0:1, grouped], jnp.where(part == 2, prm[1:2, grouped], 0.0))
            low = (dot(x[...], weight(g, cols)) + bias).astype(BF)
            qkv[g, :, cols] = low * jnp.where(part == 0, head**-0.5, 1.0).astype(BF)

        loop(3, tile)
        vt[grouped, :] = qkv[g, :, 2 * group :].T

    def attend(g):
        length = len_ref[0]

        def one(h):
            cols = span(h // 2, pair)
            keys = pl.ds(pl.multiple_of(group + (h // 2) * pair, pair), pair)
            lane = lax.broadcasted_iota(jnp.int32, (seq, pair), 1) // head
            masked = jnp.where(lane == lax.rem(h, 2), qkv[g, :, keys], jnp.zeros((), BF))
            scores = dot(masked, qkv[g, :, cols], NT)
            key = lax.broadcasted_iota(jnp.int32, scores.shape, 0)
            scores = jnp.where(key < length, scores, -1000000000.0)
            raised = jnp.exp(scores - jnp.max(scores, axis=0, keepdims=True))
            probs = (raised * (1.0 / jnp.sum(raised, axis=0, keepdims=True))).astype(BF)
            pt[g, h] = probs
            mine = pl.ds(pl.multiple_of(g * group + h * head, head), head)
            ct[mine, :] = dot(vt[mine, :], probs).astype(BF)

        loop(group // head, one)

    def out_proj(_):
        context = ct[...].T
        bo, g1, c1 = prm[2:3, :], prm[3:4, :], prm[4:5, :]
        w = weight(OUT)

        def tile(i):
            r = span(i, 128)
            h1 = x[r, :].astype(F32) + (h2[r, :] + bo)
            centred = h1 - jnp.mean(h1, -1, keepdims=True)
            inverse = lax.rsqrt(jnp.mean(centred * centred, -1, keepdims=True) + 1e-06)
            normed = centred * inverse
            n1[r, :] = normed
            rs1[r, :] = inverse
            y1b[r, :] = (normed * g1 + c1).astype(BF)

        h2[...] = dot(context, w)
        loop(seq // 128, tile)

    def feed_up(j):
        def tile(t):
            cols = span(t, half)
            wide_cols = pl.ds(pl.multiple_of(j * model + t * half, half), half)
            u = dot(y1b[...], weight(IN + j, cols)) + prm[8 + j : 9 + j, cols]
            phi = 0.5 * (1.0 + lax.erf(u * SQRT_HALF))
            act[2 * j + t] = (u * phi).astype(BF).T.reshape(CS, 4, rows, seq)
            dact[:, wide_cols] = (phi + u * (jnp.exp(-0.5 * u * u) * INV_SQRT_TAU)).astype(BF)

        loop(2, tile)

    def act_rows(m):
        return act[:, :, m].reshape(-1, seq)

    def feed_down(m):
        w = wd[:, :, :, :, m].reshape(-1, model)
        part = dot(act_rows(m), w, TN)
        if m == 0:
            h2[...] = part + (n1[...] * prm[3:4, :] + prm[4:5, :]) + prm[5:6, :]
        else:
            h2[...] += part

    def vsum(row, value):
        vg[row : row + 1, :] += jnp.sum(value, axis=0, keepdims=True)

    def norm_back(dn, n, inverse):
        return (dn - jnp.mean(dn, -1, keepdims=True) - n * jnp.mean(dn * n, -1, keepdims=True)) * inverse

    def norm_two(_):
        g2, c2 = prm[6:7, :], prm[7:8, :]

        def tile(i):
            r = span(i, 128)
            h = h2[r, :]
            centred = h - jnp.mean(h, -1, keepdims=True)
            inverse = lax.rsqrt(jnp.mean(centred * centred, -1, keepdims=True) + 1e-06)
            n = centred * inverse
            dcx[r, :] = (n * g2 + c2).astype(BF)
            dy = cot[r, :].astype(F32)
            vsum(6, dy * n)
            vsum(7, dy)
            dh = norm_back(dy * g2, n, inverse)
            h2[r, :] = dh
            low = dh.astype(BF)
            dfb[r, :] = low
            vsum(5, low.astype(F32))

        loop(seq // 128, tile)
        store_out.append(store(dcx, out_hbm.at[0], 1))

    def grad_down(m):
        gd[m] = dot(act_rows(m), dfb[...]).astype(BF).reshape(gd.shape[1:])

    def grad_act(j):
        def tile(t):
            i = 2 * j + t
            cols = span(i, 2 * 4 * rows)
            zz = i // YS
            w = wd[zz // ZL, lax.rem(zz, ZL), lax.rem(i, YS)].reshape(2 * 4 * rows, model)
            du = (dot(dfb[...], w, NT) * dact[:, cols].astype(F32)).astype(BF)
            dact[:, cols] = du
            total = jnp.sum(du.astype(F32), axis=0, keepdims=True)
            vg[8 + j : 9 + j, t * half : (t + 1) * half] = total

        tile(0)
        tile(1)

    def grad_in(j):
        if j == 0:
            sent(*range(DOWN, CHUNKS))
            y1t[...] = y1b[...].T

        def tile(t):
            wide_cols = pl.ds(pl.multiple_of(j * model + t * 256, 256), 256)
            g = dot(y1t[...], dact[:, wide_cols]).astype(BF)
            wd[:, :, :, :, j, :, span(t, 256)] = g.reshape(ZH, ZL, YS, CS, rows, 256)

        loop(model // 256, tile)

    def grad_normed(j):
        h2[...] += dot(dact[:, j * model : (j + 1) * model], weight(IN + j), NT)

    def norm_one_back(_):
        g1 = prm[3:4, :]

        def tile(i):
            r = span(i, 128)
            dy, n = h2[r, :], n1[r, :]
            vsum(3, dy * n)
            vsum(4, dy)
            dh = norm_back(dy * g1, n, rs1[r, :])
            h2[r, :] = dh
            low = dh.astype(BF)
            dfb[r, :] = low
            vsum(2, low.astype(F32))

        loop(seq // 128, tile)

    def grad_out(_):
        g = dot(ct[...], dfb[...]).astype(BF)
        go[0] = g.reshape(ZH, ZL, YS, CS, rows, model)

    def grad_context(_):
        store_out.pop().wait()
        vt[...] = x[...].T
        dcx[...] = dot(dfb[...], weight(OUT), NT).astype(BF)

    def attend_back(g):
        def one(j):
            cols = span(j, pair)
            keys = pl.ds(pl.multiple_of(group + j * pair, pair), pair)
            vals = pl.ds(pl.multiple_of(2 * group + j * pair, pair), pair)
            place = pl.ds(pl.multiple_of(g * group + j * pair, pair), pair)
            lane = lax.broadcasted_iota(jnp.int32, (seq, pair), 1) // head
            dc = dcx[:, place]
            q, k, v = qkv[g, :, cols], qkv[g, :, keys], qkv[g, :, vals]
            kt = k.T
            dk, dv, dq = [], [], []
            for e in range(2):
                probs = pt[g, 2 * j + e]
                dv.append(dot(probs, dc))
                dp = dot(jnp.where(lane == e, v, jnp.zeros((), BF)), dc, NT)
                p32 = probs.astype(F32)
                t = p32 * dp
                ds = (t - p32 * jnp.sum(t, axis=0, keepdims=True)).astype(BF)
                dk.append(dot(ds, q))
                dq.append((dot(kt[e * head : (e + 1) * head, :], ds) * head**-0.5).astype(BF))
            dv = jnp.where(lane == 0, dv[0], dv[1]).astype(BF)
            dq = jnp.concatenate(dq, axis=0).T
            qkv[g, :, cols] = dq
            qkv[g, :, keys] = jnp.where(lane == 0, dk[0], dk[1]).astype(BF)
            qkv[g, :, vals] = dv
            vg[0:1, place] = jnp.sum(dq.astype(F32), axis=0, keepdims=True)
            vg[1:2, place] = jnp.sum(dv.astype(F32), axis=0, keepdims=True)

        loop(group // pair, one)

    def grad_qkv(g):
        if g == 0:
            sent(*range(IN, DOWN))

        def tile(t):
            cols = span(t, group)
            r = dot(vt[...], qkv[g, :, cols]).astype(BF)
            wa[IN + g, :, :, :, :, :, cols] = r.reshape(ZH, ZL, YS, CS, rows, group)

        loop(3, tile)

    def grad_x(g):
        before = h2 if g == 0 else n1
        n1[...] = before[...] + dot(qkv[g], weight(g), NT)
        if g == 2:
            store_x.append(store(n1, gtok_hbm.at[0], 2))

    last = len(SUMMED) - 1
    every = (ALL, ALL)
    mine = (zh, zl)

    def at_z(zz):
        return (zz // ZL, lax.rem(zz, ZL))

    def gpiece(k, zi, yy, cc, cols=ALL):
        if k < 4:
            return gd.at[(k, *zi, yy, cc, ALL, cols)]
        if k < 8:
            return wd.at[(*zi, yy, cc, k - 4, ALL, cols)]
        if k < 9:
            return go.at[(0, *zi, yy, cc, ALL, cols)]
        return wa.at[(IN + k - 9, *zi, yy, cc, ALL, cols)]

    def left(i):
        return pl.ds(SUMMED[i][1], SUMMED[i][2])

    def right(i):
        return pl.ds(half + SUMMED[i][1], SUMMED[i][2])

    def near(i):
        return left(i)

    def both(i):
        return (ALL,) if SUMMED[i][2] == half else (left(i), right(i))

    def r_core(i, cols):
        k = SUMMED[i][0]
        return remote(
            gpiece(k, every, ALL, 1 - c, cols), rcore.at[k % RING, :, :, :, :, cols], r_sent.at[i], rrc.at[i], sibling
        )

    def r_ya(i):
        k = SUMMED[i][0]
        src, dst = gpiece(k, every, 1 - y, c, left(i)), rya.at[k, :, :, :, near(i)]
        return remote(src, dst, r_sent.at[i], rry.at[i, 0], across_y)

    def r_xb(i):
        k = SUMMED[i][0]
        src, dst = gpiece(k, (ALL, 1 - parity(i)), ALL, c, right(i)), rxb.at[k, :, :, :, near(i)]
        return remote(src, dst, r_sent.at[i], rrx.at[i, 0], across_x)

    def r_za(i, dz):
        k = SUMMED[i][0]
        src, dst = gpiece(k, at_z(ahead(dz)), y, c, left(i)), rza.at[k, dz - 1, :, near(i)]
        return remote(src, dst, r_sent.at[i], rrz.at[i, 0], device(ahead(dz), y, c, px))

    def r_yb(i):
        k = SUMMED[i][0]
        src, dst = gpiece(k, (ALL, parity(i)), 1 - y, c, right(i)), ryb.at[k, :, :, near(i)]
        return remote(src, dst, r_sent.at[i], rry.at[i, 1], across_y)

    def r_xa(i):
        k = SUMMED[i][0]
        src, dst = gpiece(k, mine, y, c, left(i)), rxa.at[k, :, near(i)]
        return remote(src, dst, r_sent.at[i], rrx.at[i, 1], across_x)

    def r_zb(i, dz):
        k = SUMMED[i][0]
        src, dst = gpiece(k, at_z(ahead(dz)), y, c, right(i)), rzb.at[k, dz - 1, :, near(i)]
        return remote(src, dst, r_sent.at[i], rrz.at[i, 1], device(ahead(dz), y, c, px))

    def r_fb(i):
        k = SUMMED[i][0]
        return remote(
            gpiece(k, mine, y, c, right(i)), rfb.at[k, :, near(i)], r_sent.at[i], rrf.at[i], across_x
        )

    v_rc = remote(gv.at[:, :, :, 1 - c], rv_core, rv_sent, wrc, sibling)
    v_ry = remote(gv.at[:, :, 1 - y, c], rv_y, rv_sent, wry, across_y)
    v_rx = remote(gv.at[(*mine, y, c)], rv_x, rv_sent, wrx, across_x)

    def v_rz(dz):
        where = device(ahead(dz), y, c, px)
        return remote(gv.at[(*at_z(ahead(dz)), y, c)], rv_z.at[dz - 1], rv_sent, wrz, where)

    def parity(i):
        return lax.rem(px + i, 2)

    def same(i):
        return zl == parity(i)


    def add_into(ref, *others):
        if len(others) == 1:
            ref[...] += others[0][...]
            return
        total = ref[...].astype(F32)
        for other in others:
            total = total + other[...].astype(F32)
        ref[...] = total.astype(BF)

    def r0(i):
        for cols in both(i):
            r_core(i, cols).start()
        if i == last:
            v_rc.start()

    def r1(i):
        k, _, width = SUMMED[i]
        drained(wa.at[0, :, :, :, 0, :, pl.ds(0, 2 * width)], rrc.at[i])

        def add(zz):
            for cols in both(i):
                add_into(gpiece(k, at_z(zz), ALL, c, cols), rcore.at[(k % RING, *at_z(zz), ALL, ALL, cols)])

        loop(ZS, add)
        r_ya(i).start()
        r_xb(i).start()
        if i == last:
            v_rc.wait_recv()
            add_into(gv.at[:, :, :, c], rv_core)
            v_ry.start()

    def r2a(i):
        k = SUMMED[i][0]
        r_ya(i).wait_recv()
        add_into(gpiece(k, every, y, c, left(i)), rya.at[k, :, :, :, near(i)])
        for dz in (1, 2, 3):
            r_za(i, dz).start()
        if i == last:
            v_ry.wait_recv()
            add_into(gv.at[:, :, y, c], rv_y)
            for dz in (1, 2, 3):
                v_rz(dz).start()

    def r2b(i):
        k = SUMMED[i][0]
        r_xb(i).wait_recv()
        add_into(gpiece(k, (ALL, parity(i)), ALL, c, right(i)), rxb.at[k, :, :, :, near(i)])
        r_yb(i).start()

    def r3a(i):
        k = SUMMED[i][0]
        drained(rza.at[k, :, :, near(i)], rrz.at[i, 0])
        add_into(gpiece(k, mine, y, c, left(i)), *(rza.at[k, dz, :, near(i)] for dz in range(3)))
        r_xa(i).start()
        if i == last:
            drained(rv_z, wrz)
            add_into(gv.at[(*mine, y, c)], rv_z.at[0], rv_z.at[1], rv_z.at[2])
            v_rx.start()

    def r3b(i):
        k = SUMMED[i][0]
        r_yb(i).wait_recv()
        add_into(gpiece(k, (ALL, parity(i)), y, c, right(i)), ryb.at[k, :, :, near(i)])
        pl.when(same(i))(lambda: r_zb(i, 2).start())

        @pl.when(jnp.logical_not(same(i)))
        def _():
            r_zb(i, 1).start()
            r_zb(i, 3).start()

    def r4a(i):
        k = SUMMED[i][0]
        r_xa(i).wait_recv()
        fin[k, :, left(i)] = gpiece(k, mine, y, c, left(i))[...].astype(F32) + rxa[k, :, near(i)].astype(F32)
        if i == last:
            v_rx.wait_recv()
            store_vec.append(store(gv.at[(*mine, y, c)], gvec_hbm.at[0], 3))
            store_vec.append(store(rv_x, gvec_hbm.at[1], 4))
        settle(k)

    def r4b(i):
        k = SUMMED[i][0]

        @pl.when(same(i))
        def _():
            drained(rzb.at[k, :, :, near(i)], rrz.at[i, 1])
            piece = gpiece(k, mine, y, c, right(i))
            add_into(piece, *(rzb.at[k, dz, :, near(i)] for dz in range(3)))
            r_fb(i).start()
            fin[k, :, right(i)] = piece[...].astype(F32)

    def r5(i):
        k = SUMMED[i][0]

        @pl.when(jnp.logical_not(same(i)))
        def _():
            r_fb(i).wait_recv()
            fin[k, :, right(i)] = rfb[k, :, near(i)].astype(F32)

        settle(k)

    store_out, store_x, store_vec = [], [], []
    open_ends = {k: 2 * sum(part[0] == k for part in SUMMED) for k in range(CHUNKS)}

    def store(src, dst, i=0):
        cp = pltpu.make_async_copy(src, dst, s_store.at[i])
        cp.start()
        return cp

    def settle(k):
        open_ends[k] -= 1
        if open_ends[k]:
            return
        if k < 4:
            store(fin.at[k], gdown_hbm.at[pl.ds(k * rows, rows)])
        elif k < 8:
            store(fin.at[k], gin_hbm.at[:, pl.ds((k - 4) * model, model)])
        elif k < 9:
            store(fin.at[k], gout_hbm)
        else:
            for part in range(3):
                store(
                    fin.at[k, :, pl.ds(part * group, group)],
                    gqkv_hbm.at[:, pl.ds(part * model + (k - 9) * group, group)],
                )

    steps = (
        e1, eo, e2, e3, e4, e5,
        r0, r1, r2a, r2b, r3a, r3b,
        r4a, r4b, r5, spread_params, project, attend,
        out_proj, feed_up, feed_down, norm_two, grad_down, grad_act,
        grad_in, grad_normed, norm_one_back, grad_out, grad_context, attend_back,
        grad_qkv, gather_grads, grad_x,
    )
    vg[...] = jnp.zeros_like(vg)
    for step, i in ORDER:
        if step == S_PROJECT and i == 0:
            load_x.wait()
        if step == S_NORM2:
            load_cot.wait()
        steps[step](i)
    sent(*range(IN))
    vec_sent()
    for i, (_, _, width) in enumerate(SUMMED):
        drained(wa.at[0, :, :, :, :, :, pl.ds(0, 2 * width)], r_sent.at[i])
    drained(gv, rv_sent)
    drained(fin, s_store.at[0])
    for cp in (*store_vec, *store_x):
        cp.wait()


def place_kernel(cuts, *refs):
    count = len(cuts)
    sources, targets, held = refs[: count + 1], refs[count + 1 : 2 * count + 2], refs[2 * count + 2 : 3 * count + 3]
    vector, sem_in, sem_out = refs[3 * count + 3 :]
    first = pltpu.make_async_copy(sources[count], held[count], sem_in.at[sum(cuts)])
    first.start()
    moves = []
    for src, dst, mid, parts in zip(sources, targets, held, cuts):
        size = src.shape[-2] // parts
        for j in range(parts):
            at = (slice(None),) * (len(src.shape) - 2) + (pl.ds(j * size, size),)
            i = len(moves)
            moves.append(
                (
                    pltpu.make_async_copy(src.at[at], mid.at[at], sem_in.at[i]),
                    pltpu.make_async_copy(mid.at[at], dst.at[at], sem_out.at[i]),
                )
            )
    for into, _ in moves:
        into.start()
    first.wait()
    segment = vector.shape[0] // 3
    total = held[count][0].astype(F32) + held[count][1].astype(F32)
    vector[...] = jnp.concatenate([total[s : s + 1, 0:segment] for s in range(3)], axis=1).reshape(-1)
    last = pltpu.make_async_copy(vector, targets[count], sem_out.at[sum(cuts)])
    last.start()
    for into, out in moves:
        into.wait()
        out.start()
    for _, out in moves:
        out.wait()
    last.wait()


def fused_layer(tokens, lengths, w_qkv, w_out, w_in, w_down, norms_biases, cotangent):
    seq, model = tokens.shape[1:]
    rows = w_qkv.shape[0]
    hidden = w_in.shape[1]
    half = model // 2
    group = model // 3
    vm, dma = pltpu.VMEM, pltpu.SemaphoreType.DMA
    grid = (ZH, ZL, YS, CS)
    n, m, u = CHUNKS, len(GATHERED), len(SUMMED)
    scratch = [
        vm((DOWN, *grid, rows, model), BF),
        vm((*grid, 4, rows, model), BF),
        vm((*grid, 16, 256), BF),
        vm((4, *grid, rows, model), BF),
        vm((1, *grid, rows, model), BF),
        vm((*grid, 16, 256), BF),
        vm((RING, ZH, ZL, YS, rows, model), BF),
        vm((n, ZH, ZL, rows, half), BF),
        vm((n, ZH, YS, rows, half), BF),
        vm((n, 3, rows, half), BF),
        vm((n, ZH, rows, half), BF),
        vm((n, 3, rows, half), BF),
        vm((n, rows, half), BF),
        vm((n, rows, half), BF),
        vm((ZH, ZL, YS, 16, 256), BF),
        vm((ZH, ZL, 16, 256), BF),
        vm((3, 16, 256), BF),
        vm((16, 256), BF),
        vm((n, rows, model), F32),
        vm(norms_biases.shape, BF),
        vm((seq, model), BF),
        vm((seq, model), BF),
        vm((3, seq, model), BF),
        vm((model, seq), BF),
        vm((3, group // (model // HEADS), seq, seq), BF),
        vm((model, seq), BF),
        vm((seq, model), F32),
        vm((seq, model), BF),
        vm((model, seq), BF),
        vm((ZS * YS, CS, 4, rows, seq), BF),
        vm((seq, hidden), BF),
        vm((seq, model), F32),
        vm((seq, model), BF),
        vm((seq, model), BF),
        vm((seq, 1), F32),
        vm((16, model), F32),
        vm((16, model), F32),
        dma((n,)), dma((3,)), dma((5,)),
        dma((m,)), dma((m,)), dma((m,)), dma((m,)), dma((m,)), dma, dma, dma, dma,
        dma((u,)), dma, dma((u,)), dma((u, 2)), dma((u, 2)), dma((u, 2)), dma((u,)), dma, dma, dma, dma,
    ]
    hbm = pl.BlockSpec(memory_space=pl.ANY)
    shape = jax.ShapeDtypeStruct
    outs = pl.pallas_call(
        layer_kernel,
        out_shape=(
            shape(tokens.shape, BF),
            shape(tokens.shape, F32),
            shape(w_qkv.shape, F32),
            shape(w_out.shape, F32),
            shape(w_in.shape, F32),
            shape(w_down.shape, F32),
            shape((2, 16, 256), BF),
        ),
        in_specs=[hbm, pl.BlockSpec(memory_space=pltpu.SMEM)] + [hbm] * 6,
        out_specs=(hbm,) * 7,
        scratch_shapes=scratch,
        compiler_params=pltpu.CompilerParams(
            collective_id=0, has_side_effects=True, vmem_limit_bytes=64 << 20
        ),
        name="layer",
    )(tokens, lengths, w_qkv, w_out, w_in, w_down, norms_biases, cotangent)
    cuts = (1, 2, 1, 1, 1, 1)
    *placed, grad_vector = pl.pallas_call(
        functools.partial(place_kernel, cuts),
        out_shape=(*(shape(o.shape, o.dtype) for o in outs[:6]), shape(norms_biases.shape, F32)),
        in_specs=[hbm] * 7,
        out_specs=(hbm,) * 7,
        scratch_shapes=[vm(o.shape, o.dtype) for o in outs]
        + [vm(norms_biases.shape, F32), dma((sum(cuts) + 1,)), dma((sum(cuts) + 1,))],
        name="place",
    )(*outs)
    return (*placed, grad_vector)


def norm_rows(values, gain_row, shift_row):
    average = jnp.mean(values, -1, keepdims=True)
    centred = values - average
    spread = jnp.mean(centred * centred, -1, keepdims=True)
    return centred * lax.rsqrt(spread + 1e-06) * gain_row + shift_row


def gelu_exact(values):
    return jax.nn.gelu(values, approximate=False)


def column_sum(values):
    return jnp.sum(values.astype(jnp.float32), 0)


def split_vector(vector, model_width, hidden_width):
    segments = [
        vector[position * model_width : (position + 1) * model_width] for position in range(8)
    ]
    return segments + [vector[8 * model_width : 8 * model_width + hidden_width]]


def pair_blocks(projected, head_count):
    row_count = projected.shape[0]
    pair_count = head_count // 2
    pair_width = projected.shape[1] // (3 * pair_count)
    return projected.reshape(row_count, 3, pair_count, pair_width).transpose(2, 1, 0, 3)


def unpair_blocks(blocks):
    pair_count = blocks.shape[0]
    row_count = blocks.shape[2]
    pair_width = blocks.shape[3]
    return blocks.transpose(2, 1, 0, 3).reshape(row_count, 3 * pair_count * pair_width)


def pair_scores(head_block, usable, factor):
    row_count = head_block.shape[1]
    queries = head_block[0].reshape(row_count, 2, -1)
    key_rows = head_block[1].reshape(row_count, 2, -1)
    values = head_block[2].reshape(row_count, 2, -1)
    scores = (
        jnp.einsum("qhd,khd->hqk", queries, key_rows, preferred_element_type=jnp.float32) * factor
    )
    return (queries, key_rows, values, jnp.where(usable[None, None, :], scores, -1000000000.0))


def attention_forward(blocks, usable, factor):

    def one_pair(head_block):
        queries, key_rows, values, scores = pair_scores(head_block, usable, factor)
        highest = jnp.max(scores, -1, keepdims=True)
        raised = jnp.exp(scores - highest)
        summed = jnp.sum(raised, -1, keepdims=True)
        attend = (raised / summed).astype(jnp.bfloat16)
        context = jnp.einsum("hqk,khd->qhd", attend, values, preferred_element_type=jnp.float32)
        return (context.reshape(context.shape[0], -1), highest[..., 0] + jnp.log(summed[..., 0]))

    return lax.map(one_pair, blocks)


def attention_backward(blocks, grad_pairs, log_totals, usable, factor):

    def one_pair(pair_inputs):
        head_block, grad_context, log_total = pair_inputs
        queries, key_rows, values, scores = pair_scores(head_block, usable, factor)
        attend = jnp.exp(scores - log_total[..., None])
        row_count = grad_context.shape[0]
        grad_heads = grad_context.reshape(row_count, 2, -1)
        grad_values = jnp.einsum(
            "hqk,qhd->khd",
            attend.astype(jnp.bfloat16),
            grad_heads,
            preferred_element_type=jnp.float32,
        )
        grad_attend = jnp.einsum(
            "qhd,khd->hqk", grad_heads, values, preferred_element_type=jnp.float32
        )
        grad_scores = attend * (grad_attend - jnp.sum(attend * grad_attend, -1, keepdims=True))
        grad_low = grad_scores.astype(jnp.bfloat16)
        grad_queries = (
            jnp.einsum("hqk,khd->qhd", grad_low, key_rows, preferred_element_type=jnp.float32)
            * factor
        )
        grad_keys = (
            jnp.einsum("hqk,qhd->khd", grad_low, queries, preferred_element_type=jnp.float32)
            * factor
        )
        return jnp.stack(
            [
                grad_queries.reshape(row_count, -1),
                grad_keys.reshape(row_count, -1),
                grad_values.reshape(row_count, -1),
            ]
        )

    return lax.map(one_pair, (blocks, grad_pairs, log_totals))


def layer_forward(inputs, length, weights):
    w_qkv, w_out, w_in, w_down, vector = weights
    row_count, model_width = inputs.shape
    hidden_width = w_in.shape[1]
    params = split_vector(vector.astype(jnp.float32), model_width, hidden_width)
    joined_bias = jnp.concatenate([params[0], jnp.zeros((model_width,), jnp.float32), params[1]])
    projected = (jnp.dot(inputs, w_qkv, preferred_element_type=jnp.float32) + joined_bias).astype(
        jnp.bfloat16
    )
    blocks = pair_blocks(projected, HEADS)
    usable = jnp.arange(row_count) < length
    factor = (model_width // HEADS) ** (-0.5)
    context_pairs, log_totals = attention_forward(blocks, usable, factor)
    context = context_pairs.transpose(1, 0, 2).reshape(row_count, model_width).astype(jnp.bfloat16)
    resid_one = inputs.astype(jnp.float32) + (
        jnp.dot(context, w_out, preferred_element_type=jnp.float32) + params[2]
    )
    normed_one = norm_rows(resid_one, params[3], params[4])
    normed_low = normed_one.astype(jnp.bfloat16)
    pre_act = jnp.dot(normed_low, w_in, preferred_element_type=jnp.float32) + params[8]
    activated = gelu_exact(pre_act).astype(jnp.bfloat16)
    resid_two = normed_one + (
        jnp.dot(activated, w_down, preferred_element_type=jnp.float32) + params[5]
    )
    result = norm_rows(resid_two, params[6], params[7])
    saved = (
        params,
        blocks,
        usable,
        factor,
        log_totals,
        context,
        resid_one,
        normed_low,
        pre_act,
        activated,
        resid_two,
    )
    return (result, saved)


def layer_backward(inputs, length, grad_result, weights):
    w_qkv, w_out, w_in, w_down, vector = weights
    unused_result, saved = layer_forward(inputs, length, weights)
    (
        params,
        blocks,
        usable,
        factor,
        log_totals,
        context,
        resid_one,
        normed_low,
        pre_act,
        activated,
        resid_two,
    ) = saved
    row_count, model_width = inputs.shape
    unused_two, norm_two_back = jax.vjp(norm_rows, resid_two, params[6], params[7])
    grad_two, grad_gain_two, grad_shift_two = norm_two_back(grad_result)
    grad_feed = grad_two.astype(jnp.bfloat16)
    grad_down = jnp.einsum("sf,sd->fd", activated, grad_feed, preferred_element_type=jnp.float32)
    grad_act = jnp.einsum("sd,fd->sf", grad_feed, w_down, preferred_element_type=jnp.float32)
    unused_act, gelu_back = jax.vjp(gelu_exact, pre_act)
    grad_pre = gelu_back(grad_act)[0].astype(jnp.bfloat16)
    grad_in = jnp.einsum("sd,sf->df", normed_low, grad_pre, preferred_element_type=jnp.float32)
    grad_normed = grad_two + jnp.einsum(
        "sf,df->sd", grad_pre, w_in, preferred_element_type=jnp.float32
    )
    unused_one, norm_one_back = jax.vjp(norm_rows, resid_one, params[3], params[4])
    grad_one, grad_gain_one, grad_shift_one = norm_one_back(grad_normed)
    grad_attended = grad_one.astype(jnp.bfloat16)
    grad_out = jnp.einsum("sd,se->de", context, grad_attended, preferred_element_type=jnp.float32)
    grad_context = jnp.einsum(
        "se,de->sd", grad_attended, w_out, preferred_element_type=jnp.float32
    ).astype(jnp.bfloat16)
    grad_pairs = grad_context.reshape(row_count, HEADS // 2, -1).transpose(1, 0, 2)
    grad_blocks = attention_backward(blocks, grad_pairs, log_totals, usable, factor)
    grad_projected = unpair_blocks(grad_blocks).astype(jnp.bfloat16)
    grad_qkv = jnp.einsum("sd,se->de", inputs, grad_projected, preferred_element_type=jnp.float32)
    grad_inputs = grad_one + jnp.einsum(
        "se,de->sd", grad_projected, w_qkv, preferred_element_type=jnp.float32
    )
    projected_sums = column_sum(grad_projected)
    grad_vector = jnp.concatenate(
        [
            projected_sums[:model_width],
            projected_sums[2 * model_width :],
            column_sum(grad_attended),
            grad_gain_one,
            grad_shift_one,
            column_sum(grad_feed),
            grad_gain_two,
            grad_shift_two,
            column_sum(grad_pre),
        ]
    )
    return (grad_inputs, (grad_qkv, grad_out, grad_in, grad_down, grad_vector))


def local(tokens, lengths, w_qkv, w_out, w_in, w_down, norms_biases, cotangent):
    weights = (
        lax.all_gather(w_qkv, "wide", axis=0, tiled=True),
        lax.all_gather(w_out, "wide", axis=0, tiled=True),
        lax.all_gather(w_in, "wide", axis=0, tiled=True),
        lax.all_gather(w_down, "wide", axis=0, tiled=True),
        lax.all_gather(norms_biases, "wide", axis=0, tiled=True),
    )

    def forward_one(sequence):
        return layer_forward(sequence[0], sequence[1], weights)[0].astype(jnp.bfloat16)

    output = lax.map(forward_one, (tokens, lengths))
    second_copy = (
        lax.all_gather(w_qkv, "wide", axis=0, tiled=True),
        lax.all_gather(w_out, "wide", axis=0, tiled=True),
        lax.all_gather(w_in, "wide", axis=0, tiled=True),
        lax.all_gather(w_down, "wide", axis=0, tiled=True),
        lax.all_gather(norms_biases, "wide", axis=0, tiled=True),
    )
    running = tuple((jnp.zeros(member.shape, jnp.float32) for member in second_copy))

    def advance(totals, sequence):
        grad_inputs, gradients = layer_backward(
            sequence[0], sequence[1], sequence[2].astype(jnp.float32), second_copy
        )
        return (jax.tree.map(jnp.add, totals, gradients), grad_inputs)

    totals, grad_tokens = lax.scan(advance, running, (tokens, lengths, cotangent))
    owned_rows = (
        lax.psum_scatter(
            totals[0].astype(jnp.bfloat16), "wide", scatter_dimension=0, tiled=True
        ).astype(jnp.float32),
        lax.psum_scatter(
            totals[1].astype(jnp.bfloat16), "wide", scatter_dimension=0, tiled=True
        ).astype(jnp.float32),
        lax.psum_scatter(
            totals[2].astype(jnp.bfloat16), "wide", scatter_dimension=0, tiled=True
        ).astype(jnp.float32),
        lax.psum_scatter(
            totals[3].astype(jnp.bfloat16), "wide", scatter_dimension=0, tiled=True
        ).astype(jnp.float32),
        lax.psum_scatter(
            totals[4].astype(jnp.bfloat16), "wide", scatter_dimension=0, tiled=True
        ).astype(jnp.float32),
    )
    summed_all = (
        lax.psum(owned_rows[0].astype(jnp.bfloat16), "narrow").astype(jnp.float32),
        lax.psum(owned_rows[1].astype(jnp.bfloat16), "narrow").astype(jnp.float32),
        lax.psum(owned_rows[2].astype(jnp.bfloat16), "narrow").astype(jnp.float32),
        lax.psum(owned_rows[3].astype(jnp.bfloat16), "narrow").astype(jnp.float32),
        lax.psum(owned_rows[4].astype(jnp.bfloat16), "narrow").astype(jnp.float32),
    )
    return (
        output,
        grad_tokens,
        summed_all[0],
        summed_all[1],
        summed_all[2],
        summed_all[3],
        summed_all[4],
    )


def solution(mesh):
    in_specs = (
        P(("wide", "narrow"), None, None),
        P(("wide", "narrow")),
        P("wide", None),
        P("wide", None),
        P("wide", None),
        P("wide", None),
        P("wide"),
        P(("wide", "narrow"), None, None),
    )
    out_specs = (
        P(("wide", "narrow"), None, None),
        P(("wide", "narrow"), None, None),
        P("wide", None),
        P("wide", None),
        P("wide", None),
        P("wide", None),
        P("wide"),
    )
    chips = (ZS * YS * CS, 2)
    fused = tuple(mesh.shape[axis] for axis in ("wide", "narrow")) == chips
    step = fused_layer if fused else local
    return jax.shard_map(step, mesh=mesh, in_specs=in_specs, out_specs=out_specs, check_vma=False)
```

```python
import functools

import jax
import jax.numpy as jnp
import numpy as np
from jax import lax
from jax.experimental import pallas as pl
from jax.experimental.pallas import tpu as pltpu
from jax.sharding import PartitionSpec as P

HEADS = 12
MESH = pl.DeviceIdType.MESH
BF = jnp.bfloat16
F32 = jnp.float32
NT = (((1,), (1,)), ((), ()))
TN = (((0,), (0,)), ((), ()))
ZH, ZL, YS, CS = 2, 2, 2, 2
ZS = ZH * ZL
QKV, OUT, IN, DOWN, CHUNKS = 0, 3, 4, 8, 12
RING = 8
(
    S_E1, S_EO, S_E2, S_E3, S_E4, S_E5, S_R0, S_R1, S_R2A, S_R2B, S_R3A,
    S_R3B, S_R4A, S_R4B, S_R5, S_SPREAD, S_PROJECT, S_ATTEND, S_OUT, S_UP, S_DOWN, S_NORM2,
    S_GDOWN, S_GACT, S_GIN, S_GNORM, S_NORM1, S_GOUT, S_GCTX, S_ABACK, S_GQKV, S_GGRADS, S_GX,
) = range(33)
GATHERED = (
    (0, 0, 384), (0, 384, 384), (1, 0, 384), (1, 384, 384), (2, 0, 384), (2, 384, 384), (3, 0, 384), (3, 384, 384),
    (4, 0, 384), (4, 384, 384), (5, 0, 384), (5, 384, 384), (6, 0, 384), (6, 384, 384), (7, 0, 384), (7, 384, 384),
    (8, 0, 384), (8, 384, 384), (9, 0, 384), (9, 384, 384), (10, 0, 384), (10, 384, 384), (11, 0, 384), (11, 384, 384),
)
SUMMED = (
    (0, 0, 128), (0, 128, 128), (0, 256, 128), (1, 0, 384), (2, 0, 384), (3, 0, 384), (4, 0, 384), (5, 0, 384),
    (6, 0, 384), (7, 0, 384), (8, 0, 384), (9, 0, 384), (10, 0, 384), (11, 0, 384),
)
ORDER = (
    (S_E1, 0), (S_EO, 0), (S_E1, 1), (S_EO, 1), (S_E1, 2), (S_EO, 2), (S_EO, 3), (S_EO, 4), (S_EO, 5), (S_E1, 3),
    (S_E2, 0), (S_EO, 6), (S_E1, 4), (S_E2, 1), (S_EO, 7), (S_E1, 5), (S_E2, 2), (S_EO, 8), (S_E3, 0), (S_E1, 6),
    (S_E2, 3), (S_EO, 9), (S_E3, 1), (S_E1, 7), (S_E2, 4), (S_EO, 10), (S_E3, 2), (S_E4, 0), (S_E1, 8), (S_E2, 5),
    (S_EO, 11), (S_E3, 3), (S_E4, 1), (S_E5, 0), (S_E1, 9), (S_E2, 6), (S_EO, 12), (S_E3, 4), (S_E4, 2), (S_E5, 1),
    (S_SPREAD, 0), (S_PROJECT, 0), (S_E1, 10), (S_E2, 7), (S_EO, 13), (S_E3, 5), (S_E4, 3), (S_E5, 2), (S_ATTEND, 0), (S_E1, 11),
    (S_E2, 8), (S_EO, 14), (S_E3, 6), (S_E4, 4), (S_E5, 3), (S_ATTEND, 1), (S_E1, 12), (S_E2, 9), (S_EO, 15), (S_E3, 7),
    (S_E4, 5), (S_E5, 4), (S_PROJECT, 1), (S_E1, 13), (S_E2, 10), (S_EO, 16), (S_E3, 8), (S_E4, 6), (S_E5, 5), (S_ATTEND, 2),
    (S_E1, 14), (S_E2, 11), (S_EO, 17), (S_E3, 9), (S_E4, 7), (S_E5, 6), (S_ATTEND, 3), (S_E1, 15), (S_E2, 12), (S_EO, 18),
    (S_E3, 10), (S_E4, 8), (S_E5, 7), (S_PROJECT, 2), (S_E1, 16), (S_E2, 13), (S_EO, 19), (S_E3, 11), (S_E4, 9), (S_E5, 8),
    (S_ATTEND, 4), (S_E1, 17), (S_E2, 14), (S_EO, 20), (S_E3, 12), (S_E4, 10), (S_E5, 9), (S_ATTEND, 5), (S_E1, 18), (S_E2, 15),
    (S_EO, 21), (S_E3, 13), (S_E4, 11), (S_E5, 10), (S_OUT, 0), (S_E1, 19), (S_E2, 16), (S_EO, 22), (S_E3, 14), (S_E4, 12),
    (S_E5, 11), (S_UP, 0), (S_E1, 20), (S_E2, 17), (S_EO, 23), (S_E3, 15), (S_E4, 13), (S_E5, 12), (S_UP, 1), (S_E1, 21),
    (S_E2, 18), (S_E3, 16), (S_E4, 14), (S_E5, 13), (S_UP, 2), (S_E1, 22), (S_E2, 19), (S_E3, 17), (S_E4, 15), (S_E5, 14),
    (S_E1, 23), (S_E2, 20), (S_E3, 18), (S_E4, 16), (S_E5, 15), (S_UP, 3), (S_E2, 21), (S_E3, 19), (S_E4, 17), (S_E5, 16),
    (S_E2, 22), (S_E3, 20), (S_E4, 18), (S_E5, 17), (S_DOWN, 0), (S_E2, 23), (S_E3, 21), (S_E4, 19), (S_E5, 18), (S_E3, 22),
    (S_E4, 20), (S_E5, 19), (S_DOWN, 1), (S_E3, 23), (S_E4, 21), (S_E5, 20), (S_E4, 22), (S_E5, 21), (S_DOWN, 2), (S_E4, 23),
    (S_E5, 22), (S_E5, 23), (S_DOWN, 3), (S_NORM2, 0), (S_GDOWN, 0), (S_R0, 0), (S_R0, 1), (S_GDOWN, 1), (S_R0, 2), (S_R0, 3),
    (S_R1, 0), (S_GDOWN, 2), (S_R1, 1), (S_R0, 4), (S_R1, 2), (S_GACT, 0), (S_R1, 3), (S_GDOWN, 3), (S_R1, 4), (S_GACT, 1),
    (S_R2A, 1), (S_GACT, 2), (S_R2A, 2), (S_GACT, 3), (S_R0, 5), (S_R2A, 0), (S_GIN, 0), (S_R2A, 3), (S_R2B, 1), (S_R2B, 2),
    (S_GNORM, 0), (S_R1, 5), (S_GIN, 1), (S_R0, 6), (S_R2A, 4), (S_GNORM, 1), (S_R2B, 3), (S_R3B, 2), (S_R3B, 1), (S_GIN, 2),
    (S_R1, 6), (S_R0, 7), (S_GNORM, 2), (S_R2A, 5), (S_R2B, 4), (S_GIN, 3), (S_R0, 8), (S_R1, 7), (S_R3B, 3), (S_R2B, 5),
    (S_R3A, 4), (S_GNORM, 3), (S_R1, 8), (S_R0, 9), (S_R2B, 6), (S_R2A, 6), (S_NORM1, 0), (S_GOUT, 0), (S_R0, 10), (S_R3B, 4),
    (S_GCTX, 0), (S_R2B, 7), (S_R1, 9), (S_R1, 10), (S_R2A, 7), (S_ABACK, 0), (S_R2B, 8), (S_R3B, 5), (S_GQKV, 0), (S_R0, 11),
    (S_R2A, 8), (S_ABACK, 1), (S_R3B, 6), (S_R3A, 1), (S_R1, 11), (S_R3B, 7), (S_R4A, 4), (S_R3A, 6), (S_GQKV, 1), (S_R3A, 3),
    (S_R2A, 9), (S_R0, 12), (S_ABACK, 2), (S_R2A, 10), (S_R2B, 11), (S_R1, 12), (S_GX, 0), (S_R2B, 9), (S_R3B, 8), (S_GQKV, 2),
    (S_R3A, 2), (S_GGRADS, 0), (S_R2A, 11), (S_R0, 13), (S_R3A, 7), (S_R4B, 6), (S_R4B, 4), (S_R4B, 1), (S_R1, 13), (S_R4A, 3),
    (S_R4A, 1), (S_R3B, 11), (S_R2B, 0), (S_R2A, 12), (S_R3A, 8), (S_R4B, 5), (S_GX, 1), (S_R4A, 2), (S_R4B, 8), (S_R3A, 9),
    (S_R4A, 6), (S_R3B, 9), (S_R2B, 12), (S_R2B, 13), (S_GX, 2), (S_R3A, 0), (S_R2A, 13), (S_R3A, 5), (S_R2B, 10), (S_R3A, 11),
    (S_R4B, 2), (S_R3A, 10), (S_R3B, 12), (S_R5, 5), (S_R4B, 11), (S_R4B, 7), (S_R4B, 3), (S_R3B, 13), (S_R4A, 9), (S_R3B, 10),
    (S_R3A, 12), (S_R3B, 0), (S_R5, 8), (S_R4A, 10), (S_R4A, 5), (S_R4A, 11), (S_R4A, 8), (S_R5, 2), (S_R5, 11), (S_R4B, 12),
    (S_R5, 3), (S_R4B, 9), (S_R4A, 7), (S_R3A, 13), (S_R4B, 13), (S_R4A, 0), (S_R5, 6), (S_R4B, 10), (S_R5, 12), (S_R4B, 0),
    (S_R4A, 12), (S_R5, 1), (S_R5, 7), (S_R4A, 13), (S_R5, 9), (S_R5, 13), (S_R5, 4), (S_R5, 10), (S_R5, 0),
)
SQRT_HALF = 0.7071067811865476
INV_SQRT_TAU = 0.3989422804014327


def dot(left, right, dims=None):
    if dims is None:
        return jnp.dot(left, right, preferred_element_type=F32)
    return lax.dot_general(left, right, dims, preferred_element_type=F32)


def loop(count, body):
    def step(index, carry):
        body(index)
        return carry

    lax.fori_loop(0, count, step, 0)


def span(index, size):
    return pl.ds(pl.multiple_of(index * size, size), size)


def layer_kernel(
    x_hbm, len_ref, wqkv_hbm, wout_hbm, win_hbm, wdown_hbm, vec_hbm, cot_hbm,
    out_hbm, gtok_hbm, gqkv_hbm, gout_hbm, gin_hbm, gdown_hbm, gvec_hbm,
    wa, wd, vb, gd, go, gv, rcore, rya, rxb, rza, ryb, rzb, rxa, rfb, rv_core, rv_y, rv_z, rv_x, fin, vec,
    x, cot, qkv, vt, pt, ct, n1, y1b, y1t, act, dact, h2, dfb, dcx, rs1, prm, vg,
    s_load, s_io, s_store,
    g_sent, grz, gry, grx, grc, v_sent, vrz, vry, vrc,
    r_sent, rv_sent, rrc, rry, rrx, rrz, rrf, wrc, wry, wrz, wrx,
):
    seq, model = x.shape
    rows = wa.shape[-2]
    hidden = dact.shape[1]
    pair = 2 * (model // HEADS)
    head = model // HEADS
    group = model // 3
    half = model // 2
    wide = lax.axis_index("wide")
    px = lax.axis_index("narrow")
    c = lax.rem(wide, CS)
    y = lax.rem(wide // CS, YS)
    z = wide // (CS * YS)
    zl = lax.rem(z, ZL)
    zh = z // ZL

    def device(zz, yy, cc, xx):
        return ((zz * YS + yy) * CS + cc, xx)

    sibling = device(z, y, 1 - c, px)
    across_y = device(z, 1 - y, c, px)
    across_x = device(z, y, c, 1 - px)

    def ahead(dz):
        return lax.rem(z + dz, ZS)

    def behind(dz):
        return lax.rem(z + ZS - dz, ZS)

    def remote(src, dst, send, recv, where):
        return pltpu.make_async_remote_copy(
            src_ref=src, dst_ref=dst, send_sem=send, recv_sem=recv, device_id=where, device_id_type=MESH
        )

    ALL = slice(None)

    def drained(ref, sem):
        pltpu.make_async_copy(ref, ref, sem).wait()

    def rows_of(count, cols):
        return x.at[pl.ds(0, count), pl.ds(0, cols)]

    def load(src, dst, sem):
        cp = pltpu.make_async_copy(src, dst, sem)
        cp.start()
        return cp

    load_vec = load(vec_hbm, vec, s_io.at[2])
    load_x = load(x_hbm.at[0], x, s_io.at[0])
    for k in range(CHUNKS):
        if k < OUT:
            for part in range(3):
                load(
                    wqkv_hbm.at[:, pl.ds(part * model + k * group, group)],
                    wa.at[k, zh, zl, y, c, :, pl.ds(part * group, group)],
                    s_load.at[k],
                )
        elif k < IN:
            load(wout_hbm, wa.at[k, zh, zl, y, c], s_load.at[k])
        elif k < DOWN:
            load(win_hbm.at[:, pl.ds((k - IN) * model, model)], wa.at[k, zh, zl, y, c], s_load.at[k])
        else:
            load(wdown_hbm.at[pl.ds((k - DOWN) * rows, rows)], wd.at[zh, zl, y, c, k - DOWN], s_load.at[k])
    load_cot = load(cot_hbm.at[0], cot, s_io.at[1])

    barrier = pltpu.get_barrier_semaphore()
    for where in (sibling, across_y, across_x, *(device(ahead(dz), y, c, px) for dz in (1, 2, 3))):
        pl.semaphore_signal(barrier, inc=1, device_id=where, device_id_type=MESH)
    pl.semaphore_wait(barrier, 6)

    third = rows // 3
    kept = pl.ds(pl.multiple_of(px * third, third), 2 * third)
    given = pl.ds(pl.multiple_of(px * 2 * third, third), third)
    taken = pl.ds(pl.multiple_of((1 - px) * 2 * third, third), third)

    def wcut(i, zz, yy, cc, r=ALL):
        k, first, count = GATHERED[i]
        cols = pl.ds(first, count)
        zi = (ALL, ALL) if zz is None else (zz // ZL, lax.rem(zz, ZL))
        if k < DOWN:
            return wa.at[(k, *zi, yy, cc, r, cols)]
        return wd.at[(*zi, yy, cc, k - DOWN, r, cols)]

    def g_z(i, dz, source):
        piece = wcut(i, source, y, c, kept)
        return remote(piece, piece, g_sent.at[i], grz.at[i], device(ahead(dz), y, c, px))

    def g_y(i, dz, column):
        piece = wcut(i, behind(dz), column, c, kept)
        return remote(piece, piece, g_sent.at[i], gry.at[i], across_y)

    def g_x1(i, dz, r):
        piece = wcut(i, behind(dz), y, c, r)
        return remote(piece, piece, g_sent.at[i], grx.at[i], across_x)

    def g_x2(i, r):
        piece = wcut(i, None, 1 - y, c, r)
        return remote(piece, piece, g_sent.at[i], grx.at[i], across_x)

    def g_core(i, core):
        piece = wcut(i, None, ALL, core)
        return remote(piece, piece, g_sent.at[i], grc.at[i], sibling)

    def v_z(dz, source):
        piece = vb.at[source // ZL, lax.rem(source, ZL), y, c]
        return remote(piece, piece, v_sent, vrz, device(ahead(dz), y, c, px))

    def v_y(column):
        piece = vb.at[:, :, column, c]
        return remote(piece, piece, v_sent, vry, across_y)

    def v_core(core):
        piece = vb.at[:, :, :, core]
        return remote(piece, piece, v_sent, vrc, sibling)

    loaded = set()

    def own(k):
        if k not in loaded:
            loaded.add(k)
            drained(rows_of(rows, model), s_load.at[k])

    def e1(i):
        own(GATHERED[i][0])
        for dz in (1, 2, 3):
            g_z(i, dz, z).start()
        if i == 1:
            load_vec.wait()
            segment = vec.shape[0] // 3
            row = vec[...].astype(F32).reshape(1, -1)
            vb[zh, zl, y, c] = jnp.zeros(vb.shape[-2:], BF)
            for s in range(3):
                vb[zh, zl, y, c, s : s + 1, 0:segment] = row[:, s * segment : (s + 1) * segment].astype(BF)
            for dz in (1, 2, 3):
                v_z(dz, z).start()

    def eo(i):
        own(GATHERED[i][0])
        g_y(i, 0, y).start()

    def e2(i):
        if i == 1:
            drained(rv_z, vrz)
            v_y(y).start()
        drained(rows_of(3 * 2 * third, GATHERED[i][2]), grz.at[i])
        for dz in (1, 2, 3):
            g_y(i, dz, y).start()
            g_x1(i, dz, given).start()

    def e3(i):
        if i == 1:
            v_y(1 - y).wait_recv()
            v_core(c).start()
        drained(rows_of(ZS * 2 * third, GATHERED[i][2]), gry.at[i])
        g_x2(i, given).start()

    def e4(i):
        drained(rows_of((ZS + ZS - 1) * third, GATHERED[i][2]), grx.at[i])
        g_core(i, c).start()

    def e5(i):
        if i == 1:
            v_core(1 - c).wait_recv()
        g_core(i, 1 - c).wait_recv()

    def sent(*chunks):
        count = (3 + ZS) * 2 * third + (2 * ZS - 1) * third + ZS * YS * rows
        for i, (k, _, cols) in enumerate(GATHERED):
            if k in chunks:
                drained(qkv.at[:, pl.ds(0, count // 3), pl.ds(0, cols)], g_sent.at[i])

    def vec_sent():
        drained(x.at[pl.ds(0, 80)], v_sent)

    def place_matrix(k, lanes):
        i = lax.broadcasted_iota(jnp.int32, (lanes, model), 0)
        j = lax.broadcasted_iota(jnp.int32, (lanes, model), 1)
        quarter = model // 4
        return jnp.where((i < quarter) & (j == i + k * quarter), 1.0, 0.0).astype(BF)

    def pick_matrix(k, count, total, slot):
        b = lax.broadcasted_iota(jnp.int32, (count, total), 0)
        r = lax.broadcasted_iota(jnp.int32, (count, total), 1)
        segment = 4 * b + k
        return jnp.where((r == slot * (segment // 3) + lax.rem(segment, 3)) & (b < 12), 1.0, 0.0).astype(BF)

    def spread_params(_):
        lanes = vb.shape[-1]
        segments = vb[...].reshape(-1, lanes)
        total = None
        for k in range(4):
            picked = dot(pick_matrix(k, 16, segments.shape[0], vb.shape[-2]), segments).astype(BF)
            part = dot(picked, place_matrix(k, lanes))
            total = part if total is None else total + part
        prm[...] = total

    def gather_grads(_):
        lanes = gv.shape[-1]
        low = vg[...].astype(BF)
        total = None
        for k in range(4):
            cut = dot(low, place_matrix(k, lanes), NT).astype(BF)
            part = dot(pick_matrix(k, 16, 16 * gv.shape[-2], gv.shape[-2]), cut, TN)
            total = part if total is None else total + part
        gv[...] = total.astype(BF).reshape(gv.shape)

    def weight(k, cols=ALL):
        block = wa[k, :, :, :, :, :, cols]
        return block.reshape(-1, block.shape[-1])

    def project(g):
        grouped = span(g, group)

        def tile(part):
            cols = span(part, group)
            bias = jnp.where(part == 0, prm[0:1, grouped], jnp.where(part == 2, prm[1:2, grouped], 0.0))
            low = (dot(x[...], weight(g, cols)) + bias).astype(BF)
            qkv[g, :, cols] = low * jnp.where(part == 0, head**-0.5, 1.0).astype(BF)

        loop(3, tile)
        vt[grouped, :] = qkv[g, :, 2 * group :].T

    def attend(half_group):
        g, first = half_group // 2, half_group % 2 * 2
        length = len_ref[0]

        def one(i):
            h = first + i
            cols = span(h // 2, pair)
            keys = pl.ds(pl.multiple_of(group + (h // 2) * pair, pair), pair)
            lane = lax.broadcasted_iota(jnp.int32, (seq, pair), 1) // head
            masked = jnp.where(lane == lax.rem(h, 2), qkv[g, :, keys], jnp.zeros((), BF))
            scores = dot(masked, qkv[g, :, cols], NT)
            key = lax.broadcasted_iota(jnp.int32, scores.shape, 0)
            scores = jnp.where(key < length, scores, -1000000000.0)
            raised = jnp.exp(scores - jnp.max(scores, axis=0, keepdims=True))
            probs = (raised * (1.0 / jnp.sum(raised, axis=0, keepdims=True))).astype(BF)
            pt[g, h] = probs
            mine = pl.ds(pl.multiple_of(g * group + h * head, head), head)
            ct[mine, :] = dot(vt[mine, :], probs).astype(BF)

        loop(2, one)

    def out_proj(_):
        context = ct[...].T
        bo, g1, c1 = prm[2:3, :], prm[3:4, :], prm[4:5, :]
        w = weight(OUT)

        def tile(i):
            r = span(i, 128)
            h1 = x[r, :].astype(F32) + (h2[r, :] + bo)
            centred = h1 - jnp.mean(h1, -1, keepdims=True)
            inverse = lax.rsqrt(jnp.mean(centred * centred, -1, keepdims=True) + 1e-06)
            normed = centred * inverse
            n1[r, :] = normed
            rs1[r, :] = inverse
            y1b[r, :] = (normed * g1 + c1).astype(BF)

        h2[...] = dot(context, w)
        loop(seq // 128, tile)

    def feed_up(j):
        def tile(t):
            cols = span(t, half)
            wide_cols = pl.ds(pl.multiple_of(j * model + t * half, half), half)
            u = dot(y1b[...], weight(IN + j, cols)) + prm[8 + j : 9 + j, cols]
            phi = 0.5 * (1.0 + lax.erf(u * SQRT_HALF))
            act[2 * j + t] = (u * phi).astype(BF).T.reshape(CS, 4, rows, seq)
            dact[:, wide_cols] = (phi + u * (jnp.exp(-0.5 * u * u) * INV_SQRT_TAU)).astype(BF)

        loop(2, tile)

    def act_rows(m):
        return act[:, :, m].reshape(-1, seq)

    def feed_down(m):
        w = wd[:, :, :, :, m].reshape(-1, model)
        part = dot(act_rows(m), w, TN)
        if m == 0:
            h2[...] = part + (n1[...] * prm[3:4, :] + prm[4:5, :]) + prm[5:6, :]
        else:
            h2[...] += part

    def vsum(row, value):
        vg[row : row + 1, :] += jnp.sum(value, axis=0, keepdims=True)

    def norm_back(dn, n, inverse):
        return (dn - jnp.mean(dn, -1, keepdims=True) - n * jnp.mean(dn * n, -1, keepdims=True)) * inverse

    def norm_two(_):
        g2, c2 = prm[6:7, :], prm[7:8, :]

        def tile(i):
            r = span(i, 128)
            h = h2[r, :]
            centred = h - jnp.mean(h, -1, keepdims=True)
            inverse = lax.rsqrt(jnp.mean(centred * centred, -1, keepdims=True) + 1e-06)
            n = centred * inverse
            dcx[r, :] = (n * g2 + c2).astype(BF)
            dy = cot[r, :].astype(F32)
            vsum(6, dy * n)
            vsum(7, dy)
            dh = norm_back(dy * g2, n, inverse)
            h2[r, :] = dh
            low = dh.astype(BF)
            dfb[r, :] = low
            vsum(5, low.astype(F32))

        loop(seq // 128, tile)
        store_out.append(store(dcx, out_hbm.at[0], 1))

    def grad_down(m):
        gd[m] = dot(act_rows(m), dfb[...]).astype(BF).reshape(gd.shape[1:])

    def grad_act(j):
        def tile(t):
            i = 2 * j + t
            cols = span(i, 2 * 4 * rows)
            zz = i // YS
            w = wd[zz // ZL, lax.rem(zz, ZL), lax.rem(i, YS)].reshape(2 * 4 * rows, model)
            du = (dot(dfb[...], w, NT) * dact[:, cols].astype(F32)).astype(BF)
            dact[:, cols] = du
            total = jnp.sum(du.astype(F32), axis=0, keepdims=True)
            vg[8 + j : 9 + j, t * half : (t + 1) * half] = total

        tile(0)
        tile(1)

    def grad_in(j):
        if j == 0:
            sent(*range(DOWN, CHUNKS))
            y1t[...] = y1b[...].T

        def tile(t):
            wide_cols = pl.ds(pl.multiple_of(j * model + t * 256, 256), 256)
            g = dot(y1t[...], dact[:, wide_cols]).astype(BF)
            wd[:, :, :, :, j, :, span(t, 256)] = g.reshape(ZH, ZL, YS, CS, rows, 256)

        loop(model // 256, tile)

    def grad_normed(j):
        h2[...] += dot(dact[:, j * model : (j + 1) * model], weight(IN + j), NT)

    def norm_one_back(_):
        g1 = prm[3:4, :]

        def tile(i):
            r = span(i, 128)
            dy, n = h2[r, :], n1[r, :]
            vsum(3, dy * n)
            vsum(4, dy)
            dh = norm_back(dy * g1, n, rs1[r, :])
            h2[r, :] = dh
            low = dh.astype(BF)
            dfb[r, :] = low
            vsum(2, low.astype(F32))

        loop(seq // 128, tile)

    def grad_out(_):
        g = dot(ct[...], dfb[...]).astype(BF)
        go[0] = g.reshape(ZH, ZL, YS, CS, rows, model)

    def grad_context(_):
        store_out.pop().wait()
        vt[...] = x[...].T
        dcx[...] = dot(dfb[...], weight(OUT), NT).astype(BF)

    def attend_back(g):
        def one(j):
            cols = span(j, pair)
            keys = pl.ds(pl.multiple_of(group + j * pair, pair), pair)
            vals = pl.ds(pl.multiple_of(2 * group + j * pair, pair), pair)
            place = pl.ds(pl.multiple_of(g * group + j * pair, pair), pair)
            lane = lax.broadcasted_iota(jnp.int32, (seq, pair), 1) // head
            dc = dcx[:, place]
            q, k, v = qkv[g, :, cols], qkv[g, :, keys], qkv[g, :, vals]
            kt = k.T
            dk, dv, dq = [], [], []
            for e in range(2):
                probs = pt[g, 2 * j + e]
                dv.append(dot(probs, dc))
                dp = dot(jnp.where(lane == e, v, jnp.zeros((), BF)), dc, NT)
                p32 = probs.astype(F32)
                t = p32 * dp
                ds = (t - p32 * jnp.sum(t, axis=0, keepdims=True)).astype(BF)
                dk.append(dot(ds, q))
                dq.append((dot(kt[e * head : (e + 1) * head, :], ds) * head**-0.5).astype(BF))
            dv = jnp.where(lane == 0, dv[0], dv[1]).astype(BF)
            dq = jnp.concatenate(dq, axis=0).T
            qkv[g, :, cols] = dq
            qkv[g, :, keys] = jnp.where(lane == 0, dk[0], dk[1]).astype(BF)
            qkv[g, :, vals] = dv
            vg[0:1, place] = jnp.sum(dq.astype(F32), axis=0, keepdims=True)
            vg[1:2, place] = jnp.sum(dv.astype(F32), axis=0, keepdims=True)

        loop(group // pair, one)

    def grad_qkv(g):
        if g == 0:
            sent(*range(IN, DOWN))

        def tile(t):
            cols = span(t, group)
            r = dot(vt[...], qkv[g, :, cols]).astype(BF)
            wa[IN + g, :, :, :, :, :, cols] = r.reshape(ZH, ZL, YS, CS, rows, group)

        loop(3, tile)

    def grad_x(g):
        before = h2 if g == 0 else n1
        n1[...] = before[...] + dot(qkv[g], weight(g), NT)
        if g == 2:
            store_x.append(store(n1, gtok_hbm.at[0], 2))

    last = len(SUMMED) - 1
    every = (ALL, ALL)
    mine = (zh, zl)

    def at_z(zz):
        return (zz // ZL, lax.rem(zz, ZL))

    def gpiece(k, zi, yy, cc, cols=ALL):
        if k < 4:
            return gd.at[(k, *zi, yy, cc, ALL, cols)]
        if k < 8:
            return wd.at[(*zi, yy, cc, k - 4, ALL, cols)]
        if k < 9:
            return go.at[(0, *zi, yy, cc, ALL, cols)]
        return wa.at[(IN + k - 9, *zi, yy, cc, ALL, cols)]

    def left(i):
        return pl.ds(SUMMED[i][1], SUMMED[i][2])

    def right(i):
        return pl.ds(half + SUMMED[i][1], SUMMED[i][2])

    def near(i):
        return left(i)

    def both(i):
        return (ALL,) if SUMMED[i][2] == half else (left(i), right(i))

    def r_core(i, cols):
        k = SUMMED[i][0]
        return remote(
            gpiece(k, every, ALL, 1 - c, cols), rcore.at[k % RING, :, :, :, :, cols], r_sent.at[i], rrc.at[i], sibling
        )

    def r_ya(i):
        k = SUMMED[i][0]
        src, dst = gpiece(k, every, 1 - y, c, left(i)), rya.at[k, :, :, :, near(i)]
        return remote(src, dst, r_sent.at[i], rry.at[i, 0], across_y)

    def r_xb(i):
        k = SUMMED[i][0]
        src, dst = gpiece(k, (ALL, 1 - parity(i)), ALL, c, right(i)), rxb.at[k, :, :, :, near(i)]
        return remote(src, dst, r_sent.at[i], rrx.at[i, 0], across_x)

    def r_za(i, dz):
        k = SUMMED[i][0]
        src, dst = gpiece(k, at_z(ahead(dz)), y, c, left(i)), rza.at[k, dz - 1, :, near(i)]
        return remote(src, dst, r_sent.at[i], rrz.at[i, 0], device(ahead(dz), y, c, px))

    def r_yb(i):
        k = SUMMED[i][0]
        src, dst = gpiece(k, (ALL, parity(i)), 1 - y, c, right(i)), ryb.at[k, :, :, near(i)]
        return remote(src, dst, r_sent.at[i], rry.at[i, 1], across_y)

    def r_xa(i):
        k = SUMMED[i][0]
        src, dst = gpiece(k, mine, y, c, left(i)), rxa.at[k, :, near(i)]
        return remote(src, dst, r_sent.at[i], rrx.at[i, 1], across_x)

    def r_zb(i, dz):
        k = SUMMED[i][0]
        src, dst = gpiece(k, at_z(ahead(dz)), y, c, right(i)), rzb.at[k, dz - 1, :, near(i)]
        return remote(src, dst, r_sent.at[i], rrz.at[i, 1], device(ahead(dz), y, c, px))

    def r_fb(i):
        k = SUMMED[i][0]
        return remote(
            gpiece(k, mine, y, c, right(i)), rfb.at[k, :, near(i)], r_sent.at[i], rrf.at[i], across_x
        )

    v_rc = remote(gv.at[:, :, :, 1 - c], rv_core, rv_sent, wrc, sibling)
    v_ry = remote(gv.at[:, :, 1 - y, c], rv_y, rv_sent, wry, across_y)
    v_rx = remote(gv.at[(*mine, y, c)], rv_x, rv_sent, wrx, across_x)

    def v_rz(dz):
        where = device(ahead(dz), y, c, px)
        return remote(gv.at[(*at_z(ahead(dz)), y, c)], rv_z.at[dz - 1], rv_sent, wrz, where)

    def parity(i):
        return lax.rem(px + i, 2)

    def same(i):
        return zl == parity(i)


    def add_into(ref, *others):
        if len(others) == 1:
            ref[...] += others[0][...]
            return
        total = ref[...].astype(F32)
        for other in others:
            total = total + other[...].astype(F32)
        ref[...] = total.astype(BF)

    def r0(i):
        for cols in both(i):
            r_core(i, cols).start()
        if i == last:
            v_rc.start()

    def r1(i):
        k, _, width = SUMMED[i]
        drained(wa.at[0, :, :, :, 0, :, pl.ds(0, 2 * width)], rrc.at[i])

        def add(zz):
            for cols in both(i):
                add_into(gpiece(k, at_z(zz), ALL, c, cols), rcore.at[(k % RING, *at_z(zz), ALL, ALL, cols)])

        loop(ZS, add)
        r_ya(i).start()
        r_xb(i).start()
        if i == last:
            v_rc.wait_recv()
            add_into(gv.at[:, :, :, c], rv_core)
            v_ry.start()

    def r2a(i):
        k = SUMMED[i][0]
        r_ya(i).wait_recv()
        add_into(gpiece(k, every, y, c, left(i)), rya.at[k, :, :, :, near(i)])
        for dz in (1, 2, 3):
            r_za(i, dz).start()
        if i == last:
            v_ry.wait_recv()
            add_into(gv.at[:, :, y, c], rv_y)
            for dz in (1, 2, 3):
                v_rz(dz).start()

    def r2b(i):
        k = SUMMED[i][0]
        r_xb(i).wait_recv()
        add_into(gpiece(k, (ALL, parity(i)), ALL, c, right(i)), rxb.at[k, :, :, :, near(i)])
        r_yb(i).start()

    def r3a(i):
        k = SUMMED[i][0]
        drained(rza.at[k, :, :, near(i)], rrz.at[i, 0])
        add_into(gpiece(k, mine, y, c, left(i)), *(rza.at[k, dz, :, near(i)] for dz in range(3)))
        r_xa(i).start()
        if i == last:
            drained(rv_z, wrz)
            add_into(gv.at[(*mine, y, c)], rv_z.at[0], rv_z.at[1], rv_z.at[2])
            v_rx.start()

    def r3b(i):
        k = SUMMED[i][0]
        r_yb(i).wait_recv()
        add_into(gpiece(k, (ALL, parity(i)), y, c, right(i)), ryb.at[k, :, :, near(i)])
        pl.when(same(i))(lambda: r_zb(i, 2).start())

        @pl.when(jnp.logical_not(same(i)))
        def _():
            r_zb(i, 1).start()
            r_zb(i, 3).start()

    def r4a(i):
        k = SUMMED[i][0]
        r_xa(i).wait_recv()
        fin[k, :, left(i)] = gpiece(k, mine, y, c, left(i))[...].astype(F32) + rxa[k, :, near(i)].astype(F32)
        if i == last:
            v_rx.wait_recv()
            store_vec.append(store(gv.at[(*mine, y, c)], gvec_hbm.at[0], 3))
            store_vec.append(store(rv_x, gvec_hbm.at[1], 4))
        settle(k)

    def r4b(i):
        k = SUMMED[i][0]

        @pl.when(same(i))
        def _():
            drained(rzb.at[k, :, :, near(i)], rrz.at[i, 1])
            piece = gpiece(k, mine, y, c, right(i))
            add_into(piece, *(rzb.at[k, dz, :, near(i)] for dz in range(3)))
            r_fb(i).start()
            fin[k, :, right(i)] = piece[...].astype(F32)

    def r5(i):
        k = SUMMED[i][0]

        @pl.when(jnp.logical_not(same(i)))
        def _():
            r_fb(i).wait_recv()
            fin[k, :, right(i)] = rfb[k, :, near(i)].astype(F32)

        settle(k)

    store_out, store_x, store_vec = [], [], []
    open_ends = {k: 2 * sum(part[0] == k for part in SUMMED) for k in range(CHUNKS)}

    def store(src, dst, i=0):
        cp = pltpu.make_async_copy(src, dst, s_store.at[i])
        cp.start()
        return cp

    def settle(k):
        open_ends[k] -= 1
        if open_ends[k]:
            return
        if k < 4:
            store(fin.at[k], gdown_hbm.at[pl.ds(k * rows, rows)])
        elif k < 8:
            store(fin.at[k], gin_hbm.at[:, pl.ds((k - 4) * model, model)])
        elif k < 9:
            store(fin.at[k], gout_hbm)
        else:
            for part in range(3):
                store(
                    fin.at[k, :, pl.ds(part * group, group)],
                    gqkv_hbm.at[:, pl.ds(part * model + (k - 9) * group, group)],
                )

    steps = (
        e1, eo, e2, e3, e4, e5,
        r0, r1, r2a, r2b, r3a, r3b,
        r4a, r4b, r5, spread_params, project, attend,
        out_proj, feed_up, feed_down, norm_two, grad_down, grad_act,
        grad_in, grad_normed, norm_one_back, grad_out, grad_context, attend_back,
        grad_qkv, gather_grads, grad_x,
    )
    vg[...] = jnp.zeros_like(vg)
    for step, i in ORDER:
        if step == S_PROJECT and i == 0:
            load_x.wait()
        if step == S_NORM2:
            load_cot.wait()
        steps[step](i)
    sent(*range(IN))
    vec_sent()
    for i, (_, _, width) in enumerate(SUMMED):
        drained(wa.at[0, :, :, :, :, :, pl.ds(0, 2 * width)], r_sent.at[i])
    drained(gv, rv_sent)
    drained(fin, s_store.at[0])
    for cp in (*store_vec, *store_x):
        cp.wait()


def place_kernel(cuts, *refs):
    count = len(cuts)
    sources, targets, held = refs[: count + 1], refs[count + 1 : 2 * count + 2], refs[2 * count + 2 : 3 * count + 3]
    vector, sem_in, sem_out = refs[3 * count + 3 :]
    first = pltpu.make_async_copy(sources[count], held[count], sem_in.at[sum(cuts)])
    first.start()
    moves = []
    for src, dst, mid, parts in zip(sources, targets, held, cuts):
        size = src.shape[-2] // parts
        for j in range(parts):
            at = (slice(None),) * (len(src.shape) - 2) + (pl.ds(j * size, size),)
            i = len(moves)
            moves.append(
                (
                    pltpu.make_async_copy(src.at[at], mid.at[at], sem_in.at[i]),
                    pltpu.make_async_copy(mid.at[at], dst.at[at], sem_out.at[i]),
                )
            )
    for into, _ in moves:
        into.start()
    first.wait()
    segment = vector.shape[0] // 3
    total = held[count][0].astype(F32) + held[count][1].astype(F32)
    vector[...] = jnp.concatenate([total[s : s + 1, 0:segment] for s in range(3)], axis=1).reshape(-1)
    last = pltpu.make_async_copy(vector, targets[count], sem_out.at[sum(cuts)])
    last.start()
    for into, out in moves:
        into.wait()
        out.start()
    for _, out in moves:
        out.wait()
    last.wait()


def fused_layer(tokens, lengths, w_qkv, w_out, w_in, w_down, norms_biases, cotangent):
    seq, model = tokens.shape[1:]
    rows = w_qkv.shape[0]
    hidden = w_in.shape[1]
    half = model // 2
    group = model // 3
    vm, dma = pltpu.VMEM, pltpu.SemaphoreType.DMA
    grid = (ZH, ZL, YS, CS)
    n, m, u = CHUNKS, len(GATHERED), len(SUMMED)
    scratch = [
        vm((DOWN, *grid, rows, model), BF),
        vm((*grid, 4, rows, model), BF),
        vm((*grid, 16, 256), BF),
        vm((4, *grid, rows, model), BF),
        vm((1, *grid, rows, model), BF),
        vm((*grid, 16, 256), BF),
        vm((RING, ZH, ZL, YS, rows, model), BF),
        vm((n, ZH, ZL, rows, half), BF),
        vm((n, ZH, YS, rows, half), BF),
        vm((n, 3, rows, half), BF),
        vm((n, ZH, rows, half), BF),
        vm((n, 3, rows, half), BF),
        vm((n, rows, half), BF),
        vm((n, rows, half), BF),
        vm((ZH, ZL, YS, 16, 256), BF),
        vm((ZH, ZL, 16, 256), BF),
        vm((3, 16, 256), BF),
        vm((16, 256), BF),
        vm((n, rows, model), F32),
        vm(norms_biases.shape, BF),
        vm((seq, model), BF),
        vm((seq, model), BF),
        vm((3, seq, model), BF),
        vm((model, seq), BF),
        vm((3, group // (model // HEADS), seq, seq), BF),
        vm((model, seq), BF),
        vm((seq, model), F32),
        vm((seq, model), BF),
        vm((model, seq), BF),
        vm((ZS * YS, CS, 4, rows, seq), BF),
        vm((seq, hidden), BF),
        vm((seq, model), F32),
        vm((seq, model), BF),
        vm((seq, model), BF),
        vm((seq, 1), F32),
        vm((16, model), F32),
        vm((16, model), F32),
        dma((n,)), dma((3,)), dma((5,)),
        dma((m,)), dma((m,)), dma((m,)), dma((m,)), dma((m,)), dma, dma, dma, dma,
        dma((u,)), dma, dma((u,)), dma((u, 2)), dma((u, 2)), dma((u, 2)), dma((u,)), dma, dma, dma, dma,
    ]
    hbm = pl.BlockSpec(memory_space=pl.ANY)
    shape = jax.ShapeDtypeStruct
    outs = pl.pallas_call(
        layer_kernel,
        out_shape=(
            shape(tokens.shape, BF),
            shape(tokens.shape, F32),
            shape(w_qkv.shape, F32),
            shape(w_out.shape, F32),
            shape(w_in.shape, F32),
            shape(w_down.shape, F32),
            shape((2, 16, 256), BF),
        ),
        in_specs=[hbm, pl.BlockSpec(memory_space=pltpu.SMEM)] + [hbm] * 6,
        out_specs=(hbm,) * 7,
        scratch_shapes=scratch,
        compiler_params=pltpu.CompilerParams(
            collective_id=0, has_side_effects=True, vmem_limit_bytes=64 << 20
        ),
        name="layer",
    )(tokens, lengths, w_qkv, w_out, w_in, w_down, norms_biases, cotangent)
    cuts = (1, 2, 1, 1, 1, 1)
    *placed, grad_vector = pl.pallas_call(
        functools.partial(place_kernel, cuts),
        out_shape=(*(shape(o.shape, o.dtype) for o in outs[:6]), shape(norms_biases.shape, F32)),
        in_specs=[hbm] * 7,
        out_specs=(hbm,) * 7,
        scratch_shapes=[vm(o.shape, o.dtype) for o in outs]
        + [vm(norms_biases.shape, F32), dma((sum(cuts) + 1,)), dma((sum(cuts) + 1,))],
        name="place",
    )(*outs)
    return (*placed, grad_vector)


def norm_rows(values, gain_row, shift_row):
    average = jnp.mean(values, -1, keepdims=True)
    centred = values - average
    spread = jnp.mean(centred * centred, -1, keepdims=True)
    return centred * lax.rsqrt(spread + 1e-06) * gain_row + shift_row


def gelu_exact(values):
    return jax.nn.gelu(values, approximate=False)


def column_sum(values):
    return jnp.sum(values.astype(jnp.float32), 0)


def split_vector(vector, model_width, hidden_width):
    segments = [
        vector[position * model_width : (position + 1) * model_width] for position in range(8)
    ]
    return segments + [vector[8 * model_width : 8 * model_width + hidden_width]]


def pair_blocks(projected, head_count):
    row_count = projected.shape[0]
    pair_count = head_count // 2
    pair_width = projected.shape[1] // (3 * pair_count)
    return projected.reshape(row_count, 3, pair_count, pair_width).transpose(2, 1, 0, 3)


def unpair_blocks(blocks):
    pair_count = blocks.shape[0]
    row_count = blocks.shape[2]
    pair_width = blocks.shape[3]
    return blocks.transpose(2, 1, 0, 3).reshape(row_count, 3 * pair_count * pair_width)


def pair_scores(head_block, usable, factor):
    row_count = head_block.shape[1]
    queries = head_block[0].reshape(row_count, 2, -1)
    key_rows = head_block[1].reshape(row_count, 2, -1)
    values = head_block[2].reshape(row_count, 2, -1)
    scores = (
        jnp.einsum("qhd,khd->hqk", queries, key_rows, preferred_element_type=jnp.float32) * factor
    )
    return (queries, key_rows, values, jnp.where(usable[None, None, :], scores, -1000000000.0))


def attention_forward(blocks, usable, factor):

    def one_pair(head_block):
        queries, key_rows, values, scores = pair_scores(head_block, usable, factor)
        highest = jnp.max(scores, -1, keepdims=True)
        raised = jnp.exp(scores - highest)
        summed = jnp.sum(raised, -1, keepdims=True)
        attend = (raised / summed).astype(jnp.bfloat16)
        context = jnp.einsum("hqk,khd->qhd", attend, values, preferred_element_type=jnp.float32)
        return (context.reshape(context.shape[0], -1), highest[..., 0] + jnp.log(summed[..., 0]))

    return lax.map(one_pair, blocks)


def attention_backward(blocks, grad_pairs, log_totals, usable, factor):

    def one_pair(pair_inputs):
        head_block, grad_context, log_total = pair_inputs
        queries, key_rows, values, scores = pair_scores(head_block, usable, factor)
        attend = jnp.exp(scores - log_total[..., None])
        row_count = grad_context.shape[0]
        grad_heads = grad_context.reshape(row_count, 2, -1)
        grad_values = jnp.einsum(
            "hqk,qhd->khd",
            attend.astype(jnp.bfloat16),
            grad_heads,
            preferred_element_type=jnp.float32,
        )
        grad_attend = jnp.einsum(
            "qhd,khd->hqk", grad_heads, values, preferred_element_type=jnp.float32
        )
        grad_scores = attend * (grad_attend - jnp.sum(attend * grad_attend, -1, keepdims=True))
        grad_low = grad_scores.astype(jnp.bfloat16)
        grad_queries = (
            jnp.einsum("hqk,khd->qhd", grad_low, key_rows, preferred_element_type=jnp.float32)
            * factor
        )
        grad_keys = (
            jnp.einsum("hqk,qhd->khd", grad_low, queries, preferred_element_type=jnp.float32)
            * factor
        )
        return jnp.stack(
            [
                grad_queries.reshape(row_count, -1),
                grad_keys.reshape(row_count, -1),
                grad_values.reshape(row_count, -1),
            ]
        )

    return lax.map(one_pair, (blocks, grad_pairs, log_totals))


def layer_forward(inputs, length, weights):
    w_qkv, w_out, w_in, w_down, vector = weights
    row_count, model_width = inputs.shape
    hidden_width = w_in.shape[1]
    params = split_vector(vector.astype(jnp.float32), model_width, hidden_width)
    joined_bias = jnp.concatenate([params[0], jnp.zeros((model_width,), jnp.float32), params[1]])
    projected = (jnp.dot(inputs, w_qkv, preferred_element_type=jnp.float32) + joined_bias).astype(
        jnp.bfloat16
    )
    blocks = pair_blocks(projected, HEADS)
    usable = jnp.arange(row_count) < length
    factor = (model_width // HEADS) ** (-0.5)
    context_pairs, log_totals = attention_forward(blocks, usable, factor)
    context = context_pairs.transpose(1, 0, 2).reshape(row_count, model_width).astype(jnp.bfloat16)
    resid_one = inputs.astype(jnp.float32) + (
        jnp.dot(context, w_out, preferred_element_type=jnp.float32) + params[2]
    )
    normed_one = norm_rows(resid_one, params[3], params[4])
    normed_low = normed_one.astype(jnp.bfloat16)
    pre_act = jnp.dot(normed_low, w_in, preferred_element_type=jnp.float32) + params[8]
    activated = gelu_exact(pre_act).astype(jnp.bfloat16)
    resid_two = normed_one + (
        jnp.dot(activated, w_down, preferred_element_type=jnp.float32) + params[5]
    )
    result = norm_rows(resid_two, params[6], params[7])
    saved = (
        params,
        blocks,
        usable,
        factor,
        log_totals,
        context,
        resid_one,
        normed_low,
        pre_act,
        activated,
        resid_two,
    )
    return (result, saved)


def layer_backward(inputs, length, grad_result, weights):
    w_qkv, w_out, w_in, w_down, vector = weights
    unused_result, saved = layer_forward(inputs, length, weights)
    (
        params,
        blocks,
        usable,
        factor,
        log_totals,
        context,
        resid_one,
        normed_low,
        pre_act,
        activated,
        resid_two,
    ) = saved
    row_count, model_width = inputs.shape
    unused_two, norm_two_back = jax.vjp(norm_rows, resid_two, params[6], params[7])
    grad_two, grad_gain_two, grad_shift_two = norm_two_back(grad_result)
    grad_feed = grad_two.astype(jnp.bfloat16)
    grad_down = jnp.einsum("sf,sd->fd", activated, grad_feed, preferred_element_type=jnp.float32)
    grad_act = jnp.einsum("sd,fd->sf", grad_feed, w_down, preferred_element_type=jnp.float32)
    unused_act, gelu_back = jax.vjp(gelu_exact, pre_act)
    grad_pre = gelu_back(grad_act)[0].astype(jnp.bfloat16)
    grad_in = jnp.einsum("sd,sf->df", normed_low, grad_pre, preferred_element_type=jnp.float32)
    grad_normed = grad_two + jnp.einsum(
        "sf,df->sd", grad_pre, w_in, preferred_element_type=jnp.float32
    )
    unused_one, norm_one_back = jax.vjp(norm_rows, resid_one, params[3], params[4])
    grad_one, grad_gain_one, grad_shift_one = norm_one_back(grad_normed)
    grad_attended = grad_one.astype(jnp.bfloat16)
    grad_out = jnp.einsum("sd,se->de", context, grad_attended, preferred_element_type=jnp.float32)
    grad_context = jnp.einsum(
        "se,de->sd", grad_attended, w_out, preferred_element_type=jnp.float32
    ).astype(jnp.bfloat16)
    grad_pairs = grad_context.reshape(row_count, HEADS // 2, -1).transpose(1, 0, 2)
    grad_blocks = attention_backward(blocks, grad_pairs, log_totals, usable, factor)
    grad_projected = unpair_blocks(grad_blocks).astype(jnp.bfloat16)
    grad_qkv = jnp.einsum("sd,se->de", inputs, grad_projected, preferred_element_type=jnp.float32)
    grad_inputs = grad_one + jnp.einsum(
        "se,de->sd", grad_projected, w_qkv, preferred_element_type=jnp.float32
    )
    projected_sums = column_sum(grad_projected)
    grad_vector = jnp.concatenate(
        [
            projected_sums[:model_width],
            projected_sums[2 * model_width :],
            column_sum(grad_attended),
            grad_gain_one,
            grad_shift_one,
            column_sum(grad_feed),
            grad_gain_two,
            grad_shift_two,
            column_sum(grad_pre),
        ]
    )
    return (grad_inputs, (grad_qkv, grad_out, grad_in, grad_down, grad_vector))


def local(tokens, lengths, w_qkv, w_out, w_in, w_down, norms_biases, cotangent):
    weights = (
        lax.all_gather(w_qkv, "wide", axis=0, tiled=True),
        lax.all_gather(w_out, "wide", axis=0, tiled=True),
        lax.all_gather(w_in, "wide", axis=0, tiled=True),
        lax.all_gather(w_down, "wide", axis=0, tiled=True),
        lax.all_gather(norms_biases, "wide", axis=0, tiled=True),
    )

    def forward_one(sequence):
        return layer_forward(sequence[0], sequence[1], weights)[0].astype(jnp.bfloat16)

    output = lax.map(forward_one, (tokens, lengths))
    second_copy = (
        lax.all_gather(w_qkv, "wide", axis=0, tiled=True),
        lax.all_gather(w_out, "wide", axis=0, tiled=True),
        lax.all_gather(w_in, "wide", axis=0, tiled=True),
        lax.all_gather(w_down, "wide", axis=0, tiled=True),
        lax.all_gather(norms_biases, "wide", axis=0, tiled=True),
    )
    running = tuple((jnp.zeros(member.shape, jnp.float32) for member in second_copy))

    def advance(totals, sequence):
        grad_inputs, gradients = layer_backward(
            sequence[0], sequence[1], sequence[2].astype(jnp.float32), second_copy
        )
        return (jax.tree.map(jnp.add, totals, gradients), grad_inputs)

    totals, grad_tokens = lax.scan(advance, running, (tokens, lengths, cotangent))
    owned_rows = (
        lax.psum_scatter(
            totals[0].astype(jnp.bfloat16), "wide", scatter_dimension=0, tiled=True
        ).astype(jnp.float32),
        lax.psum_scatter(
            totals[1].astype(jnp.bfloat16), "wide", scatter_dimension=0, tiled=True
        ).astype(jnp.float32),
        lax.psum_scatter(
            totals[2].astype(jnp.bfloat16), "wide", scatter_dimension=0, tiled=True
        ).astype(jnp.float32),
        lax.psum_scatter(
            totals[3].astype(jnp.bfloat16), "wide", scatter_dimension=0, tiled=True
        ).astype(jnp.float32),
        lax.psum_scatter(
            totals[4].astype(jnp.bfloat16), "wide", scatter_dimension=0, tiled=True
        ).astype(jnp.float32),
    )
    summed_all = (
        lax.psum(owned_rows[0].astype(jnp.bfloat16), "narrow").astype(jnp.float32),
        lax.psum(owned_rows[1].astype(jnp.bfloat16), "narrow").astype(jnp.float32),
        lax.psum(owned_rows[2].astype(jnp.bfloat16), "narrow").astype(jnp.float32),
        lax.psum(owned_rows[3].astype(jnp.bfloat16), "narrow").astype(jnp.float32),
        lax.psum(owned_rows[4].astype(jnp.bfloat16), "narrow").astype(jnp.float32),
    )
    return (
        output,
        grad_tokens,
        summed_all[0],
        summed_all[1],
        summed_all[2],
        summed_all[3],
        summed_all[4],
    )


def solution(mesh):
    in_specs = (
        P(("wide", "narrow"), None, None),
        P(("wide", "narrow")),
        P("wide", None),
        P("wide", None),
        P("wide", None),
        P("wide", None),
        P("wide"),
        P(("wide", "narrow"), None, None),
    )
    out_specs = (
        P(("wide", "narrow"), None, None),
        P(("wide", "narrow"), None, None),
        P("wide", None),
        P("wide", None),
        P("wide", None),
        P("wide", None),
        P("wide"),
    )
    chips = (ZS * YS * CS, 2)
    fused = tuple(mesh.shape[axis] for axis in ("wide", "narrow")) == chips
    step = fused_layer if fused else local
    return jax.shard_map(step, mesh=mesh, in_specs=in_specs, out_specs=out_specs, check_vma=False)
```

```python
import functools

import jax
import jax.numpy as jnp
import numpy as np
from jax import lax
from jax.experimental import pallas as pl
from jax.experimental.pallas import tpu as pltpu
from jax.sharding import PartitionSpec as P

HEADS = 12
MESH = pl.DeviceIdType.MESH
BF = jnp.bfloat16
F32 = jnp.float32
NT = (((1,), (1,)), ((), ()))
TN = (((0,), (0,)), ((), ()))
ZH, ZL, YS, CS = 2, 2, 2, 2
ZS = ZH * ZL
QKV, OUT, IN, DOWN, CHUNKS = 0, 3, 4, 8, 12
RING = 8
(
    S_E1, S_EO, S_E2, S_E3, S_E4, S_E5, S_R0, S_R1, S_R2A, S_R2B, S_R3A,
    S_R3B, S_R4A, S_R4B, S_R5, S_SPREAD, S_PROJECT, S_ATTEND, S_OUT, S_UP, S_DOWN, S_NORM2,
    S_GDOWN, S_GACT, S_GIN, S_GNORM, S_NORM1, S_GOUT, S_GCTX, S_ABACK, S_GQKV, S_GGRADS, S_GX,
) = range(33)
GATHERED = (
    (0, 0, 384), (0, 384, 384), (1, 0, 384), (1, 384, 384), (2, 0, 384), (2, 384, 384), (3, 0, 384), (3, 384, 384),
    (4, 0, 384), (4, 384, 384), (5, 0, 384), (5, 384, 384), (6, 0, 384), (6, 384, 384), (7, 0, 384), (7, 384, 384),
    (8, 0, 384), (8, 384, 384), (9, 0, 384), (9, 384, 384), (10, 0, 384), (10, 384, 384), (11, 0, 256), (11, 256, 256),
    (11, 512, 256),
)
SUMMED = (
    (0, 0, 128), (0, 128, 128), (0, 256, 128), (1, 0, 384), (2, 0, 384), (3, 0, 384), (4, 0, 384), (5, 0, 384),
    (6, 0, 384), (7, 0, 384), (8, 0, 384), (9, 0, 384), (10, 0, 384), (11, 0, 384),
)
ORDER = (
    (S_E1, 0), (S_EO, 0), (S_E1, 1), (S_EO, 1), (S_E1, 2), (S_EO, 2), (S_EO, 3), (S_EO, 4), (S_EO, 5), (S_EO, 6),
    (S_EO, 7), (S_E1, 3), (S_E2, 0), (S_EO, 8), (S_E1, 4), (S_E2, 1), (S_EO, 9), (S_E1, 5), (S_E2, 2), (S_EO, 10),
    (S_E3, 0), (S_E1, 6), (S_E2, 3), (S_EO, 11), (S_E3, 1), (S_E1, 7), (S_E2, 4), (S_EO, 12), (S_E3, 2), (S_E4, 0),
    (S_E1, 8), (S_E2, 5), (S_EO, 13), (S_E3, 3), (S_E4, 1), (S_E5, 0), (S_E1, 9), (S_E2, 6), (S_EO, 14), (S_E3, 4),
    (S_E4, 2), (S_E5, 1), (S_SPREAD, 0), (S_PROJECT, 0), (S_E1, 10), (S_E2, 7), (S_EO, 15), (S_E3, 5), (S_E4, 3), (S_E5, 2),
    (S_ATTEND, 0), (S_E1, 11), (S_E2, 8), (S_EO, 16), (S_E3, 6), (S_E4, 4), (S_E5, 3), (S_ATTEND, 1), (S_E1, 12), (S_E2, 9),
    (S_EO, 17), (S_E3, 7), (S_E4, 5), (S_E5, 4), (S_PROJECT, 1), (S_E1, 13), (S_E2, 10), (S_EO, 18), (S_E3, 8), (S_E4, 6),
    (S_E5, 5), (S_ATTEND, 2), (S_E1, 14), (S_E2, 11), (S_EO, 19), (S_E3, 9), (S_E4, 7), (S_E5, 6), (S_ATTEND, 3), (S_E1, 15),
    (S_E2, 12), (S_EO, 20), (S_E3, 10), (S_E4, 8), (S_E5, 7), (S_PROJECT, 2), (S_E1, 16), (S_E2, 13), (S_EO, 21), (S_E3, 11),
    (S_E4, 9), (S_E5, 8), (S_ATTEND, 4), (S_E1, 17), (S_E2, 14), (S_EO, 22), (S_E3, 12), (S_E4, 10), (S_E5, 9), (S_ATTEND, 5),
    (S_E1, 18), (S_E2, 15), (S_EO, 23), (S_E3, 13), (S_E4, 11), (S_E5, 10), (S_OUT, 0), (S_E1, 19), (S_E2, 16), (S_EO, 24),
    (S_E3, 14), (S_E4, 12), (S_E5, 11), (S_UP, 0), (S_E1, 20), (S_E2, 17), (S_E3, 15), (S_E4, 13), (S_E5, 12), (S_UP, 1),
    (S_E1, 21), (S_E2, 18), (S_E3, 16), (S_E4, 14), (S_E5, 13), (S_UP, 2), (S_E1, 22), (S_E2, 19), (S_E3, 17), (S_E4, 15),
    (S_E5, 14), (S_E1, 23), (S_E2, 20), (S_E3, 18), (S_E4, 16), (S_E5, 15), (S_UP, 3), (S_E1, 24), (S_E2, 21), (S_E3, 19),
    (S_E4, 17), (S_E5, 16), (S_E2, 22), (S_E3, 20), (S_E4, 18), (S_E5, 17), (S_DOWN, 0), (S_E2, 23), (S_E3, 21), (S_E4, 19),
    (S_E5, 18), (S_E2, 24), (S_E3, 22), (S_E4, 20), (S_E5, 19), (S_DOWN, 1), (S_E3, 23), (S_E4, 21), (S_E5, 20), (S_E3, 24),
    (S_E4, 22), (S_E5, 21), (S_DOWN, 2), (S_E4, 23), (S_E5, 22), (S_E4, 24), (S_E5, 23), (S_E5, 24), (S_DOWN, 3), (S_NORM2, 0),
    (S_GDOWN, 0), (S_R0, 0), (S_R0, 1), (S_GDOWN, 1), (S_R0, 2), (S_R0, 3), (S_R1, 0), (S_GDOWN, 2), (S_R1, 1), (S_R0, 4),
    (S_R1, 2), (S_GACT, 0), (S_R1, 3), (S_GDOWN, 3), (S_R1, 4), (S_GACT, 1), (S_R2A, 1), (S_GACT, 2), (S_R2A, 2), (S_GACT, 3),
    (S_R0, 5), (S_R2A, 0), (S_GIN, 0), (S_R2A, 3), (S_R2B, 1), (S_R2B, 2), (S_GNORM, 0), (S_R1, 5), (S_GIN, 1), (S_R0, 6),
    (S_R2A, 4), (S_GNORM, 1), (S_R2B, 3), (S_R3B, 2), (S_R3B, 1), (S_GIN, 2), (S_R1, 6), (S_R0, 7), (S_GNORM, 2), (S_R2A, 5),
    (S_R2B, 4), (S_GIN, 3), (S_R0, 8), (S_R1, 7), (S_R3B, 3), (S_R2B, 5), (S_R3A, 4), (S_GNORM, 3), (S_R1, 8), (S_R0, 9),
    (S_R2B, 6), (S_R2A, 6), (S_NORM1, 0), (S_GOUT, 0), (S_R0, 10), (S_R3B, 4), (S_GCTX, 0), (S_R2B, 7), (S_R1, 9), (S_R1, 10),
    (S_R2A, 7), (S_ABACK, 0), (S_R2B, 8), (S_R3B, 5), (S_GQKV, 0), (S_R0, 11), (S_R2A, 8), (S_ABACK, 1), (S_R3B, 6), (S_R3A, 1),
    (S_R1, 11), (S_R3B, 7), (S_R4A, 4), (S_R3A, 6), (S_GQKV, 1), (S_R3A, 3), (S_R2A, 9), (S_R0, 12), (S_ABACK, 2), (S_R2A, 10),
    (S_R2B, 11), (S_R1, 12), (S_GX, 0), (S_R2B, 9), (S_R3B, 8), (S_GQKV, 2), (S_R3A, 2), (S_GGRADS, 0), (S_R2A, 11), (S_R0, 13),
    (S_R3A, 7), (S_R4B, 6), (S_R4B, 4), (S_R4B, 1), (S_R1, 13), (S_R4A, 3), (S_R4A, 1), (S_R3B, 11), (S_R2B, 0), (S_R2A, 12),
    (S_R3A, 8), (S_R4B, 5), (S_GX, 1), (S_R4A, 2), (S_R4B, 8), (S_R3A, 9), (S_R4A, 6), (S_R3B, 9), (S_R2B, 12), (S_R2B, 13),
    (S_GX, 2), (S_R3A, 0), (S_R2A, 13), (S_R3A, 5), (S_R2B, 10), (S_R3A, 11), (S_R4B, 2), (S_R3A, 10), (S_R3B, 12), (S_R5, 5),
    (S_R4B, 11), (S_R4B, 7), (S_R4B, 3), (S_R3B, 13), (S_R4A, 9), (S_R3B, 10), (S_R3A, 12), (S_R3B, 0), (S_R5, 8), (S_R4A, 10),
    (S_R4A, 5), (S_R4A, 11), (S_R4A, 8), (S_R5, 2), (S_R5, 11), (S_R4B, 12), (S_R5, 3), (S_R4B, 9), (S_R4A, 7), (S_R3A, 13),
    (S_R4B, 13), (S_R4A, 0), (S_R5, 6), (S_R4B, 10), (S_R5, 12), (S_R4B, 0), (S_R4A, 12), (S_R5, 1), (S_R5, 7), (S_R4A, 13),
    (S_R5, 9), (S_R5, 13), (S_R5, 4), (S_R5, 10), (S_R5, 0),
)
SQRT_HALF = 0.7071067811865476
INV_SQRT_TAU = 0.3989422804014327


def dot(left, right, dims=None):
    if dims is None:
        return jnp.dot(left, right, preferred_element_type=F32)
    return lax.dot_general(left, right, dims, preferred_element_type=F32)


def loop(count, body):
    def step(index, carry):
        body(index)
        return carry

    lax.fori_loop(0, count, step, 0)


def span(index, size):
    return pl.ds(pl.multiple_of(index * size, size), size)


def layer_kernel(
    x_hbm, len_ref, wqkv_hbm, wout_hbm, win_hbm, wdown_hbm, vec_hbm, cot_hbm,
    out_hbm, gtok_hbm, gqkv_hbm, gout_hbm, gin_hbm, gdown_hbm, gvec_hbm,
    wa, wd, vb, gd, go, gv, rcore, rya, rxb, rza, ryb, rzb, rxa, rfb, rv_core, rv_y, rv_z, rv_x, fin, vec,
    x, cot, qkv, vt, pt, ct, n1, y1b, y1t, act, dact, h2, dfb, dcx, rs1, prm, vg,
    s_load, s_io, s_store,
    g_sent, grz, gry, grx, grc, v_sent, vrz, vry, vrc,
    r_sent, rv_sent, rrc, rry, rrx, rrz, rrf, wrc, wry, wrz, wrx,
):
    seq, model = x.shape
    rows = wa.shape[-2]
    hidden = dact.shape[1]
    pair = 2 * (model // HEADS)
    head = model // HEADS
    group = model // 3
    half = model // 2
    wide = lax.axis_index("wide")
    px = lax.axis_index("narrow")
    c = lax.rem(wide, CS)
    y = lax.rem(wide // CS, YS)
    z = wide // (CS * YS)
    zl = lax.rem(z, ZL)
    zh = z // ZL

    def device(zz, yy, cc, xx):
        return ((zz * YS + yy) * CS + cc, xx)

    sibling = device(z, y, 1 - c, px)
    across_y = device(z, 1 - y, c, px)
    across_x = device(z, y, c, 1 - px)

    def ahead(dz):
        return lax.rem(z + dz, ZS)

    def behind(dz):
        return lax.rem(z + ZS - dz, ZS)

    def remote(src, dst, send, recv, where):
        return pltpu.make_async_remote_copy(
            src_ref=src, dst_ref=dst, send_sem=send, recv_sem=recv, device_id=where, device_id_type=MESH
        )

    ALL = slice(None)

    def drained(ref, sem):
        pltpu.make_async_copy(ref, ref, sem).wait()

    def rows_of(count, cols):
        return x.at[pl.ds(0, count), pl.ds(0, cols)]

    def load(src, dst, sem):
        cp = pltpu.make_async_copy(src, dst, sem)
        cp.start()
        return cp

    load_vec = load(vec_hbm, vec, s_io.at[2])
    load_x = load(x_hbm.at[0], x, s_io.at[0])
    for k in range(CHUNKS):
        if k < OUT:
            for part in range(3):
                load(
                    wqkv_hbm.at[:, pl.ds(part * model + k * group, group)],
                    wa.at[k, zh, zl, y, c, :, pl.ds(part * group, group)],
                    s_load.at[k],
                )
        elif k < IN:
            load(wout_hbm, wa.at[k, zh, zl, y, c], s_load.at[k])
        elif k < DOWN:
            load(win_hbm.at[:, pl.ds((k - IN) * model, model)], wa.at[k, zh, zl, y, c], s_load.at[k])
        else:
            load(wdown_hbm.at[pl.ds((k - DOWN) * rows, rows)], wd.at[zh, zl, y, c, k - DOWN], s_load.at[k])
    load_cot = load(cot_hbm.at[0], cot, s_io.at[1])

    barrier = pltpu.get_barrier_semaphore()
    for where in (sibling, across_y, across_x, *(device(ahead(dz), y, c, px) for dz in (1, 2, 3))):
        pl.semaphore_signal(barrier, inc=1, device_id=where, device_id_type=MESH)
    pl.semaphore_wait(barrier, 6)

    third = rows // 3
    kept = pl.ds(pl.multiple_of(px * third, third), 2 * third)
    given = pl.ds(pl.multiple_of(px * 2 * third, third), third)
    taken = pl.ds(pl.multiple_of((1 - px) * 2 * third, third), third)

    def wcut(i, zz, yy, cc, r=ALL):
        k, first, count = GATHERED[i]
        cols = pl.ds(first, count)
        zi = (ALL, ALL) if zz is None else (zz // ZL, lax.rem(zz, ZL))
        if k < DOWN:
            return wa.at[(k, *zi, yy, cc, r, cols)]
        return wd.at[(*zi, yy, cc, k - DOWN, r, cols)]

    def g_z(i, dz, source):
        piece = wcut(i, source, y, c, kept)
        return remote(piece, piece, g_sent.at[i], grz.at[i], device(ahead(dz), y, c, px))

    def g_y(i, dz, column):
        piece = wcut(i, behind(dz), column, c, kept)
        return remote(piece, piece, g_sent.at[i], gry.at[i], across_y)

    def g_x1(i, dz, r):
        piece = wcut(i, behind(dz), y, c, r)
        return remote(piece, piece, g_sent.at[i], grx.at[i], across_x)

    def g_x2(i, r):
        piece = wcut(i, None, 1 - y, c, r)
        return remote(piece, piece, g_sent.at[i], grx.at[i], across_x)

    def g_core(i, core):
        piece = wcut(i, None, ALL, core)
        return remote(piece, piece, g_sent.at[i], grc.at[i], sibling)

    def v_z(dz, source):
        piece = vb.at[source // ZL, lax.rem(source, ZL), y, c]
        return remote(piece, piece, v_sent, vrz, device(ahead(dz), y, c, px))

    def v_y(column):
        piece = vb.at[:, :, column, c]
        return remote(piece, piece, v_sent, vry, across_y)

    def v_core(core):
        piece = vb.at[:, :, :, core]
        return remote(piece, piece, v_sent, vrc, sibling)

    loaded = set()

    def own(k):
        if k not in loaded:
            loaded.add(k)
            drained(rows_of(rows, model), s_load.at[k])

    def e1(i):
        own(GATHERED[i][0])
        for dz in (1, 2, 3):
            g_z(i, dz, z).start()
        if i == 1:
            load_vec.wait()
            segment = vec.shape[0] // 3
            row = vec[...].astype(F32).reshape(1, -1)
            vb[zh, zl, y, c] = jnp.zeros(vb.shape[-2:], BF)
            for s in range(3):
                vb[zh, zl, y, c, s : s + 1, 0:segment] = row[:, s * segment : (s + 1) * segment].astype(BF)
            for dz in (1, 2, 3):
                v_z(dz, z).start()

    def eo(i):
        own(GATHERED[i][0])
        g_y(i, 0, y).start()

    def e2(i):
        if i == 1:
            drained(rv_z, vrz)
            v_y(y).start()
        drained(rows_of(3 * 2 * third, GATHERED[i][2]), grz.at[i])
        for dz in (1, 2, 3):
            g_y(i, dz, y).start()
            g_x1(i, dz, given).start()

    def e3(i):
        if i == 1:
            v_y(1 - y).wait_recv()
            v_core(c).start()
        drained(rows_of(ZS * 2 * third, GATHERED[i][2]), gry.at[i])
        g_x2(i, given).start()

    def e4(i):
        drained(rows_of((ZS + ZS - 1) * third, GATHERED[i][2]), grx.at[i])
        g_core(i, c).start()

    def e5(i):
        if i == 1:
            v_core(1 - c).wait_recv()
        g_core(i, 1 - c).wait_recv()

    def sent(*chunks):
        count = (3 + ZS) * 2 * third + (2 * ZS - 1) * third + ZS * YS * rows
        for i, (k, _, cols) in enumerate(GATHERED):
            if k in chunks:
                drained(qkv.at[:, pl.ds(0, count // 3), pl.ds(0, cols)], g_sent.at[i])

    def vec_sent():
        drained(x.at[pl.ds(0, 80)], v_sent)

    def place_matrix(k, lanes):
        i = lax.broadcasted_iota(jnp.int32, (lanes, model), 0)
        j = lax.broadcasted_iota(jnp.int32, (lanes, model), 1)
        quarter = model // 4
        return jnp.where((i < quarter) & (j == i + k * quarter), 1.0, 0.0).astype(BF)

    def pick_matrix(k, count, total, slot):
        b = lax.broadcasted_iota(jnp.int32, (count, total), 0)
        r = lax.broadcasted_iota(jnp.int32, (count, total), 1)
        segment = 4 * b + k
        return jnp.where((r == slot * (segment // 3) + lax.rem(segment, 3)) & (b < 12), 1.0, 0.0).astype(BF)

    def spread_params(_):
        lanes = vb.shape[-1]
        segments = vb[...].reshape(-1, lanes)
        total = None
        for k in range(4):
            picked = dot(pick_matrix(k, 16, segments.shape[0], vb.shape[-2]), segments).astype(BF)
            part = dot(picked, place_matrix(k, lanes))
            total = part if total is None else total + part
        prm[...] = total

    def gather_grads(_):
        lanes = gv.shape[-1]
        low = vg[...].astype(BF)
        total = None
        for k in range(4):
            cut = dot(low, place_matrix(k, lanes), NT).astype(BF)
            part = dot(pick_matrix(k, 16, 16 * gv.shape[-2], gv.shape[-2]), cut, TN)
            total = part if total is None else total + part
        gv[...] = total.astype(BF).reshape(gv.shape)

    def weight(k, cols=ALL):
        block = wa[k, :, :, :, :, :, cols]
        return block.reshape(-1, block.shape[-1])

    def project(g):
        grouped = span(g, group)

        def tile(part):
            cols = span(part, group)
            bias = jnp.where(part == 0, prm[0:1, grouped], jnp.where(part == 2, prm[1:2, grouped], 0.0))
            low = (dot(x[...], weight(g, cols)) + bias).astype(BF)
            qkv[g, :, cols] = low * jnp.where(part == 0, head**-0.5, 1.0).astype(BF)

        loop(3, tile)
        vt[grouped, :] = qkv[g, :, 2 * group :].T

    def attend(half_group):
        g, first = half_group // 2, half_group % 2 * 2
        length = len_ref[0]

        def one(i):
            h = first + i
            cols = span(h // 2, pair)
            keys = pl.ds(pl.multiple_of(group + (h // 2) * pair, pair), pair)
            lane = lax.broadcasted_iota(jnp.int32, (seq, pair), 1) // head
            masked = jnp.where(lane == lax.rem(h, 2), qkv[g, :, keys], jnp.zeros((), BF))
            scores = dot(masked, qkv[g, :, cols], NT)
            key = lax.broadcasted_iota(jnp.int32, scores.shape, 0)
            scores = jnp.where(key < length, scores, -1000000000.0)
            raised = jnp.exp(scores - jnp.max(scores, axis=0, keepdims=True))
            probs = (raised * (1.0 / jnp.sum(raised, axis=0, keepdims=True))).astype(BF)
            pt[g, h] = probs
            mine = pl.ds(pl.multiple_of(g * group + h * head, head), head)
            ct[mine, :] = dot(vt[mine, :], probs).astype(BF)

        loop(2, one)

    def out_proj(_):
        context = ct[...].T
        bo, g1, c1 = prm[2:3, :], prm[3:4, :], prm[4:5, :]
        w = weight(OUT)

        def tile(i):
            r = span(i, 128)
            h1 = x[r, :].astype(F32) + (h2[r, :] + bo)
            centred = h1 - jnp.mean(h1, -1, keepdims=True)
            inverse = lax.rsqrt(jnp.mean(centred * centred, -1, keepdims=True) + 1e-06)
            normed = centred * inverse
            n1[r, :] = normed
            rs1[r, :] = inverse
            y1b[r, :] = (normed * g1 + c1).astype(BF)

        h2[...] = dot(context, w)
        loop(seq // 128, tile)

    def feed_up(j):
        def tile(t):
            cols = span(t, half)
            wide_cols = pl.ds(pl.multiple_of(j * model + t * half, half), half)
            u = dot(y1b[...], weight(IN + j, cols)) + prm[8 + j : 9 + j, cols]
            phi = 0.5 * (1.0 + lax.erf(u * SQRT_HALF))
            act[2 * j + t] = (u * phi).astype(BF).T.reshape(CS, 4, rows, seq)
            dact[:, wide_cols] = (phi + u * (jnp.exp(-0.5 * u * u) * INV_SQRT_TAU)).astype(BF)

        loop(2, tile)

    def act_rows(m):
        return act[:, :, m].reshape(-1, seq)

    def feed_down(m):
        w = wd[:, :, :, :, m].reshape(-1, model)
        part = dot(act_rows(m), w, TN)
        if m == 0:
            h2[...] = part + (n1[...] * prm[3:4, :] + prm[4:5, :]) + prm[5:6, :]
        else:
            h2[...] += part

    def vsum(row, value):
        vg[row : row + 1, :] += jnp.sum(value, axis=0, keepdims=True)

    def norm_back(dn, n, inverse):
        return (dn - jnp.mean(dn, -1, keepdims=True) - n * jnp.mean(dn * n, -1, keepdims=True)) * inverse

    def norm_two(_):
        g2, c2 = prm[6:7, :], prm[7:8, :]

        def tile(i):
            r = span(i, 128)
            h = h2[r, :]
            centred = h - jnp.mean(h, -1, keepdims=True)
            inverse = lax.rsqrt(jnp.mean(centred * centred, -1, keepdims=True) + 1e-06)
            n = centred * inverse
            dcx[r, :] = (n * g2 + c2).astype(BF)
            dy = cot[r, :].astype(F32)
            vsum(6, dy * n)
            vsum(7, dy)
            dh = norm_back(dy * g2, n, inverse)
            h2[r, :] = dh
            low = dh.astype(BF)
            dfb[r, :] = low
            vsum(5, low.astype(F32))

        loop(seq // 128, tile)
        store_out.append(store(dcx, out_hbm.at[0], 1))

    def grad_down(m):
        gd[m] = dot(act_rows(m), dfb[...]).astype(BF).reshape(gd.shape[1:])

    def grad_act(j):
        def tile(t):
            i = 2 * j + t
            cols = span(i, 2 * 4 * rows)
            zz = i // YS
            w = wd[zz // ZL, lax.rem(zz, ZL), lax.rem(i, YS)].reshape(2 * 4 * rows, model)
            du = (dot(dfb[...], w, NT) * dact[:, cols].astype(F32)).astype(BF)
            dact[:, cols] = du
            total = jnp.sum(du.astype(F32), axis=0, keepdims=True)
            vg[8 + j : 9 + j, t * half : (t + 1) * half] = total

        tile(0)
        tile(1)

    def grad_in(j):
        if j == 0:
            sent(*range(DOWN, CHUNKS))
            y1t[...] = y1b[...].T

        def tile(t):
            wide_cols = pl.ds(pl.multiple_of(j * model + t * 256, 256), 256)
            g = dot(y1t[...], dact[:, wide_cols]).astype(BF)
            wd[:, :, :, :, j, :, span(t, 256)] = g.reshape(ZH, ZL, YS, CS, rows, 256)

        loop(model // 256, tile)

    def grad_normed(j):
        h2[...] += dot(dact[:, j * model : (j + 1) * model], weight(IN + j), NT)

    def norm_one_back(_):
        g1 = prm[3:4, :]

        def tile(i):
            r = span(i, 128)
            dy, n = h2[r, :], n1[r, :]
            vsum(3, dy * n)
            vsum(4, dy)
            dh = norm_back(dy * g1, n, rs1[r, :])
            h2[r, :] = dh
            low = dh.astype(BF)
            dfb[r, :] = low
            vsum(2, low.astype(F32))

        loop(seq // 128, tile)

    def grad_out(_):
        g = dot(ct[...], dfb[...]).astype(BF)
        go[0] = g.reshape(ZH, ZL, YS, CS, rows, model)

    def grad_context(_):
        store_out.pop().wait()
        vt[...] = x[...].T
        dcx[...] = dot(dfb[...], weight(OUT), NT).astype(BF)

    def attend_back(g):
        def one(j):
            cols = span(j, pair)
            keys = pl.ds(pl.multiple_of(group + j * pair, pair), pair)
            vals = pl.ds(pl.multiple_of(2 * group + j * pair, pair), pair)
            place = pl.ds(pl.multiple_of(g * group + j * pair, pair), pair)
            lane = lax.broadcasted_iota(jnp.int32, (seq, pair), 1) // head
            dc = dcx[:, place]
            q, k, v = qkv[g, :, cols], qkv[g, :, keys], qkv[g, :, vals]
            kt = k.T
            dk, dv, dq = [], [], []
            for e in range(2):
                probs = pt[g, 2 * j + e]
                dv.append(dot(probs, dc))
                dp = dot(jnp.where(lane == e, v, jnp.zeros((), BF)), dc, NT)
                p32 = probs.astype(F32)
                t = p32 * dp
                ds = (t - p32 * jnp.sum(t, axis=0, keepdims=True)).astype(BF)
                dk.append(dot(ds, q))
                dq.append((dot(kt[e * head : (e + 1) * head, :], ds) * head**-0.5).astype(BF))
            dv = jnp.where(lane == 0, dv[0], dv[1]).astype(BF)
            dq = jnp.concatenate(dq, axis=0).T
            qkv[g, :, cols] = dq
            qkv[g, :, keys] = jnp.where(lane == 0, dk[0], dk[1]).astype(BF)
            qkv[g, :, vals] = dv
            vg[0:1, place] = jnp.sum(dq.astype(F32), axis=0, keepdims=True)
            vg[1:2, place] = jnp.sum(dv.astype(F32), axis=0, keepdims=True)

        loop(group // pair, one)

    def grad_qkv(g):
        if g == 0:
            sent(*range(IN, DOWN))

        def tile(t):
            cols = span(t, group)
            r = dot(vt[...], qkv[g, :, cols]).astype(BF)
            wa[IN + g, :, :, :, :, :, cols] = r.reshape(ZH, ZL, YS, CS, rows, group)

        loop(3, tile)

    def grad_x(g):
        before = h2 if g == 0 else n1
        n1[...] = before[...] + dot(qkv[g], weight(g), NT)
        if g == 2:
            store_x.append(store(n1, gtok_hbm.at[0], 2))

    last = len(SUMMED) - 1
    every = (ALL, ALL)
    mine = (zh, zl)

    def at_z(zz):
        return (zz // ZL, lax.rem(zz, ZL))

    def gpiece(k, zi, yy, cc, cols=ALL):
        if k < 4:
            return gd.at[(k, *zi, yy, cc, ALL, cols)]
        if k < 8:
            return wd.at[(*zi, yy, cc, k - 4, ALL, cols)]
        if k < 9:
            return go.at[(0, *zi, yy, cc, ALL, cols)]
        return wa.at[(IN + k - 9, *zi, yy, cc, ALL, cols)]

    def left(i):
        return pl.ds(SUMMED[i][1], SUMMED[i][2])

    def right(i):
        return pl.ds(half + SUMMED[i][1], SUMMED[i][2])

    def near(i):
        return left(i)

    def both(i):
        return (ALL,) if SUMMED[i][2] == half else (left(i), right(i))

    def r_core(i, cols):
        k = SUMMED[i][0]
        return remote(
            gpiece(k, every, ALL, 1 - c, cols), rcore.at[k % RING, :, :, :, :, cols], r_sent.at[i], rrc.at[i], sibling
        )

    def r_ya(i):
        k = SUMMED[i][0]
        src, dst = gpiece(k, every, 1 - y, c, left(i)), rya.at[k, :, :, :, near(i)]
        return remote(src, dst, r_sent.at[i], rry.at[i, 0], across_y)

    def r_xb(i):
        k = SUMMED[i][0]
        src, dst = gpiece(k, (ALL, 1 - parity(i)), ALL, c, right(i)), rxb.at[k, :, :, :, near(i)]
        return remote(src, dst, r_sent.at[i], rrx.at[i, 0], across_x)

    def r_za(i, dz):
        k = SUMMED[i][0]
        src, dst = gpiece(k, at_z(ahead(dz)), y, c, left(i)), rza.at[k, dz - 1, :, near(i)]
        return remote(src, dst, r_sent.at[i], rrz.at[i, 0], device(ahead(dz), y, c, px))

    def r_yb(i):
        k = SUMMED[i][0]
        src, dst = gpiece(k, (ALL, parity(i)), 1 - y, c, right(i)), ryb.at[k, :, :, near(i)]
        return remote(src, dst, r_sent.at[i], rry.at[i, 1], across_y)

    def r_xa(i):
        k = SUMMED[i][0]
        src, dst = gpiece(k, mine, y, c, left(i)), rxa.at[k, :, near(i)]
        return remote(src, dst, r_sent.at[i], rrx.at[i, 1], across_x)

    def r_zb(i, dz):
        k = SUMMED[i][0]
        src, dst = gpiece(k, at_z(ahead(dz)), y, c, right(i)), rzb.at[k, dz - 1, :, near(i)]
        return remote(src, dst, r_sent.at[i], rrz.at[i, 1], device(ahead(dz), y, c, px))

    def r_fb(i):
        k = SUMMED[i][0]
        return remote(
            gpiece(k, mine, y, c, right(i)), rfb.at[k, :, near(i)], r_sent.at[i], rrf.at[i], across_x
        )

    v_rc = remote(gv.at[:, :, :, 1 - c], rv_core, rv_sent, wrc, sibling)
    v_ry = remote(gv.at[:, :, 1 - y, c], rv_y, rv_sent, wry, across_y)
    v_rx = remote(gv.at[(*mine, y, c)], rv_x, rv_sent, wrx, across_x)

    def v_rz(dz):
        where = device(ahead(dz), y, c, px)
        return remote(gv.at[(*at_z(ahead(dz)), y, c)], rv_z.at[dz - 1], rv_sent, wrz, where)

    def parity(i):
        return lax.rem(px + i, 2)

    def same(i):
        return zl == parity(i)


    def add_into(ref, *others):
        if len(others) == 1:
            ref[...] += others[0][...]
            return
        total = ref[...].astype(F32)
        for other in others:
            total = total + other[...].astype(F32)
        ref[...] = total.astype(BF)

    def r0(i):
        for cols in both(i):
            r_core(i, cols).start()
        if i == last:
            v_rc.start()

    def r1(i):
        k, _, width = SUMMED[i]
        drained(wa.at[0, :, :, :, 0, :, pl.ds(0, 2 * width)], rrc.at[i])

        def add(zz):
            for cols in both(i):
                add_into(gpiece(k, at_z(zz), ALL, c, cols), rcore.at[(k % RING, *at_z(zz), ALL, ALL, cols)])

        loop(ZS, add)
        r_ya(i).start()
        r_xb(i).start()
        if i == last:
            v_rc.wait_recv()
            add_into(gv.at[:, :, :, c], rv_core)
            v_ry.start()

    def r2a(i):
        k = SUMMED[i][0]
        r_ya(i).wait_recv()
        add_into(gpiece(k, every, y, c, left(i)), rya.at[k, :, :, :, near(i)])
        for dz in (1, 2, 3):
            r_za(i, dz).start()
        if i == last:
            v_ry.wait_recv()
            add_into(gv.at[:, :, y, c], rv_y)
            for dz in (1, 2, 3):
                v_rz(dz).start()

    def r2b(i):
        k = SUMMED[i][0]
        r_xb(i).wait_recv()
        add_into(gpiece(k, (ALL, parity(i)), ALL, c, right(i)), rxb.at[k, :, :, :, near(i)])
        r_yb(i).start()

    def r3a(i):
        k = SUMMED[i][0]
        drained(rza.at[k, :, :, near(i)], rrz.at[i, 0])
        add_into(gpiece(k, mine, y, c, left(i)), *(rza.at[k, dz, :, near(i)] for dz in range(3)))
        r_xa(i).start()
        if i == last:
            drained(rv_z, wrz)
            add_into(gv.at[(*mine, y, c)], rv_z.at[0], rv_z.at[1], rv_z.at[2])
            v_rx.start()

    def r3b(i):
        k = SUMMED[i][0]
        r_yb(i).wait_recv()
        add_into(gpiece(k, (ALL, parity(i)), y, c, right(i)), ryb.at[k, :, :, near(i)])
        pl.when(same(i))(lambda: r_zb(i, 2).start())

        @pl.when(jnp.logical_not(same(i)))
        def _():
            r_zb(i, 1).start()
            r_zb(i, 3).start()

    def r4a(i):
        k = SUMMED[i][0]
        r_xa(i).wait_recv()
        fin[k, :, left(i)] = gpiece(k, mine, y, c, left(i))[...].astype(F32) + rxa[k, :, near(i)].astype(F32)
        if i == last:
            v_rx.wait_recv()
            store_vec.append(store(gv.at[(*mine, y, c)], gvec_hbm.at[0], 3))
            store_vec.append(store(rv_x, gvec_hbm.at[1], 4))
        settle(k)

    def r4b(i):
        k = SUMMED[i][0]

        @pl.when(same(i))
        def _():
            drained(rzb.at[k, :, :, near(i)], rrz.at[i, 1])
            piece = gpiece(k, mine, y, c, right(i))
            add_into(piece, *(rzb.at[k, dz, :, near(i)] for dz in range(3)))
            r_fb(i).start()
            fin[k, :, right(i)] = piece[...].astype(F32)

    def r5(i):
        k = SUMMED[i][0]

        @pl.when(jnp.logical_not(same(i)))
        def _():
            r_fb(i).wait_recv()
            fin[k, :, right(i)] = rfb[k, :, near(i)].astype(F32)

        settle(k)

    store_out, store_x, store_vec = [], [], []
    open_ends = {k: 2 * sum(part[0] == k for part in SUMMED) for k in range(CHUNKS)}

    def store(src, dst, i=0):
        cp = pltpu.make_async_copy(src, dst, s_store.at[i])
        cp.start()
        return cp

    def settle(k):
        open_ends[k] -= 1
        if open_ends[k]:
            return
        if k < 4:
            store(fin.at[k], gdown_hbm.at[pl.ds(k * rows, rows)])
        elif k < 8:
            store(fin.at[k], gin_hbm.at[:, pl.ds((k - 4) * model, model)])
        elif k < 9:
            store(fin.at[k], gout_hbm)
        else:
            for part in range(3):
                store(
                    fin.at[k, :, pl.ds(part * group, group)],
                    gqkv_hbm.at[:, pl.ds(part * model + (k - 9) * group, group)],
                )

    steps = (
        e1, eo, e2, e3, e4, e5,
        r0, r1, r2a, r2b, r3a, r3b,
        r4a, r4b, r5, spread_params, project, attend,
        out_proj, feed_up, feed_down, norm_two, grad_down, grad_act,
        grad_in, grad_normed, norm_one_back, grad_out, grad_context, attend_back,
        grad_qkv, gather_grads, grad_x,
    )
    vg[...] = jnp.zeros_like(vg)
    for step, i in ORDER:
        if step == S_PROJECT and i == 0:
            load_x.wait()
        if step == S_NORM2:
            load_cot.wait()
        steps[step](i)
    sent(*range(IN))
    vec_sent()
    for i, (_, _, width) in enumerate(SUMMED):
        drained(wa.at[0, :, :, :, :, :, pl.ds(0, 2 * width)], r_sent.at[i])
    drained(gv, rv_sent)
    drained(fin, s_store.at[0])
    for cp in (*store_vec, *store_x):
        cp.wait()


def place_kernel(cuts, *refs):
    count = len(cuts)
    sources, targets, held = refs[: count + 1], refs[count + 1 : 2 * count + 2], refs[2 * count + 2 : 3 * count + 3]
    vector, sem_in, sem_out = refs[3 * count + 3 :]
    first = pltpu.make_async_copy(sources[count], held[count], sem_in.at[sum(cuts)])
    first.start()
    moves = []
    for src, dst, mid, parts in zip(sources, targets, held, cuts):
        size = src.shape[-2] // parts
        for j in range(parts):
            at = (slice(None),) * (len(src.shape) - 2) + (pl.ds(j * size, size),)
            i = len(moves)
            moves.append(
                (
                    pltpu.make_async_copy(src.at[at], mid.at[at], sem_in.at[i]),
                    pltpu.make_async_copy(mid.at[at], dst.at[at], sem_out.at[i]),
                )
            )
    for into, _ in moves:
        into.start()
    first.wait()
    segment = vector.shape[0] // 3
    total = held[count][0].astype(F32) + held[count][1].astype(F32)
    vector[...] = jnp.concatenate([total[s : s + 1, 0:segment] for s in range(3)], axis=1).reshape(-1)
    last = pltpu.make_async_copy(vector, targets[count], sem_out.at[sum(cuts)])
    last.start()
    for into, out in moves:
        into.wait()
        out.start()
    for _, out in moves:
        out.wait()
    last.wait()


def fused_layer(tokens, lengths, w_qkv, w_out, w_in, w_down, norms_biases, cotangent):
    seq, model = tokens.shape[1:]
    rows = w_qkv.shape[0]
    hidden = w_in.shape[1]
    half = model // 2
    group = model // 3
    vm, dma = pltpu.VMEM, pltpu.SemaphoreType.DMA
    grid = (ZH, ZL, YS, CS)
    n, m, u = CHUNKS, len(GATHERED), len(SUMMED)
    scratch = [
        vm((DOWN, *grid, rows, model), BF),
        vm((*grid, 4, rows, model), BF),
        vm((*grid, 16, 256), BF),
        vm((4, *grid, rows, model), BF),
        vm((1, *grid, rows, model), BF),
        vm((*grid, 16, 256), BF),
        vm((RING, ZH, ZL, YS, rows, model), BF),
        vm((n, ZH, ZL, rows, half), BF),
        vm((n, ZH, YS, rows, half), BF),
        vm((n, 3, rows, half), BF),
        vm((n, ZH, rows, half), BF),
        vm((n, 3, rows, half), BF),
        vm((n, rows, half), BF),
        vm((n, rows, half), BF),
        vm((ZH, ZL, YS, 16, 256), BF),
        vm((ZH, ZL, 16, 256), BF),
        vm((3, 16, 256), BF),
        vm((16, 256), BF),
        vm((n, rows, model), F32),
        vm(norms_biases.shape, BF),
        vm((seq, model), BF),
        vm((seq, model), BF),
        vm((3, seq, model), BF),
        vm((model, seq), BF),
        vm((3, group // (model // HEADS), seq, seq), BF),
        vm((model, seq), BF),
        vm((seq, model), F32),
        vm((seq, model), BF),
        vm((model, seq), BF),
        vm((ZS * YS, CS, 4, rows, seq), BF),
        vm((seq, hidden), BF),
        vm((seq, model), F32),
        vm((seq, model), BF),
        vm((seq, model), BF),
        vm((seq, 1), F32),
        vm((16, model), F32),
        vm((16, model), F32),
        dma((n,)), dma((3,)), dma((5,)),
        dma((m,)), dma((m,)), dma((m,)), dma((m,)), dma((m,)), dma, dma, dma, dma,
        dma((u,)), dma, dma((u,)), dma((u, 2)), dma((u, 2)), dma((u, 2)), dma((u,)), dma, dma, dma, dma,
    ]
    hbm = pl.BlockSpec(memory_space=pl.ANY)
    shape = jax.ShapeDtypeStruct
    outs = pl.pallas_call(
        layer_kernel,
        out_shape=(
            shape(tokens.shape, BF),
            shape(tokens.shape, F32),
            shape(w_qkv.shape, F32),
            shape(w_out.shape, F32),
            shape(w_in.shape, F32),
            shape(w_down.shape, F32),
            shape((2, 16, 256), BF),
        ),
        in_specs=[hbm, pl.BlockSpec(memory_space=pltpu.SMEM)] + [hbm] * 6,
        out_specs=(hbm,) * 7,
        scratch_shapes=scratch,
        compiler_params=pltpu.CompilerParams(
            collective_id=0, has_side_effects=True, vmem_limit_bytes=64 << 20
        ),
        name="layer",
    )(tokens, lengths, w_qkv, w_out, w_in, w_down, norms_biases, cotangent)
    cuts = (1, 2, 1, 1, 1, 1)
    *placed, grad_vector = pl.pallas_call(
        functools.partial(place_kernel, cuts),
        out_shape=(*(shape(o.shape, o.dtype) for o in outs[:6]), shape(norms_biases.shape, F32)),
        in_specs=[hbm] * 7,
        out_specs=(hbm,) * 7,
        scratch_shapes=[vm(o.shape, o.dtype) for o in outs]
        + [vm(norms_biases.shape, F32), dma((sum(cuts) + 1,)), dma((sum(cuts) + 1,))],
        name="place",
    )(*outs)
    return (*placed, grad_vector)


def norm_rows(values, gain_row, shift_row):
    average = jnp.mean(values, -1, keepdims=True)
    centred = values - average
    spread = jnp.mean(centred * centred, -1, keepdims=True)
    return centred * lax.rsqrt(spread + 1e-06) * gain_row + shift_row


def gelu_exact(values):
    return jax.nn.gelu(values, approximate=False)


def column_sum(values):
    return jnp.sum(values.astype(jnp.float32), 0)


def split_vector(vector, model_width, hidden_width):
    segments = [
        vector[position * model_width : (position + 1) * model_width] for position in range(8)
    ]
    return segments + [vector[8 * model_width : 8 * model_width + hidden_width]]


def pair_blocks(projected, head_count):
    row_count = projected.shape[0]
    pair_count = head_count // 2
    pair_width = projected.shape[1] // (3 * pair_count)
    return projected.reshape(row_count, 3, pair_count, pair_width).transpose(2, 1, 0, 3)


def unpair_blocks(blocks):
    pair_count = blocks.shape[0]
    row_count = blocks.shape[2]
    pair_width = blocks.shape[3]
    return blocks.transpose(2, 1, 0, 3).reshape(row_count, 3 * pair_count * pair_width)


def pair_scores(head_block, usable, factor):
    row_count = head_block.shape[1]
    queries = head_block[0].reshape(row_count, 2, -1)
    key_rows = head_block[1].reshape(row_count, 2, -1)
    values = head_block[2].reshape(row_count, 2, -1)
    scores = (
        jnp.einsum("qhd,khd->hqk", queries, key_rows, preferred_element_type=jnp.float32) * factor
    )
    return (queries, key_rows, values, jnp.where(usable[None, None, :], scores, -1000000000.0))


def attention_forward(blocks, usable, factor):

    def one_pair(head_block):
        queries, key_rows, values, scores = pair_scores(head_block, usable, factor)
        highest = jnp.max(scores, -1, keepdims=True)
        raised = jnp.exp(scores - highest)
        summed = jnp.sum(raised, -1, keepdims=True)
        attend = (raised / summed).astype(jnp.bfloat16)
        context = jnp.einsum("hqk,khd->qhd", attend, values, preferred_element_type=jnp.float32)
        return (context.reshape(context.shape[0], -1), highest[..., 0] + jnp.log(summed[..., 0]))

    return lax.map(one_pair, blocks)


def attention_backward(blocks, grad_pairs, log_totals, usable, factor):

    def one_pair(pair_inputs):
        head_block, grad_context, log_total = pair_inputs
        queries, key_rows, values, scores = pair_scores(head_block, usable, factor)
        attend = jnp.exp(scores - log_total[..., None])
        row_count = grad_context.shape[0]
        grad_heads = grad_context.reshape(row_count, 2, -1)
        grad_values = jnp.einsum(
            "hqk,qhd->khd",
            attend.astype(jnp.bfloat16),
            grad_heads,
            preferred_element_type=jnp.float32,
        )
        grad_attend = jnp.einsum(
            "qhd,khd->hqk", grad_heads, values, preferred_element_type=jnp.float32
        )
        grad_scores = attend * (grad_attend - jnp.sum(attend * grad_attend, -1, keepdims=True))
        grad_low = grad_scores.astype(jnp.bfloat16)
        grad_queries = (
            jnp.einsum("hqk,khd->qhd", grad_low, key_rows, preferred_element_type=jnp.float32)
            * factor
        )
        grad_keys = (
            jnp.einsum("hqk,qhd->khd", grad_low, queries, preferred_element_type=jnp.float32)
            * factor
        )
        return jnp.stack(
            [
                grad_queries.reshape(row_count, -1),
                grad_keys.reshape(row_count, -1),
                grad_values.reshape(row_count, -1),
            ]
        )

    return lax.map(one_pair, (blocks, grad_pairs, log_totals))


def layer_forward(inputs, length, weights):
    w_qkv, w_out, w_in, w_down, vector = weights
    row_count, model_width = inputs.shape
    hidden_width = w_in.shape[1]
    params = split_vector(vector.astype(jnp.float32), model_width, hidden_width)
    joined_bias = jnp.concatenate([params[0], jnp.zeros((model_width,), jnp.float32), params[1]])
    projected = (jnp.dot(inputs, w_qkv, preferred_element_type=jnp.float32) + joined_bias).astype(
        jnp.bfloat16
    )
    blocks = pair_blocks(projected, HEADS)
    usable = jnp.arange(row_count) < length
    factor = (model_width // HEADS) ** (-0.5)
    context_pairs, log_totals = attention_forward(blocks, usable, factor)
    context = context_pairs.transpose(1, 0, 2).reshape(row_count, model_width).astype(jnp.bfloat16)
    resid_one = inputs.astype(jnp.float32) + (
        jnp.dot(context, w_out, preferred_element_type=jnp.float32) + params[2]
    )
    normed_one = norm_rows(resid_one, params[3], params[4])
    normed_low = normed_one.astype(jnp.bfloat16)
    pre_act = jnp.dot(normed_low, w_in, preferred_element_type=jnp.float32) + params[8]
    activated = gelu_exact(pre_act).astype(jnp.bfloat16)
    resid_two = normed_one + (
        jnp.dot(activated, w_down, preferred_element_type=jnp.float32) + params[5]
    )
    result = norm_rows(resid_two, params[6], params[7])
    saved = (
        params,
        blocks,
        usable,
        factor,
        log_totals,
        context,
        resid_one,
        normed_low,
        pre_act,
        activated,
        resid_two,
    )
    return (result, saved)


def layer_backward(inputs, length, grad_result, weights):
    w_qkv, w_out, w_in, w_down, vector = weights
    unused_result, saved = layer_forward(inputs, length, weights)
    (
        params,
        blocks,
        usable,
        factor,
        log_totals,
        context,
        resid_one,
        normed_low,
        pre_act,
        activated,
        resid_two,
    ) = saved
    row_count, model_width = inputs.shape
    unused_two, norm_two_back = jax.vjp(norm_rows, resid_two, params[6], params[7])
    grad_two, grad_gain_two, grad_shift_two = norm_two_back(grad_result)
    grad_feed = grad_two.astype(jnp.bfloat16)
    grad_down = jnp.einsum("sf,sd->fd", activated, grad_feed, preferred_element_type=jnp.float32)
    grad_act = jnp.einsum("sd,fd->sf", grad_feed, w_down, preferred_element_type=jnp.float32)
    unused_act, gelu_back = jax.vjp(gelu_exact, pre_act)
    grad_pre = gelu_back(grad_act)[0].astype(jnp.bfloat16)
    grad_in = jnp.einsum("sd,sf->df", normed_low, grad_pre, preferred_element_type=jnp.float32)
    grad_normed = grad_two + jnp.einsum(
        "sf,df->sd", grad_pre, w_in, preferred_element_type=jnp.float32
    )
    unused_one, norm_one_back = jax.vjp(norm_rows, resid_one, params[3], params[4])
    grad_one, grad_gain_one, grad_shift_one = norm_one_back(grad_normed)
    grad_attended = grad_one.astype(jnp.bfloat16)
    grad_out = jnp.einsum("sd,se->de", context, grad_attended, preferred_element_type=jnp.float32)
    grad_context = jnp.einsum(
        "se,de->sd", grad_attended, w_out, preferred_element_type=jnp.float32
    ).astype(jnp.bfloat16)
    grad_pairs = grad_context.reshape(row_count, HEADS // 2, -1).transpose(1, 0, 2)
    grad_blocks = attention_backward(blocks, grad_pairs, log_totals, usable, factor)
    grad_projected = unpair_blocks(grad_blocks).astype(jnp.bfloat16)
    grad_qkv = jnp.einsum("sd,se->de", inputs, grad_projected, preferred_element_type=jnp.float32)
    grad_inputs = grad_one + jnp.einsum(
        "se,de->sd", grad_projected, w_qkv, preferred_element_type=jnp.float32
    )
    projected_sums = column_sum(grad_projected)
    grad_vector = jnp.concatenate(
        [
            projected_sums[:model_width],
            projected_sums[2 * model_width :],
            column_sum(grad_attended),
            grad_gain_one,
            grad_shift_one,
            column_sum(grad_feed),
            grad_gain_two,
            grad_shift_two,
            column_sum(grad_pre),
        ]
    )
    return (grad_inputs, (grad_qkv, grad_out, grad_in, grad_down, grad_vector))


def local(tokens, lengths, w_qkv, w_out, w_in, w_down, norms_biases, cotangent):
    weights = (
        lax.all_gather(w_qkv, "wide", axis=0, tiled=True),
        lax.all_gather(w_out, "wide", axis=0, tiled=True),
        lax.all_gather(w_in, "wide", axis=0, tiled=True),
        lax.all_gather(w_down, "wide", axis=0, tiled=True),
        lax.all_gather(norms_biases, "wide", axis=0, tiled=True),
    )

    def forward_one(sequence):
        return layer_forward(sequence[0], sequence[1], weights)[0].astype(jnp.bfloat16)

    output = lax.map(forward_one, (tokens, lengths))
    second_copy = (
        lax.all_gather(w_qkv, "wide", axis=0, tiled=True),
        lax.all_gather(w_out, "wide", axis=0, tiled=True),
        lax.all_gather(w_in, "wide", axis=0, tiled=True),
        lax.all_gather(w_down, "wide", axis=0, tiled=True),
        lax.all_gather(norms_biases, "wide", axis=0, tiled=True),
    )
    running = tuple((jnp.zeros(member.shape, jnp.float32) for member in second_copy))

    def advance(totals, sequence):
        grad_inputs, gradients = layer_backward(
            sequence[0], sequence[1], sequence[2].astype(jnp.float32), second_copy
        )
        return (jax.tree.map(jnp.add, totals, gradients), grad_inputs)

    totals, grad_tokens = lax.scan(advance, running, (tokens, lengths, cotangent))
    owned_rows = (
        lax.psum_scatter(
            totals[0].astype(jnp.bfloat16), "wide", scatter_dimension=0, tiled=True
        ).astype(jnp.float32),
        lax.psum_scatter(
            totals[1].astype(jnp.bfloat16), "wide", scatter_dimension=0, tiled=True
        ).astype(jnp.float32),
        lax.psum_scatter(
            totals[2].astype(jnp.bfloat16), "wide", scatter_dimension=0, tiled=True
        ).astype(jnp.float32),
        lax.psum_scatter(
            totals[3].astype(jnp.bfloat16), "wide", scatter_dimension=0, tiled=True
        ).astype(jnp.float32),
        lax.psum_scatter(
            totals[4].astype(jnp.bfloat16), "wide", scatter_dimension=0, tiled=True
        ).astype(jnp.float32),
    )
    summed_all = (
        lax.psum(owned_rows[0].astype(jnp.bfloat16), "narrow").astype(jnp.float32),
        lax.psum(owned_rows[1].astype(jnp.bfloat16), "narrow").astype(jnp.float32),
        lax.psum(owned_rows[2].astype(jnp.bfloat16), "narrow").astype(jnp.float32),
        lax.psum(owned_rows[3].astype(jnp.bfloat16), "narrow").astype(jnp.float32),
        lax.psum(owned_rows[4].astype(jnp.bfloat16), "narrow").astype(jnp.float32),
    )
    return (
        output,
        grad_tokens,
        summed_all[0],
        summed_all[1],
        summed_all[2],
        summed_all[3],
        summed_all[4],
    )


def solution(mesh):
    in_specs = (
        P(("wide", "narrow"), None, None),
        P(("wide", "narrow")),
        P("wide", None),
        P("wide", None),
        P("wide", None),
        P("wide", None),
        P("wide"),
        P(("wide", "narrow"), None, None),
    )
    out_specs = (
        P(("wide", "narrow"), None, None),
        P(("wide", "narrow"), None, None),
        P("wide", None),
        P("wide", None),
        P("wide", None),
        P("wide", None),
        P("wide"),
    )
    chips = (ZS * YS * CS, 2)
    fused = tuple(mesh.shape[axis] for axis in ("wide", "narrow")) == chips
    step = fused_layer if fused else local
    return jax.shard_map(step, mesh=mesh, in_specs=in_specs, out_specs=out_specs, check_vma=False)
```
